512 devices in a mesh: sec: 32 (over z, y_lo), blk: 16 (over x, y_hi, core).
Axes of the slice: x: 4, y: 8 (y_hi: 2, y_lo: 4; y = y_hi * 4 + y_lo), z: 8, core: 2. Of those that a mesh axis runs over, the one named last changes fastest.
Arguments:
- image: bfloat16 [32, 2048, 4096], P('sec', 'blk'), may hold values from -6 to 6
- tissue_mask: int32 [32, 2048, 4096], P('sec', 'blk'), may hold values 0 or 1
- anchor: float32 [32, 512, 1024], P('sec', 'blk'), may hold values from 0.1 to 3
- fixed_nodes: int32 [32, 512, 1024], P('sec', 'blk'), may hold values from 0 to 1, as said below
- prior_shift: float32 [2, 32, 512, 1024], P(None, 'sec', 'blk'), may hold values from -6 to 6
Outputs:
- displacement: float32 [2, 32, 512, 1024], P(None, 'sec', 'blk')
The draws below stay inside these ranges and needn't reach their ends.
Inputs may be any that keep to these rules, and one draw needn't show every extreme that they name: `fixed_nodes`: the share of fixed nodes differs from one aligned block of 64 rows to another; in some sections a whole aligned block of 64 rows is fixed.
All inputs are finite; a program needn't handle non-finite values. No bound on the sum of `tissue_mask` on one device may be relied on, other than what follows from the above.
Results may differ from the reference program's by a relative error of at most 0.011.
Values may be sent and summed in bfloat16 or wider, within the bound.
A program may use at most 64 MiB of HBM per device.

```python
import math
import jax
import jax.numpy as jnp
from jax import lax

P_SIZE = 128
NPATCH = 32
NODES_PATCH = 32
MR = 32
ITERS = 4
SECTIONS = 32
IMG_ROWS = 2048
IMG_COLS = 4096
ROWS = 512
NODE_COLS = 1024


def draw_anchor(key, part):
    key = jax.random.fold_in(key, 11)
    shape = (SECTIONS, ROWS, NODE_COLS)
    base = jnp.exp(jax.random.uniform(key, shape, jnp.float32, jnp.log(0.1), 0.0))
    rows = jnp.arange(ROWS, dtype=jnp.int32).astype(jnp.float32)
    rising = 1.0 + 2.0 * rows / float(max(ROWS - 1, 1))
    return base * rising[None, :, None]


def draw_fixed_nodes(key, part):
    key = jax.random.fold_in(key, 23)
    key_level, key_coins, key_where, key_pick, key_chosen = jax.random.split(key, 5)
    block = 2 * MR
    nblocks = ROWS // block
    row_block = jnp.arange(ROWS, dtype=jnp.int32) // block
    level = jax.random.randint(key_level, (SECTIONS, nblocks), 1, 6)
    level_rows = jnp.take(level, row_block, axis=1)
    coins = jax.random.randint(key_coins, (SECTIONS, ROWS, NODE_COLS), 0, 16)
    scattered = (coins < level_rows[:, :, None]).astype(jnp.int32)
    where_block = jax.random.randint(key_where, (SECTIONS,), 0, nblocks)
    pick = jax.random.randint(key_pick, (SECTIONS,), 0, 2)
    chosen = jax.random.randint(key_chosen, (), 0, SECTIONS)
    sections = jnp.arange(SECTIONS, dtype=jnp.int32)
    active = (pick == 1) | (sections == chosen)
    whole = active[:, None] & (row_block[None, :] == where_block[:, None])
    return jnp.maximum(scattered, whole[:, :, None].astype(jnp.int32))


def with_ends(drawn, stream_key, smallest, largest):
    longest = drawn.shape.index(max(drawn.shape))
    spots = []
    for shift in (0, 1):
        where = [jax.random.randint(jax.random.fold_in(stream_key, axis), (), 0, length) for axis, length in enumerate(drawn.shape)]
        where[longest] = (where[longest] + shift) % drawn.shape[longest]
        spots.append(tuple(where))
    return drawn.at[spots[0]].set(smallest).at[spots[1]].set(largest)


def block_scale(rng, dims, shards, smallest, largest):
    factor_of, own = 1.0, jax.random.fold_in(rng, 6)
    for position, blocks in shards:
        heights = jnp.exp(jax.random.uniform(jax.random.fold_in(own, position), (blocks,), jnp.float32, smallest / len(shards), largest / len(shards)))
        factor_of = factor_of * jnp.repeat(heights, dims[position] // blocks).reshape([-1 if axis == position else 1 for axis in range(len(dims))])
    return factor_of


def centred(stream_key, shape, deviation, bound, cuts=(), held_as=jnp.bfloat16):
    array = deviation * jax.random.normal(stream_key, shape, jnp.float32)
    if cuts:
        array = array * block_scale(stream_key, shape, cuts, -0.22, 0.18)
    return jnp.clip(array, -bound, bound).astype(held_as)


def setup_inputs(seed: int = 0) -> dict:
    keys = jax.random.split(jax.random.key(seed), 6)
    image = centred(keys[0], (SECTIONS, IMG_ROWS, IMG_COLS), 1.0, 6.0, ((0, 32), (1, 16)))
    tissue_mask = with_ends((jax.random.randint(keys[1], (SECTIONS, IMG_ROWS, IMG_COLS), 0, 8) < 7).astype(jnp.int32), jax.random.fold_in(keys[1], 1), 0, 1)
    anchor = draw_anchor(jax.random.fold_in(keys[5], 71), 0)
    fixed_nodes = draw_fixed_nodes(jax.random.fold_in(keys[5], 71), 0)
    prior_shift = centred(keys[4], (2, SECTIONS, ROWS, NODE_COLS), 1.0, 6.0, ((1, 32), (2, 16)), jnp.float32)
    return dict(image=image, tissue_mask=tissue_mask, anchor=anchor, fixed_nodes=fixed_nodes, prior_shift=prior_shift)


def tables(size):
    j = jnp.arange(size, dtype=jnp.int32)
    angle = ((j[:, None] * j[None, :]) % size).astype(jnp.float32) * (2.0 * math.pi / size)
    return jnp.cos(angle).astype(jnp.bfloat16), jnp.sin(angle).astype(jnp.bfloat16)


def spectrum(block, cosine, sine):
    xf = block.astype(jnp.float32)
    cf = cosine.astype(jnp.float32)
    sf = sine.astype(jnp.float32)
    half_re = jnp.einsum('ki,bipj->bkpj', cf, xf).astype(jnp.bfloat16).astype(jnp.float32)
    half_im = (-jnp.einsum('ki,bipj->bkpj', sf, xf)).astype(jnp.bfloat16).astype(jnp.float32)
    spec_re = (jnp.einsum('bkpj,jl->bkpl', half_re, cf) + jnp.einsum('bkpj,jl->bkpl', half_im, sf)).astype(jnp.bfloat16)
    spec_im = (jnp.einsum('bkpj,jl->bkpl', half_im, cf) - jnp.einsum('bkpj,jl->bkpl', half_re, sf)).astype(jnp.bfloat16)
    return jnp.stack([spec_re, spec_im])


def correlate(own, other, cosine, sine):
    cf = cosine.astype(jnp.float32)
    sf = sine.astype(jnp.float32)
    a_re = own[0].astype(jnp.float32)
    a_im = own[1].astype(jnp.float32)
    b_re = other[0].astype(jnp.float32)
    b_im = other[1].astype(jnp.float32)
    cross_re = (a_re * b_re + a_im * b_im).astype(jnp.bfloat16).astype(jnp.float32)
    cross_im = (a_im * b_re - a_re * b_im).astype(jnp.bfloat16).astype(jnp.float32)
    back_re = (jnp.einsum('ki,bipj->bkpj', cf, cross_re) - jnp.einsum('ki,bipj->bkpj', sf, cross_im)).astype(jnp.bfloat16).astype(jnp.float32)
    back_im = (jnp.einsum('ki,bipj->bkpj', sf, cross_re) + jnp.einsum('ki,bipj->bkpj', cf, cross_im)).astype(jnp.bfloat16).astype(jnp.float32)
    corr = (jnp.einsum('bkpj,jl->bkpl', back_re, cf) - jnp.einsum('bkpj,jl->bkpl', back_im, sf)) / float(P_SIZE * P_SIZE)
    weight = corr * corr
    offset = (((jnp.arange(P_SIZE, dtype=jnp.int32) + P_SIZE // 2) % P_SIZE) - P_SIZE // 2).astype(jnp.float32)
    total = jnp.mean(weight, axis=(1, 3)) + 1e-6
    row_flow = jnp.mean(weight * offset[None, :, None, None], axis=(1, 3)) / total
    col_flow = jnp.mean(weight * offset[None, None, None, :], axis=(1, 3)) / total
    return jnp.stack([row_flow, col_flow])


def operate(field, anchor, free, fixed):
    moved = free * field
    padded = jnp.pad(moved, ((0, 0), (0, 0), (1, 1), (1, 1)))
    beside = padded[:, :, 2:, 1:-1] + padded[:, :, :-2, 1:-1] + padded[:, :, 1:-1, 2:] + padded[:, :, 1:-1, :-2]
    return free * ((4.0 + anchor) * field - beside) + fixed * field


def reference(image, tissue_mask, anchor, fixed_nodes, prior_shift):
    cosine, sine = tables(P_SIZE)
    bands = image.shape[1] // P_SIZE
    masked = (image.astype(jnp.float32) * tissue_mask.astype(jnp.float32)).astype(jnp.bfloat16)
    masked = masked.reshape(SECTIONS, bands, P_SIZE, NPATCH, P_SIZE)

    def visit(carry, section):
        own = spectrum(section, cosine, sine)
        return own, correlate(own, carry, cosine, sine)

    start = jnp.zeros((2, bands, P_SIZE, NPATCH, P_SIZE), jnp.bfloat16)
    _, flows = lax.scan(visit, start, masked, reverse=True)
    flows = jnp.transpose(flows, (1, 0, 2, 3))
    target = jnp.repeat(jnp.repeat(flows, MR, axis=2), NODES_PATCH, axis=3)
    free = (1 - fixed_nodes).astype(jnp.float32)[None]
    fixed = fixed_nodes.astype(jnp.float32)[None]
    anchor_f = anchor[None]
    rhs = free * anchor_f * (target + prior_shift)
    solution = jnp.zeros_like(rhs)
    residual = rhs
    direction = rhs
    norm_now = jnp.sum(residual * residual, axis=(2, 3), keepdims=True)
    for step in range(ITERS):
        image_dir = operate(direction, anchor_f, free, fixed)
        alpha = norm_now / jnp.sum(direction * image_dir, axis=(2, 3), keepdims=True)
        solution = solution + alpha * direction
        residual = residual - alpha * image_dir
        norm_next = jnp.sum(residual * residual, axis=(2, 3), keepdims=True)
        direction = residual + (norm_next / norm_now) * direction
        norm_now = norm_next
    return solution
```

```python
import functools
import math

import jax
import jax.numpy as jnp
import ml_dtypes
import numpy as np
from jax import lax
from jax.experimental import pallas as pl
from jax.experimental.pallas import tpu as pltpu
from jax.sharding import PartitionSpec as P

MESH = pl.DeviceIdType.MESH
ITERS = 4
SIZE = 128
PAIR = 2 * SIZE
LANES = 128
EDGE = 8
SPAN = 4
SHIFTS = (1.0, 4.0, 1.0, 4.0)
SCALE = 0.25
PAIRS = tuple((i, j) for i in range(ITERS) for j in range(i, ITERS)) + tuple((i, ITERS) for i in range(ITERS))


def tables():
    j = np.arange(SIZE)
    angle = (j[:, None] * j[None, :] % SIZE).astype(np.float32) * np.float32(2.0 * math.pi / SIZE)
    cosine = np.cos(angle).astype(ml_dtypes.bfloat16)
    sine = np.sin(angle).astype(ml_dtypes.bfloat16)
    both = np.block([[cosine, -sine], [sine, cosine]])
    return both, np.concatenate([cosine, -sine], axis=0)


def matmul(left, right):
    return jnp.dot(left, right, preferred_element_type=jnp.float32)


def beside(pair):
    rows = [
        jnp.concatenate([pair[:SIZE, p * SIZE : (p + 1) * SIZE], pair[SIZE:, p * SIZE : (p + 1) * SIZE]], axis=1)
        for p in range(2)
    ]
    return jnp.concatenate(rows, axis=0)


def stacked(re, im):
    rows = [jnp.concatenate([part[:SIZE], part[SIZE:]], axis=1) for part in (re, im)]
    return jnp.concatenate(rows, axis=0)


def spectrum(block, narrow, both):
    half = matmul(narrow, block).astype(jnp.bfloat16)
    return matmul(beside(half), both).astype(jnp.bfloat16)


def offsets(shape, axis):
    index = lax.broadcasted_iota(jnp.int32, shape, axis)
    return (((index + SIZE // 2) % SIZE) - SIZE // 2).astype(jnp.float32)


def flows_of(own, other, narrow, both):
    a = own.astype(jnp.float32)
    b = other.astype(jnp.float32)
    a_re, a_im, b_re, b_im = a[:, :SIZE], a[:, SIZE:], b[:, :SIZE], b[:, SIZE:]
    cross_re = (a_re * b_re + a_im * b_im).astype(jnp.bfloat16)
    cross_im = (a_im * b_re - a_re * b_im).astype(jnp.bfloat16)
    back = matmul(both, stacked(cross_re, cross_im)).astype(jnp.bfloat16)
    corr = matmul(beside(back), narrow)
    weight = (corr * corr).reshape(2, SIZE, SIZE)
    whole = jnp.sum(weight, axis=1)
    tilted = jnp.sum(weight * offsets((1, SIZE, SIZE), 1), axis=1)
    unit = 2.0**-42
    total = jnp.sum(whole, axis=1, keepdims=True) * unit + 1e-6
    row_flow = jnp.sum(tilted, axis=1, keepdims=True) * unit / total
    col_flow = jnp.sum(whole * offsets((2, SIZE), 1), axis=1, keepdims=True) * unit / total
    return row_flow, col_flow


def neighbours(value):
    tiles, rows, _ = value.shape
    lane = lax.broadcasted_iota(jnp.int32, value.shape, 2)
    none = jnp.zeros((1, rows, LANES), value.dtype)
    right = pltpu.roll(value, 1, 2)
    right = jnp.where(lane == 0, jnp.concatenate([none, right[:-1]], axis=0), right)
    left = pltpu.roll(value, LANES - 1, 2)
    left = jnp.where(lane == LANES - 1, jnp.concatenate([left[1:], none], axis=0), left)
    return pltpu.roll(value, 1, 1) + pltpu.roll(value, rows - 1, 1) + right + left


def coefficients(gram):
    def inner(left, right):
        terms = [l * r * gram[min(i, j), max(i, j)] for i, l in enumerate(left) for j, r in enumerate(right)]
        return functools.reduce(lambda p, q: p + q, terms)

    zero = jnp.zeros_like(gram[0, 0])
    solution = [zero] * ITERS
    residual = [jnp.ones_like(zero)]
    direction = list(residual)
    norm_now = gram[0, 0]
    for step in range(ITERS):
        image = [SHIFTS[j] * direction[j] for j in range(step + 1)] + [zero]
        image = [image[j] + (direction[j - 1] / SCALE if j else 0.0) for j in range(step + 2)]
        curve = inner(direction, image)
        alpha = jnp.where(curve > 0.0, jnp.clip(norm_now / curve, 0.0, 10.1), 0.0)
        solution = [solution[j] + alpha * direction[j] if j <= step else solution[j] for j in range(ITERS)]
        if step == ITERS - 1:
            break
        residual = [r - alpha * i for r, i in zip(residual + [zero], image)]
        norm_next = jnp.maximum(inner(residual, residual), 0.0)
        beta = jnp.where(norm_now > 0.0, norm_next / norm_now, 0.0)
        direction = [r + beta * d for r, d in zip(residual, direction + [zero])]
        norm_now = norm_next
    return solution


def kernel(
    sections,
    bands,
    image_hbm,
    mask_hbm,
    anchor_hbm,
    fixed_hbm,
    prior_hbm,
    both_hbm,
    narrow_hbm,
    out_ref,
    image,
    mask,
    masked,
    arrived,
    spectra,
    both,
    narrow,
    anchor,
    fixed,
    prior,
    edge_out,
    edge_in,
    pull,
    diag,
    link,
    base,
    flow,
    flow_in,
    basis,
    share,
    shares,
    load_sem,
    mesh_sem,
    send_sem,
    recv_sem,
    edge_send,
    edge_recv,
    flow_send,
    flow_recv,
    share_send,
    share_recv,
):
    chunks = image.shape[0]
    tiles = pull.shape[0]
    rows = anchor.shape[0]
    sec = lax.axis_index("sec")
    blk = lax.axis_index("blk")
    has_above, has_below = blk > 0, blk < bands - 1
    has_prev, has_next = sec > 0, sec < sections - 1
    others = [lax.rem(blk + d, bands) for d in range(1, bands)]

    def pixels(c):
        return pl.ds(pl.multiple_of(c * PAIR, PAIR), PAIR)

    def loads(c):
        return (
            pltpu.make_async_copy(image_hbm.at[0, :, pixels(c)], image.at[c], load_sem.at[0, c]),
            pltpu.make_async_copy(mask_hbm.at[0, :, pixels(c)], mask.at[c], load_sem.at[1, c]),
        )

    def sent(c):
        return pltpu.make_async_remote_copy(
            masked.at[c], arrived.at[c], send_sem.at[c], recv_sem.at[c], device_id={"sec": sec - 1}, device_id_type=MESH
        )

    mesh_loads = [
        pltpu.make_async_copy(both_hbm, both, mesh_sem.at[0]),
        pltpu.make_async_copy(narrow_hbm, narrow, mesh_sem.at[1]),
        pltpu.make_async_copy(anchor_hbm.at[0], anchor, mesh_sem.at[2]),
        pltpu.make_async_copy(fixed_hbm.at[0], fixed, mesh_sem.at[3]),
        pltpu.make_async_copy(prior_hbm.at[:, 0], prior, mesh_sem.at[4]),
    ]

    barrier = pltpu.get_barrier_semaphore()

    def greet(device):
        pl.semaphore_signal(barrier, inc=1, device_id=device, device_id_type=MESH)

    pl.when(has_prev)(lambda: greet({"sec": sec - 1}))
    pl.when(has_next)(lambda: greet({"sec": sec + 1}))
    for other in others:
        greet({"blk": other})

    def start_loads(c, _):
        for copy in loads(c):
            copy.start()
        return 0

    lax.fori_loop(0, 4, start_loads, 0)
    for copy in mesh_loads:
        copy.start()
    lax.fori_loop(4, chunks, start_loads, 0)

    def hide(c):
        for copy in loads(c):
            copy.wait()
        masked[c] = image[c] * mask[c].astype(jnp.float32).astype(jnp.bfloat16)

    def hide_and_send(c, _):
        hide(c)
        pl.when(has_prev)(lambda: sent(c).start())
        return 0

    hide(0)
    pl.semaphore_wait(barrier, bands - 1 + has_prev.astype(jnp.int32) + has_next.astype(jnp.int32))
    pl.when(has_prev)(lambda: sent(0).start())
    lax.fori_loop(1, 4, hide_and_send, 0)

    for copy in mesh_loads:
        copy.wait()
    free = 1.0 - fixed[...].astype(jnp.float32)
    own_pull = free * anchor[...]
    own = [own_pull, own_pull * prior[0], own_pull * prior[1]]

    def edge_copy(up):
        slot = 0 if up else 1
        return pltpu.make_async_remote_copy(
            edge_out.at[slot],
            edge_in.at[slot],
            edge_send.at[slot],
            edge_recv.at[slot],
            device_id={"blk": blk - 1 if up else blk + 1},
            device_id_type=MESH,
        )

    def flow_copy(up):
        slot = 0 if up else 1
        return pltpu.make_async_remote_copy(
            flow,
            flow_in.at[slot],
            flow_send.at[slot],
            flow_recv.at[slot],
            device_id={"blk": blk - 1 if up else blk + 1},
            device_id_type=MESH,
        )

    width = 3 * tiles * LANES // 4

    def packed(first):
        flat = jnp.concatenate([part[first : first + SPAN] for part in own], axis=1)
        return jnp.concatenate([flat[:, k * width : (k + 1) * width] for k in range(4)], axis=0).astype(jnp.bfloat16)

    def unpacked(block):
        block = block.astype(jnp.float32)
        flat = jnp.concatenate([block[k * SPAN : (k + 1) * SPAN] for k in range(4)], axis=1)
        return [flat[:, k * tiles * LANES : (k + 1) * tiles * LANES] for k in range(3)]

    edge_out[0] = packed(0)
    edge_out[1] = packed(rows - SPAN)
    pl.when(has_above)(lambda: edge_copy(True).start())
    pl.when(has_below)(lambda: edge_copy(False).start())
    lax.fori_loop(4, chunks, hide_and_send, 0)

    def own_spectrum(c, _):
        spectra[c] = spectrum(masked[c], narrow[...], both[...])
        return 0

    lax.fori_loop(0, chunks, own_spectrum, 0)

    pull[...] = jnp.zeros_like(pull)
    base[...] = jnp.zeros_like(base)
    for g in range(tiles):
        at = slice(g * LANES, (g + 1) * LANES)
        pull[g, EDGE : EDGE + rows] = own[0][:, at]
        base[0, g, EDGE : EDGE + rows] = own[1][:, at]
        base[1, g, EDGE : EDGE + rows] = own[2][:, at]

    def take_edge(slot, first):
        parts = unpacked(edge_in[slot])
        for g in range(tiles):
            at = slice(g * LANES, (g + 1) * LANES)
            pull[g, first : first + SPAN] = parts[0][:, at]
            base[0, g, first : first + SPAN] = parts[1][:, at]
            base[1, g, first : first + SPAN] = parts[2][:, at]

    @pl.when(has_below)
    def _():
        edge_copy(True).wait_recv()
        take_edge(0, EDGE + rows)

    @pl.when(has_above)
    def _():
        edge_copy(False).wait_recv()
        take_edge(1, EDGE - SPAN)

    loose = jnp.where(pull[...] > 0.0, SCALE, 0.0)
    link[...] = loose
    diag[...] = 4.0 * loose + SCALE * pull[...]

    flow[...] = jnp.zeros_like(flow)
    tile_row = lax.broadcasted_iota(jnp.int32, (tiles, LANES), 0)
    quarter = lax.broadcasted_iota(jnp.int32, (tiles, LANES), 1) // (LANES // 4)

    def correlate(c, _):
        sent(c).wait_recv()
        other = spectrum(arrived[c], narrow[...], both[...])
        for k, value in enumerate(flows_of(spectra[c], other, narrow[...], both[...])):
            held = flow[k]
            for p in range(2):
                here = (tile_row == c // 2) & (quarter == 2 * (c % 2) + p)
                held = jnp.where(here, value[p : p + 1], held)
            flow[k] = held
        return 0

    @pl.when(has_next)
    def _():
        lax.fori_loop(0, chunks, correlate, 0)

    pl.when(has_above)(lambda: flow_copy(True).start())
    pl.when(has_below)(lambda: flow_copy(False).start())

    @pl.when(has_below)
    def _():
        flow_copy(True).wait_recv()

    @pl.when(has_above)
    def _():
        flow_copy(False).wait_recv()

    @pl.when(jnp.logical_not(has_below))
    def _():
        flow_in[0] = jnp.zeros_like(flow)

    @pl.when(jnp.logical_not(has_above))
    def _():
        flow_in[1] = jnp.zeros_like(flow)

    for k in range(2):
        for g in range(tiles):
            for source, first, count in (
                (flow_in.at[1], 0, EDGE),
                (flow, EDGE, rows),
                (flow_in.at[0], EDGE + rows, EDGE),
            ):
                at = slice(first, first + count)
                basis[k, 0, g, at] = base[k, g, at] + pull[g, at] * source[k, g : g + 1, :]

    lane = lax.broadcasted_iota(jnp.int32, (8, LANES), 1)
    sums = []
    for k in range(2):
        for step in range(ITERS):
            value = basis[k, step]
            basis[k, step + 1] = (diag[...] - SCALE * SHIFTS[step]) * value - link[...] * neighbours(value)
        lines = []
        for i, j in PAIRS:
            product = basis[k, i, :, EDGE : EDGE + rows] * basis[k, j, :, EDGE : EDGE + rows]
            total = jnp.sum(product.reshape(tiles * rows // 8, 8, LANES), axis=0)
            lines.append(jnp.sum(total, axis=0, keepdims=True))
        lines += [jnp.zeros((1, LANES), jnp.float32)] * (16 - len(lines))
        for half in range(2):
            block = jnp.concatenate(lines[8 * half : 8 * half + 8], axis=0)
            block = block + pltpu.roll(block, LANES // 2, 1)
            sums.append(block + pltpu.roll(block, LANES // 4, 1))
    part = lane // (LANES // 4)
    mine = sums[3]
    for n in range(3):
        mine = jnp.where(part == n, sums[n], mine)
    share[...] = mine

    def share_copy(n):
        return pltpu.make_async_remote_copy(
            share,
            shares.at[blk],
            share_send.at[n],
            share_recv.at[n],
            device_id={"blk": others[n]},
            device_id_type=MESH,
        )

    for n in range(bands - 1):
        share_copy(n).start()
    shares[blk] = share[...]
    for n in range(bands - 1):
        share_copy(n).wait_recv()
    total = jnp.sum(shares[...], axis=0)
    quarters = [jnp.sum(jnp.where(part == n, total, 0.0), axis=1, keepdims=True) for n in range(4)]
    gram = {}
    for n, pair in enumerate(PAIRS):
        line = [quarters[2 * k + n // 8][n % 8 : n % 8 + 1] for k in range(2)]
        gram[pair] = jnp.where(lane[:1] < LANES // 2, line[0], line[1])
    found = coefficients(gram)
    for k in range(2):
        weights = [value[:, k * LANES // 2 : k * LANES // 2 + 1] for value in found]
        for g in range(tiles):
            at = slice(EDGE, EDGE + rows)
            value = weights[0] * basis[k, 0, g, at]
            for step in range(1, ITERS):
                value = value + weights[step] * basis[k, step, g, at]
            out_ref[k, :, g * LANES : (g + 1) * LANES] = value

    for n in range(bands - 1):
        share_copy(n).wait_send()

    @pl.when(has_above)
    def _():
        edge_copy(True).wait_send()
        flow_copy(True).wait_send()

    @pl.when(has_below)
    def _():
        edge_copy(False).wait_send()
        flow_copy(False).wait_send()

    def drain(c, _):
        sent(c).wait_send()
        return 0

    @pl.when(has_prev)
    def _():
        lax.fori_loop(0, chunks, drain, 0)


def per_device(sections, bands, image, tissue_mask, anchor, fixed_nodes, prior_shift):
    _, size, columns = image.shape
    _, rows, nodes = anchor.shape
    chunks = columns // PAIR
    tiles = nodes // LANES
    wide = 2 * EDGE + rows
    width = 3 * nodes // 4
    both, narrow = tables()
    out = pl.pallas_call(
        functools.partial(kernel, sections, bands),
        out_shape=jax.ShapeDtypeStruct((2, rows, nodes), jnp.float32),
        in_specs=[pl.BlockSpec(memory_space=pl.ANY)] * 7,
        out_specs=pl.BlockSpec(memory_space=pltpu.VMEM),
        scratch_shapes=[
            pltpu.VMEM((chunks, size, PAIR), jnp.bfloat16),
            pltpu.VMEM((chunks, size, PAIR), jnp.int32),
            pltpu.VMEM((chunks, size, PAIR), jnp.bfloat16),
            pltpu.VMEM((chunks, size, PAIR), jnp.bfloat16),
            pltpu.VMEM((chunks, PAIR, PAIR), jnp.bfloat16),
            pltpu.VMEM((PAIR, PAIR), jnp.bfloat16),
            pltpu.VMEM((PAIR, SIZE), jnp.bfloat16),
            pltpu.VMEM((rows, nodes), jnp.float32),
            pltpu.VMEM((rows, nodes), jnp.int32),
            pltpu.VMEM((2, rows, nodes), jnp.float32),
            pltpu.VMEM((2, 4 * SPAN, width), jnp.bfloat16),
            pltpu.VMEM((2, 4 * SPAN, width), jnp.bfloat16),
            pltpu.VMEM((tiles, wide, LANES), jnp.float32),
            pltpu.VMEM((tiles, wide, LANES), jnp.float32),
            pltpu.VMEM((tiles, wide, LANES), jnp.float32),
            pltpu.VMEM((2, tiles, wide, LANES), jnp.float32),
            pltpu.VMEM((2, tiles, LANES), jnp.float32),
            pltpu.VMEM((2, 2, tiles, LANES), jnp.float32),
            pltpu.VMEM((2, ITERS + 1, tiles, wide, LANES), jnp.float32),
            pltpu.VMEM((8, LANES), jnp.float32),
            pltpu.VMEM((bands, 8, LANES), jnp.float32),
            pltpu.SemaphoreType.DMA((2, chunks)),
            pltpu.SemaphoreType.DMA((5,)),
            pltpu.SemaphoreType.DMA((chunks,)),
            pltpu.SemaphoreType.DMA((chunks,)),
            pltpu.SemaphoreType.DMA((2,)),
            pltpu.SemaphoreType.DMA((2,)),
            pltpu.SemaphoreType.DMA((2,)),
            pltpu.SemaphoreType.DMA((2,)),
            pltpu.SemaphoreType.DMA((bands - 1,)),
            pltpu.SemaphoreType.DMA((bands - 1,)),
        ],
        compiler_params=pltpu.CompilerParams(
            collective_id=0, has_side_effects=True, vmem_limit_bytes=40 * 1024 * 1024
        ),
        cost_estimate=pl.CostEstimate(flops=2_400_000_000, bytes_accessed=4_000_000, transcendentals=0),
    )(image, tissue_mask, anchor, fixed_nodes, prior_shift, jnp.asarray(both), jnp.asarray(narrow))
    return out[:, None]


def solution(mesh):
    sections, bands = mesh.shape["sec"], mesh.shape["blk"]
    return jax.shard_map(
        functools.partial(per_device, sections, bands),
        mesh=mesh,
        in_specs=(
            P("sec", "blk", None),
            P("sec", "blk", None),
            P("sec", "blk", None),
            P("sec", "blk", None),
            P(None, "sec", "blk", None),
        ),
        out_specs=P(None, "sec", "blk", None),
        check_vma=False,
    )
```

```python
import functools
import math

import jax
import jax.numpy as jnp
import ml_dtypes
import numpy as np
from jax import lax
from jax.experimental import pallas as pl
from jax.experimental.pallas import tpu as pltpu
from jax.sharding import PartitionSpec as P

MESH = pl.DeviceIdType.MESH
ITERS = 4
SIZE = 128
PAIR = 2 * SIZE
LANES = 128
EDGE = 8
SPAN = 4
SHIFTS = (1.0, 4.0, 1.0, 4.0)
SCALE = 0.25
PAIRS = tuple((i, j) for i in range(ITERS) for j in range(i, ITERS)) + tuple((i, ITERS) for i in range(ITERS))


def tables():
    j = np.arange(SIZE)
    angle = (j[:, None] * j[None, :] % SIZE).astype(np.float32) * np.float32(2.0 * math.pi / SIZE)
    cosine = np.cos(angle).astype(ml_dtypes.bfloat16)
    sine = np.sin(angle).astype(ml_dtypes.bfloat16)
    both = np.block([[cosine, -sine], [sine, cosine]])
    return both, np.concatenate([cosine, -sine], axis=0)


def matmul(left, right):
    return jnp.dot(left, right, preferred_element_type=jnp.float32)


def beside(pair):
    rows = [
        jnp.concatenate([pair[:SIZE, p * SIZE : (p + 1) * SIZE], pair[SIZE:, p * SIZE : (p + 1) * SIZE]], axis=1)
        for p in range(2)
    ]
    return jnp.concatenate(rows, axis=0)


def stacked(re, im):
    rows = [jnp.concatenate([part[:SIZE], part[SIZE:]], axis=1) for part in (re, im)]
    return jnp.concatenate(rows, axis=0)


def spectrum(block, narrow, both):
    half = matmul(narrow, block).astype(jnp.bfloat16)
    return matmul(beside(half), both).astype(jnp.bfloat16)


def offsets(shape, axis):
    index = lax.broadcasted_iota(jnp.int32, shape, axis)
    return (((index + SIZE // 2) % SIZE) - SIZE // 2).astype(jnp.float32)


def flows_of(own, other, narrow, both):
    a = own.astype(jnp.float32)
    b = other.astype(jnp.float32)
    a_re, a_im, b_re, b_im = a[:, :SIZE], a[:, SIZE:], b[:, :SIZE], b[:, SIZE:]
    cross_re = (a_re * b_re + a_im * b_im).astype(jnp.bfloat16)
    cross_im = (a_im * b_re - a_re * b_im).astype(jnp.bfloat16)
    back = matmul(both, stacked(cross_re, cross_im)).astype(jnp.bfloat16)
    corr = matmul(beside(back), narrow)
    weight = (corr * corr).reshape(2, SIZE, SIZE)
    whole = jnp.sum(weight, axis=1)
    tilted = jnp.sum(weight * offsets((1, SIZE, SIZE), 1), axis=1)
    unit = 2.0**-42
    total = jnp.sum(whole, axis=1, keepdims=True) * unit + 1e-6
    row_flow = jnp.sum(tilted, axis=1, keepdims=True) * unit / total
    col_flow = jnp.sum(whole * offsets((2, SIZE), 1), axis=1, keepdims=True) * unit / total
    return row_flow, col_flow


def neighbours(value):
    tiles, rows, _ = value.shape
    lane = lax.broadcasted_iota(jnp.int32, value.shape, 2)
    none = jnp.zeros((1, rows, LANES), value.dtype)
    right = pltpu.roll(value, 1, 2)
    right = jnp.where(lane == 0, jnp.concatenate([none, right[:-1]], axis=0), right)
    left = pltpu.roll(value, LANES - 1, 2)
    left = jnp.where(lane == LANES - 1, jnp.concatenate([left[1:], none], axis=0), left)
    return pltpu.roll(value, 1, 1) + pltpu.roll(value, rows - 1, 1) + right + left


def coefficients(gram):
    def inner(left, right):
        terms = [l * r * gram[min(i, j), max(i, j)] for i, l in enumerate(left) for j, r in enumerate(right)]
        return functools.reduce(lambda p, q: p + q, terms)

    zero = jnp.zeros_like(gram[0, 0])
    solution = [zero] * ITERS
    residual = [jnp.ones_like(zero)]
    direction = list(residual)
    norm_now = gram[0, 0]
    for step in range(ITERS):
        image = [SHIFTS[j] * direction[j] for j in range(step + 1)] + [zero]
        image = [image[j] + (direction[j - 1] / SCALE if j else 0.0) for j in range(step + 2)]
        curve = inner(direction, image)
        alpha = jnp.where(curve > 0.0, jnp.clip(norm_now / curve, 0.0, 10.1), 0.0)
        solution = [solution[j] + alpha * direction[j] if j <= step else solution[j] for j in range(ITERS)]
        if step == ITERS - 1:
            break
        residual = [r - alpha * i for r, i in zip(residual + [zero], image)]
        norm_next = jnp.maximum(inner(residual, residual), 0.0)
        beta = jnp.where(norm_now > 0.0, norm_next / norm_now, 0.0)
        direction = [r + beta * d for r, d in zip(residual, direction + [zero])]
        norm_now = norm_next
    return solution


def kernel(
    sections,
    bands,
    image_hbm,
    mask_hbm,
    anchor_hbm,
    fixed_hbm,
    prior_hbm,
    both_hbm,
    narrow_hbm,
    out_ref,
    image,
    mask,
    masked,
    arrived,
    spectra,
    both,
    narrow,
    anchor,
    fixed,
    prior,
    edge_out,
    edge_in,
    pull,
    diag,
    link,
    base,
    flow,
    flow_in,
    basis,
    share,
    shares,
    load_sem,
    mesh_sem,
    send_sem,
    recv_sem,
    edge_send,
    edge_recv,
    flow_send,
    flow_recv,
    share_send,
    share_recv,
    round_sem,
):
    chunks = image.shape[0]
    tiles = pull.shape[0]
    rows = anchor.shape[0]
    sec = lax.axis_index("sec")
    blk = lax.axis_index("blk")
    has_above, has_below = blk > 0, blk < bands - 1
    has_prev, has_next = sec > 0, sec < sections - 1
    turns = bands // 4
    here = (blk // 4, lax.rem(blk // 2, 2), lax.rem(blk, 2))

    def moved(dx, dy, dc):
        return lax.rem(here[0] + dx, turns) * 4 + lax.rem(here[1] + dy, 2) * 2 + lax.rem(here[2] + dc, 2)

    order = [dx if dx <= turns // 2 else dx - turns for dx in range(turns)]
    steps = sorted(
        ((dx % turns, dy, dc) for dx in order for dy in range(2) for dc in range(2)),
        key=lambda step: (-step[1], -min(step[0], turns - step[0]), -step[2]),
    )
    others = [moved(*step) for step in steps if any(step)]

    def pixels(c):
        return pl.ds(pl.multiple_of(c * PAIR, PAIR), PAIR)

    def loads(c):
        return (
            pltpu.make_async_copy(image_hbm.at[0, :, pixels(c)], image.at[c], load_sem.at[0, c]),
            pltpu.make_async_copy(mask_hbm.at[0, :, pixels(c)], mask.at[c], load_sem.at[1, c]),
        )

    def sent(c):
        return pltpu.make_async_remote_copy(
            masked.at[c], arrived.at[c], send_sem.at[c], recv_sem.at[c], device_id={"sec": sec - 1}, device_id_type=MESH
        )

    mesh_loads = [
        pltpu.make_async_copy(both_hbm, both, mesh_sem.at[0]),
        pltpu.make_async_copy(narrow_hbm, narrow, mesh_sem.at[1]),
        pltpu.make_async_copy(anchor_hbm.at[0], anchor, mesh_sem.at[2]),
        pltpu.make_async_copy(fixed_hbm.at[0], fixed, mesh_sem.at[3]),
        pltpu.make_async_copy(prior_hbm.at[:, 0], prior, mesh_sem.at[4]),
    ]

    barrier = pltpu.get_barrier_semaphore()

    def greet(device):
        pl.semaphore_signal(barrier, inc=1, device_id=device, device_id_type=MESH)

    pl.when(has_prev)(lambda: greet({"sec": sec - 1}))
    pl.when(has_next)(lambda: greet({"sec": sec + 1}))
    pl.when(has_above)(lambda: greet({"blk": blk - 1}))
    pl.when(has_below)(lambda: greet({"blk": blk + 1}))
    across, over = moved(0, 0, 1), moved(0, 1, 0)
    along = [moved(dx, 0, 0) for dx in range(1, turns)]
    for other in [across, over] + along:
        greet({"blk": other})

    def start_loads(c, _):
        for copy in loads(c):
            copy.start()
        return 0

    lax.fori_loop(0, 1, start_loads, 0)
    for copy in mesh_loads:
        copy.start()
    lax.fori_loop(1, chunks, start_loads, 0)

    def hide(c):
        for copy in loads(c):
            copy.wait()
        masked[c] = image[c] * mask[c].astype(jnp.float32).astype(jnp.bfloat16)

    def hide_and_send(c, _):
        hide(c)
        pl.when(has_prev)(lambda: sent(c).start())
        return 0

    hide(0)
    for copy in mesh_loads:
        copy.wait()
    free = 1.0 - fixed[...].astype(jnp.float32)
    own_pull = free * anchor[...]
    own = [own_pull, own_pull * prior[0], own_pull * prior[1]]

    def edge_copy(up):
        slot = 0 if up else 1
        return pltpu.make_async_remote_copy(
            edge_out.at[slot],
            edge_in.at[slot],
            edge_send.at[slot],
            edge_recv.at[slot],
            device_id={"blk": blk - 1 if up else blk + 1},
            device_id_type=MESH,
        )

    def flow_copy(up):
        slot = 0 if up else 1
        return pltpu.make_async_remote_copy(
            flow,
            flow_in.at[slot],
            flow_send.at[slot],
            flow_recv.at[slot],
            device_id={"blk": blk - 1 if up else blk + 1},
            device_id_type=MESH,
        )

    width = 3 * tiles * LANES // 4

    def packed(first):
        flat = jnp.concatenate([part[first : first + SPAN] for part in own], axis=1)
        return jnp.concatenate([flat[:, k * width : (k + 1) * width] for k in range(4)], axis=0).astype(jnp.bfloat16)

    def unpacked(block):
        block = block.astype(jnp.float32)
        flat = jnp.concatenate([block[k * SPAN : (k + 1) * SPAN] for k in range(4)], axis=1)
        return [flat[:, k * tiles * LANES : (k + 1) * tiles * LANES] for k in range(3)]

    edge_out[0] = packed(0)
    edge_out[1] = packed(rows - SPAN)
    greeted = has_prev, has_next, has_above, has_below
    pl.semaphore_wait(barrier, turns + 1 + functools.reduce(lambda p, q: p + q, [g.astype(jnp.int32) for g in greeted]))
    pl.when(has_above)(lambda: edge_copy(True).start())
    pl.when(has_below)(lambda: edge_copy(False).start())
    pl.when(has_prev)(lambda: sent(0).start())
    pl.semaphore_signal(round_sem.at[0], inc=1, device_id={"blk": across}, device_id_type=MESH)
    lax.fori_loop(1, 8, hide_and_send, 0)
    pl.semaphore_wait(round_sem.at[0], 1)
    pl.semaphore_signal(round_sem.at[1], inc=1, device_id={"blk": over}, device_id_type=MESH)
    lax.fori_loop(8, chunks, hide_and_send, 0)

    def own_spectrum(c, _):
        spectra[c] = spectrum(masked[c], narrow[...], both[...])
        return 0

    lax.fori_loop(0, chunks, own_spectrum, 0)
    pl.semaphore_wait(round_sem.at[1], 1)

    pull[...] = jnp.zeros_like(pull)
    base[...] = jnp.zeros_like(base)
    for g in range(tiles):
        at = slice(g * LANES, (g + 1) * LANES)
        pull[g, EDGE : EDGE + rows] = own[0][:, at]
        base[0, g, EDGE : EDGE + rows] = own[1][:, at]
        base[1, g, EDGE : EDGE + rows] = own[2][:, at]

    def take_edge(slot, first):
        parts = unpacked(edge_in[slot])
        for g in range(tiles):
            at = slice(g * LANES, (g + 1) * LANES)
            pull[g, first : first + SPAN] = parts[0][:, at]
            base[0, g, first : first + SPAN] = parts[1][:, at]
            base[1, g, first : first + SPAN] = parts[2][:, at]

    flow[...] = jnp.zeros_like(flow)
    tile_row = lax.broadcasted_iota(jnp.int32, (tiles, LANES), 0)
    quarter = lax.broadcasted_iota(jnp.int32, (tiles, LANES), 1) // (LANES // 4)

    def correlate(c, _):
        sent(c).wait_recv()
        other = spectrum(arrived[c], narrow[...], both[...])
        for k, value in enumerate(flows_of(spectra[c], other, narrow[...], both[...])):
            held = flow[k]
            for p in range(2):
                spot = (tile_row == c // 2) & (quarter == 2 * (c % 2) + p)
                held = jnp.where(spot, value[p : p + 1], held)
            flow[k] = held
        return 0

    late = chunks * 3 // 4

    @pl.when(has_next)
    def _():
        lax.fori_loop(0, late, correlate, 0)

    @pl.when(has_below)
    def _():
        edge_copy(True).wait_recv()
        take_edge(0, EDGE + rows)

    @pl.when(has_above)
    def _():
        edge_copy(False).wait_recv()
        take_edge(1, EDGE - SPAN)

    loose = jnp.where(pull[...] > 0.0, SCALE, 0.0)
    link[...] = loose
    diag[...] = 4.0 * loose + SCALE * pull[...]

    @pl.when(has_next)
    def _():
        lax.fori_loop(late, chunks, correlate, 0)

    pl.when(has_above)(lambda: flow_copy(True).start())
    pl.when(has_below)(lambda: flow_copy(False).start())

    @pl.when(has_below)
    def _():
        flow_copy(True).wait_recv()

    @pl.when(has_above)
    def _():
        flow_copy(False).wait_recv()

    @pl.when(jnp.logical_not(has_below))
    def _():
        flow_in[0] = jnp.zeros_like(flow)

    @pl.when(jnp.logical_not(has_above))
    def _():
        flow_in[1] = jnp.zeros_like(flow)

    for k in range(2):
        for g in range(tiles):
            for source, first, count in (
                (flow_in.at[1], 0, EDGE),
                (flow, EDGE, rows),
                (flow_in.at[0], EDGE + rows, EDGE),
            ):
                at = slice(first, first + count)
                basis[k, 0, g, at] = base[k, g, at] + pull[g, at] * source[k, g : g + 1, :]

    lane = lax.broadcasted_iota(jnp.int32, (8, LANES), 1)
    sums = []
    for k in range(2):
        for step in range(ITERS):
            value = basis[k, step]
            basis[k, step + 1] = (diag[...] - SCALE * SHIFTS[step]) * value - link[...] * neighbours(value)
        lines = []
        for i, j in PAIRS:
            product = basis[k, i, :, EDGE : EDGE + rows] * basis[k, j, :, EDGE : EDGE + rows]
            total = jnp.sum(product.reshape(tiles * rows // 8, 8, LANES), axis=0)
            lines.append(jnp.sum(total, axis=0, keepdims=True))
        lines += [jnp.zeros((1, LANES), jnp.float32)] * (16 - len(lines))
        for half in range(2):
            block = jnp.concatenate(lines[8 * half : 8 * half + 8], axis=0)
            block = block + pltpu.roll(block, LANES // 2, 1)
            sums.append(block + pltpu.roll(block, LANES // 4, 1))
    part = lane // (LANES // 4)
    mine = sums[3]
    for n in range(3):
        mine = jnp.where(part == n, sums[n], mine)
    share[...] = mine

    def share_copy(n):
        return pltpu.make_async_remote_copy(
            share,
            shares.at[blk],
            share_send.at[n],
            share_recv.at[n],
            device_id={"blk": others[n]},
            device_id_type=MESH,
        )

    for n in range(bands - 1):
        share_copy(n).start()
    shares[blk] = share[...]
    for n in range(bands - 1):
        share_copy(n).wait_recv()
    total = jnp.sum(shares[...], axis=0)
    quarters = [jnp.sum(jnp.where(part == n, total, 0.0), axis=1, keepdims=True) for n in range(4)]
    gram = {}
    for n, pair in enumerate(PAIRS):
        line = [quarters[2 * k + n // 8][n % 8 : n % 8 + 1] for k in range(2)]
        gram[pair] = jnp.where(lane[:1] < LANES // 2, line[0], line[1])
    found = coefficients(gram)
    for k in range(2):
        weights = [value[:, k * LANES // 2 : k * LANES // 2 + 1] for value in found]
        for g in range(tiles):
            at = slice(EDGE, EDGE + rows)
            value = weights[0] * basis[k, 0, g, at]
            for step in range(1, ITERS):
                value = value + weights[step] * basis[k, step, g, at]
            out_ref[k, :, g * LANES : (g + 1) * LANES] = value

    for n in range(bands - 1):
        share_copy(n).wait_send()

    @pl.when(has_above)
    def _():
        edge_copy(True).wait_send()
        flow_copy(True).wait_send()

    @pl.when(has_below)
    def _():
        edge_copy(False).wait_send()
        flow_copy(False).wait_send()

    def drain(c, _):
        sent(c).wait_send()
        return 0

    @pl.when(has_prev)
    def _():
        lax.fori_loop(0, chunks, drain, 0)


def per_device(sections, bands, image, tissue_mask, anchor, fixed_nodes, prior_shift):
    _, size, columns = image.shape
    _, rows, nodes = anchor.shape
    chunks = columns // PAIR
    tiles = nodes // LANES
    wide = 2 * EDGE + rows
    width = 3 * nodes // 4
    both, narrow = tables()
    out = pl.pallas_call(
        functools.partial(kernel, sections, bands),
        out_shape=jax.ShapeDtypeStruct((2, rows, nodes), jnp.float32),
        in_specs=[pl.BlockSpec(memory_space=pl.ANY)] * 7,
        out_specs=pl.BlockSpec(memory_space=pltpu.VMEM),
        scratch_shapes=[
            pltpu.VMEM((chunks, size, PAIR), jnp.bfloat16),
            pltpu.VMEM((chunks, size, PAIR), jnp.int32),
            pltpu.VMEM((chunks, size, PAIR), jnp.bfloat16),
            pltpu.VMEM((chunks, size, PAIR), jnp.bfloat16),
            pltpu.VMEM((chunks, PAIR, PAIR), jnp.bfloat16),
            pltpu.VMEM((PAIR, PAIR), jnp.bfloat16),
            pltpu.VMEM((PAIR, SIZE), jnp.bfloat16),
            pltpu.VMEM((rows, nodes), jnp.float32),
            pltpu.VMEM((rows, nodes), jnp.int32),
            pltpu.VMEM((2, rows, nodes), jnp.float32),
            pltpu.VMEM((2, 4 * SPAN, width), jnp.bfloat16),
            pltpu.VMEM((2, 4 * SPAN, width), jnp.bfloat16),
            pltpu.VMEM((tiles, wide, LANES), jnp.float32),
            pltpu.VMEM((tiles, wide, LANES), jnp.float32),
            pltpu.VMEM((tiles, wide, LANES), jnp.float32),
            pltpu.VMEM((2, tiles, wide, LANES), jnp.float32),
            pltpu.VMEM((2, tiles, LANES), jnp.float32),
            pltpu.VMEM((2, 2, tiles, LANES), jnp.float32),
            pltpu.VMEM((2, ITERS + 1, tiles, wide, LANES), jnp.float32),
            pltpu.VMEM((8, LANES), jnp.float32),
            pltpu.VMEM((bands, 8, LANES), jnp.float32),
            pltpu.SemaphoreType.DMA((2, chunks)),
            pltpu.SemaphoreType.DMA((5,)),
            pltpu.SemaphoreType.DMA((chunks,)),
            pltpu.SemaphoreType.DMA((chunks,)),
            pltpu.SemaphoreType.DMA((2,)),
            pltpu.SemaphoreType.DMA((2,)),
            pltpu.SemaphoreType.DMA((2,)),
            pltpu.SemaphoreType.DMA((2,)),
            pltpu.SemaphoreType.DMA((bands - 1,)),
            pltpu.SemaphoreType.DMA((bands - 1,)),
            pltpu.SemaphoreType.REGULAR((2,)),
        ],
        compiler_params=pltpu.CompilerParams(
            collective_id=0, has_side_effects=True, vmem_limit_bytes=60 * 1024 * 1024
        ),
        cost_estimate=pl.CostEstimate(flops=2_400_000_000, bytes_accessed=4_000_000, transcendentals=0),
    )(image, tissue_mask, anchor, fixed_nodes, prior_shift, jnp.asarray(both), jnp.asarray(narrow))
    return out[:, None]


def solution(mesh):
    sections, bands = mesh.shape["sec"], mesh.shape["blk"]
    return jax.shard_map(
        functools.partial(per_device, sections, bands),
        mesh=mesh,
        in_specs=(
            P("sec", "blk", None),
            P("sec", "blk", None),
            P("sec", "blk", None),
            P("sec", "blk", None),
            P(None, "sec", "blk", None),
        ),
        out_specs=P(None, "sec", "blk", None),
        check_vma=False,
    )
```

```python
import functools
import math

import jax
import jax.numpy as jnp
import ml_dtypes
import numpy as np
from jax import lax
from jax.experimental import pallas as pl
from jax.experimental.pallas import tpu as pltpu
from jax.sharding import PartitionSpec as P

MESH = pl.DeviceIdType.MESH
ITERS = 4
SIZE = 128
PAIR = 2 * SIZE
LANES = 128
EDGE = 8
SPAN = 4
SHIFTS = (1.0, 4.0, 1.0, 4.0)
SCALE = 0.25
PAIRS = tuple((i, j) for i in range(ITERS) for j in range(i, ITERS)) + tuple((i, ITERS) for i in range(ITERS))


def tables():
    j = np.arange(SIZE)
    angle = (j[:, None] * j[None, :] % SIZE).astype(np.float32) * np.float32(2.0 * math.pi / SIZE)
    cosine = np.cos(angle).astype(ml_dtypes.bfloat16)
    sine = np.sin(angle).astype(ml_dtypes.bfloat16)
    both = np.block([[cosine, -sine], [sine, cosine]])
    return both, np.concatenate([cosine, -sine], axis=0)


def matmul(left, right):
    return jnp.dot(left, right, preferred_element_type=jnp.float32)


def beside(pair):
    rows = [
        jnp.concatenate([pair[:SIZE, p * SIZE : (p + 1) * SIZE], pair[SIZE:, p * SIZE : (p + 1) * SIZE]], axis=1)
        for p in range(2)
    ]
    return jnp.concatenate(rows, axis=0)


def stacked(re, im):
    rows = [jnp.concatenate([part[:SIZE], part[SIZE:]], axis=1) for part in (re, im)]
    return jnp.concatenate(rows, axis=0)


def spectrum(block, narrow, both):
    half = matmul(narrow, block).astype(jnp.bfloat16)
    return matmul(beside(half), both).astype(jnp.bfloat16)


def offsets(shape, axis):
    index = lax.broadcasted_iota(jnp.int32, shape, axis)
    return (((index + SIZE // 2) % SIZE) - SIZE // 2).astype(jnp.float32)


def flows_of(own, other, narrow, both):
    a = own.astype(jnp.float32)
    b = other.astype(jnp.float32)
    a_re, a_im, b_re, b_im = a[:, :SIZE], a[:, SIZE:], b[:, :SIZE], b[:, SIZE:]
    cross_re = (a_re * b_re + a_im * b_im).astype(jnp.bfloat16)
    cross_im = (a_im * b_re - a_re * b_im).astype(jnp.bfloat16)
    back = matmul(both, stacked(cross_re, cross_im)).astype(jnp.bfloat16)
    corr = matmul(beside(back), narrow)
    weight = (corr * corr).reshape(2, SIZE, SIZE)
    whole = jnp.sum(weight, axis=1)
    tilted = jnp.sum(weight * offsets((1, SIZE, SIZE), 1), axis=1)
    unit = 2.0**-42
    total = jnp.sum(whole, axis=1, keepdims=True) * unit + 1e-6
    row_flow = jnp.sum(tilted, axis=1, keepdims=True) * unit / total
    col_flow = jnp.sum(whole * offsets((2, SIZE), 1), axis=1, keepdims=True) * unit / total
    return row_flow, col_flow


def neighbours(value):
    tiles, rows, _ = value.shape
    lane = lax.broadcasted_iota(jnp.int32, value.shape, 2)
    none = jnp.zeros((1, rows, LANES), value.dtype)
    right = pltpu.roll(value, 1, 2)
    right = jnp.where(lane == 0, jnp.concatenate([none, right[:-1]], axis=0), right)
    left = pltpu.roll(value, LANES - 1, 2)
    left = jnp.where(lane == LANES - 1, jnp.concatenate([left[1:], none], axis=0), left)
    return pltpu.roll(value, 1, 1) + pltpu.roll(value, rows - 1, 1) + right + left


def coefficients(gram):
    def inner(left, right):
        terms = [l * r * gram[min(i, j), max(i, j)] for i, l in enumerate(left) for j, r in enumerate(right)]
        return functools.reduce(lambda p, q: p + q, terms)

    zero = jnp.zeros_like(gram[0, 0])
    solution = [zero] * ITERS
    residual = [jnp.ones_like(zero)]
    direction = list(residual)
    norm_now = gram[0, 0]
    for step in range(ITERS):
        image = [SHIFTS[j] * direction[j] for j in range(step + 1)] + [zero]
        image = [image[j] + (direction[j - 1] / SCALE if j else 0.0) for j in range(step + 2)]
        curve = inner(direction, image)
        alpha = jnp.where(curve > 0.0, jnp.clip(norm_now / curve, 0.0, 10.1), 0.0)
        solution = [solution[j] + alpha * direction[j] if j <= step else solution[j] for j in range(ITERS)]
        if step == ITERS - 1:
            break
        residual = [r - alpha * i for r, i in zip(residual + [zero], image)]
        norm_next = jnp.maximum(inner(residual, residual), 0.0)
        beta = jnp.where(norm_now > 0.0, norm_next / norm_now, 0.0)
        direction = [r + beta * d for r, d in zip(residual, direction + [zero])]
        norm_now = norm_next
    return solution


def kernel(
    sections,
    bands,
    image_hbm,
    mask_hbm,
    anchor_hbm,
    fixed_hbm,
    prior_hbm,
    both_hbm,
    narrow_hbm,
    out_ref,
    image,
    mask,
    masked,
    arrived,
    spectra,
    both,
    narrow,
    anchor,
    fixed,
    prior,
    edge_out,
    edge_in,
    pull,
    diag,
    link,
    base,
    flow,
    flow_in,
    basis,
    share,
    shares,
    load_sem,
    mesh_sem,
    send_sem,
    recv_sem,
    edge_send,
    edge_recv,
    flow_send,
    flow_recv,
    share_send,
    share_recv,
    round_sem,
):
    chunks = image.shape[0]
    tiles = pull.shape[0]
    rows = anchor.shape[0]
    sec = lax.axis_index("sec")
    blk = lax.axis_index("blk")
    has_above, has_below = blk > 0, blk < bands - 1
    has_prev, has_next = sec > 0, sec < sections - 1
    turns = bands // 4
    here = (blk // 4, lax.rem(blk // 2, 2), lax.rem(blk, 2))

    def moved(dx, dy, dc):
        return lax.rem(here[0] + dx, turns) * 4 + lax.rem(here[1] + dy, 2) * 2 + lax.rem(here[2] + dc, 2)

    order = [dx if dx <= turns // 2 else dx - turns for dx in range(turns)]
    steps = sorted(
        ((dx % turns, dy, dc) for dx in order for dy in range(2) for dc in range(2)),
        key=lambda step: (-step[1], -min(step[0], turns - step[0]), -step[2]),
    )
    others = [moved(*step) for step in steps if any(step)]

    def pixels(c):
        return pl.ds(pl.multiple_of(c * PAIR, PAIR), PAIR)

    def loads(c):
        return (
            pltpu.make_async_copy(image_hbm.at[0, :, pixels(c)], image.at[c], load_sem.at[0, c]),
            pltpu.make_async_copy(mask_hbm.at[0, :, pixels(c)], mask.at[c], load_sem.at[1, c]),
        )

    def sent(c):
        return pltpu.make_async_remote_copy(
            masked.at[c], arrived.at[c], send_sem.at[c], recv_sem.at[c], device_id={"sec": sec - 1}, device_id_type=MESH
        )

    mesh_loads = [
        pltpu.make_async_copy(both_hbm, both, mesh_sem.at[0]),
        pltpu.make_async_copy(narrow_hbm, narrow, mesh_sem.at[1]),
        pltpu.make_async_copy(anchor_hbm.at[0], anchor, mesh_sem.at[2]),
        pltpu.make_async_copy(fixed_hbm.at[0], fixed, mesh_sem.at[3]),
        pltpu.make_async_copy(prior_hbm.at[:, 0], prior, mesh_sem.at[4]),
    ]

    barrier = pltpu.get_barrier_semaphore()

    def greet(device):
        pl.semaphore_signal(barrier, inc=1, device_id=device, device_id_type=MESH)

    pl.when(has_prev)(lambda: greet({"sec": sec - 1}))
    pl.when(has_next)(lambda: greet({"sec": sec + 1}))
    pl.when(has_above)(lambda: greet({"blk": blk - 1}))
    pl.when(has_below)(lambda: greet({"blk": blk + 1}))
    across, over = moved(0, 0, 1), moved(0, 1, 0)
    along = [moved(dx, 0, 0) for dx in range(1, turns)]
    for other in [across, over] + along:
        greet({"blk": other})

    def start_loads(c, _):
        for copy in loads(c):
            copy.start()
        return 0

    lax.fori_loop(0, 1, start_loads, 0)
    for copy in mesh_loads:
        copy.start()
    lax.fori_loop(1, chunks, start_loads, 0)

    def hide(c):
        for copy in loads(c):
            copy.wait()
        masked[c] = image[c] * mask[c].astype(jnp.float32).astype(jnp.bfloat16)

    def hide_and_send(c, _):
        hide(c)
        pl.when(has_prev)(lambda: sent(c).start())
        return 0

    hide(0)
    for copy in mesh_loads:
        copy.wait()
    free = 1.0 - fixed[...].astype(jnp.float32)
    own_pull = free * anchor[...]
    own = [own_pull, own_pull * prior[0], own_pull * prior[1]]

    def edge_copy(up):
        slot = 0 if up else 1
        return pltpu.make_async_remote_copy(
            edge_out.at[slot],
            edge_in.at[slot],
            edge_send.at[slot],
            edge_recv.at[slot],
            device_id={"blk": blk - 1 if up else blk + 1},
            device_id_type=MESH,
        )

    def flow_copy(up):
        slot = 0 if up else 1
        return pltpu.make_async_remote_copy(
            flow,
            flow_in.at[slot],
            flow_send.at[slot],
            flow_recv.at[slot],
            device_id={"blk": blk - 1 if up else blk + 1},
            device_id_type=MESH,
        )

    width = 3 * tiles * LANES // 4

    def packed(first):
        flat = jnp.concatenate([part[first : first + SPAN] for part in own], axis=1)
        return jnp.concatenate([flat[:, k * width : (k + 1) * width] for k in range(4)], axis=0).astype(jnp.bfloat16)

    def unpacked(block):
        block = block.astype(jnp.float32)
        flat = jnp.concatenate([block[k * SPAN : (k + 1) * SPAN] for k in range(4)], axis=1)
        return [flat[:, k * tiles * LANES : (k + 1) * tiles * LANES] for k in range(3)]

    edge_out[0] = packed(0)
    edge_out[1] = packed(rows - SPAN)
    greeted = has_prev, has_next, has_above, has_below
    pl.semaphore_wait(barrier, turns + 1 + functools.reduce(lambda p, q: p + q, [g.astype(jnp.int32) for g in greeted]))
    pl.when(has_above)(lambda: edge_copy(True).start())
    pl.when(has_below)(lambda: edge_copy(False).start())
    pl.when(has_prev)(lambda: sent(0).start())
    pl.semaphore_signal(round_sem.at[0], inc=1, device_id={"blk": across}, device_id_type=MESH)
    lax.fori_loop(1, 8, hide_and_send, 0)
    pl.semaphore_wait(round_sem.at[0], 1)
    pl.semaphore_signal(round_sem.at[1], inc=1, device_id={"blk": over}, device_id_type=MESH)
    lax.fori_loop(8, chunks, hide_and_send, 0)

    def own_spectrum(c, _):
        spectra[c] = spectrum(masked[c], narrow[...], both[...])
        return 0

    lax.fori_loop(0, chunks, own_spectrum, 0)
    pl.semaphore_wait(round_sem.at[1], 1)

    pull[...] = jnp.zeros_like(pull)
    base[...] = jnp.zeros_like(base)
    for g in range(tiles):
        at = slice(g * LANES, (g + 1) * LANES)
        pull[g, EDGE : EDGE + rows] = own[0][:, at]
        base[0, g, EDGE : EDGE + rows] = own[1][:, at]
        base[1, g, EDGE : EDGE + rows] = own[2][:, at]

    def take_edge(slot, first):
        parts = unpacked(edge_in[slot])
        for g in range(tiles):
            at = slice(g * LANES, (g + 1) * LANES)
            pull[g, first : first + SPAN] = parts[0][:, at]
            base[0, g, first : first + SPAN] = parts[1][:, at]
            base[1, g, first : first + SPAN] = parts[2][:, at]

    flow[...] = jnp.zeros_like(flow)
    tile_row = lax.broadcasted_iota(jnp.int32, (tiles, LANES), 0)
    quarter = lax.broadcasted_iota(jnp.int32, (tiles, LANES), 1) // (LANES // 4)

    def correlate(c, _):
        sent(c).wait_recv()
        other = spectrum(arrived[c], narrow[...], both[...])
        for k, value in enumerate(flows_of(spectra[c], other, narrow[...], both[...])):
            held = flow[k]
            for p in range(2):
                spot = (tile_row == c // 2) & (quarter == 2 * (c % 2) + p)
                held = jnp.where(spot, value[p : p + 1], held)
            flow[k] = held
        return 0

    late = chunks * 3 // 4

    @pl.when(has_next)
    def _():
        lax.fori_loop(0, late, correlate, 0)

    @pl.when(has_below)
    def _():
        edge_copy(True).wait_recv()
        take_edge(0, EDGE + rows)

    @pl.when(has_above)
    def _():
        edge_copy(False).wait_recv()
        take_edge(1, EDGE - SPAN)

    loose = jnp.where(pull[...] > 0.0, SCALE, 0.0)
    link[...] = loose
    diag[...] = 4.0 * loose + SCALE * pull[...]

    @pl.when(has_next)
    def _():
        lax.fori_loop(late, chunks, correlate, 0)

    pl.when(has_above)(lambda: flow_copy(True).start())
    pl.when(has_below)(lambda: flow_copy(False).start())

    @pl.when(has_below)
    def _():
        flow_copy(True).wait_recv()

    @pl.when(has_above)
    def _():
        flow_copy(False).wait_recv()

    @pl.when(jnp.logical_not(has_below))
    def _():
        flow_in[0] = jnp.zeros_like(flow)

    @pl.when(jnp.logical_not(has_above))
    def _():
        flow_in[1] = jnp.zeros_like(flow)

    for k in range(2):
        for g in range(tiles):
            for source, first, count in (
                (flow_in.at[1], 0, EDGE),
                (flow, EDGE, rows),
                (flow_in.at[0], EDGE + rows, EDGE),
            ):
                at = slice(first, first + count)
                basis[k, 0, g, at] = base[k, g, at] + pull[g, at] * source[k, g : g + 1, :]

    lane = lax.broadcasted_iota(jnp.int32, (8, LANES), 1)
    sums = []
    for k in range(2):
        for step in range(ITERS):
            value = basis[k, step]
            basis[k, step + 1] = (diag[...] - SCALE * SHIFTS[step]) * value - link[...] * neighbours(value)
        lines = []
        for i, j in PAIRS:
            product = basis[k, i, :, EDGE : EDGE + rows] * basis[k, j, :, EDGE : EDGE + rows]
            total = jnp.sum(product.reshape(tiles * rows // 8, 8, LANES), axis=0)
            lines.append(jnp.sum(total, axis=0, keepdims=True))
        lines += [jnp.zeros((1, LANES), jnp.float32)] * (16 - len(lines))
        for half in range(2):
            block = jnp.concatenate(lines[8 * half : 8 * half + 8], axis=0)
            block = block + pltpu.roll(block, LANES // 2, 1)
            sums.append(block + pltpu.roll(block, LANES // 4, 1))
    part = lane // (LANES // 4)
    mine = sums[3]
    for n in range(3):
        mine = jnp.where(part == n, sums[n], mine)
    share[...] = mine

    def share_copy(n):
        return pltpu.make_async_remote_copy(
            share,
            shares.at[blk],
            share_send.at[n],
            share_recv.at[n],
            device_id={"blk": others[n]},
            device_id_type=MESH,
        )

    for n in range(bands - 1):
        share_copy(n).start()
    shares[blk] = share[...]
    for n in range(bands - 1):
        share_copy(n).wait_recv()
    total = jnp.sum(shares[...], axis=0)
    quarters = [jnp.sum(jnp.where(part == n, total, 0.0), axis=1, keepdims=True) for n in range(4)]
    gram = {}
    for n, pair in enumerate(PAIRS):
        line = [quarters[2 * k + n // 8][n % 8 : n % 8 + 1] for k in range(2)]
        gram[pair] = jnp.where(lane[:1] < LANES // 2, line[0], line[1])
    found = coefficients(gram)
    for k in range(2):
        weights = [value[:, k * LANES // 2 : k * LANES // 2 + 1] for value in found]
        for g in range(tiles):
            at = slice(EDGE, EDGE + rows)
            value = weights[0] * basis[k, 0, g, at]
            for step in range(1, ITERS):
                value = value + weights[step] * basis[k, step, g, at]
            out_ref[k, :, g * LANES : (g + 1) * LANES] = value

    for n in range(bands - 1):
        share_copy(n).wait_send()

    @pl.when(has_above)
    def _():
        edge_copy(True).wait_send()
        flow_copy(True).wait_send()

    @pl.when(has_below)
    def _():
        edge_copy(False).wait_send()
        flow_copy(False).wait_send()

    def drain(c, _):
        sent(c).wait_send()
        return 0

    @pl.when(has_prev)
    def _():
        lax.fori_loop(0, chunks, drain, 0)


def per_device(sections, bands, image, tissue_mask, anchor, fixed_nodes, prior_shift):
    _, size, columns = image.shape
    _, rows, nodes = anchor.shape
    chunks = columns // PAIR
    tiles = nodes // LANES
    wide = 2 * EDGE + rows
    width = 3 * nodes // 4
    both, narrow = tables()
    operands = image, tissue_mask, anchor, fixed_nodes, prior_shift, jnp.asarray(both), jnp.asarray(narrow)
    operands = [pltpu.with_memory_space_constraint(operand, pltpu.HBM) for operand in operands]
    out = pl.pallas_call(
        functools.partial(kernel, sections, bands),
        out_shape=jax.ShapeDtypeStruct((2, rows, nodes), jnp.float32),
        in_specs=[pl.BlockSpec(memory_space=pl.ANY)] * 7,
        out_specs=pl.BlockSpec(memory_space=pltpu.VMEM),
        scratch_shapes=[
            pltpu.VMEM((chunks, size, PAIR), jnp.bfloat16),
            pltpu.VMEM((chunks, size, PAIR), jnp.int32),
            pltpu.VMEM((chunks, size, PAIR), jnp.bfloat16),
            pltpu.VMEM((chunks, size, PAIR), jnp.bfloat16),
            pltpu.VMEM((chunks, PAIR, PAIR), jnp.bfloat16),
            pltpu.VMEM((PAIR, PAIR), jnp.bfloat16),
            pltpu.VMEM((PAIR, SIZE), jnp.bfloat16),
            pltpu.VMEM((rows, nodes), jnp.float32),
            pltpu.VMEM((rows, nodes), jnp.int32),
            pltpu.VMEM((2, rows, nodes), jnp.float32),
            pltpu.VMEM((2, 4 * SPAN, width), jnp.bfloat16),
            pltpu.VMEM((2, 4 * SPAN, width), jnp.bfloat16),
            pltpu.VMEM((tiles, wide, LANES), jnp.float32),
            pltpu.VMEM((tiles, wide, LANES), jnp.float32),
            pltpu.VMEM((tiles, wide, LANES), jnp.float32),
            pltpu.VMEM((2, tiles, wide, LANES), jnp.float32),
            pltpu.VMEM((2, tiles, LANES), jnp.float32),
            pltpu.VMEM((2, 2, tiles, LANES), jnp.float32),
            pltpu.VMEM((2, ITERS + 1, tiles, wide, LANES), jnp.float32),
            pltpu.VMEM((8, LANES), jnp.float32),
            pltpu.VMEM((bands, 8, LANES), jnp.float32),
            pltpu.SemaphoreType.DMA((2, chunks)),
            pltpu.SemaphoreType.DMA((5,)),
            pltpu.SemaphoreType.DMA((chunks,)),
            pltpu.SemaphoreType.DMA((chunks,)),
            pltpu.SemaphoreType.DMA((2,)),
            pltpu.SemaphoreType.DMA((2,)),
            pltpu.SemaphoreType.DMA((2,)),
            pltpu.SemaphoreType.DMA((2,)),
            pltpu.SemaphoreType.DMA((bands - 1,)),
            pltpu.SemaphoreType.DMA((bands - 1,)),
            pltpu.SemaphoreType.REGULAR((2,)),
        ],
        compiler_params=pltpu.CompilerParams(
            collective_id=0, has_side_effects=True, vmem_limit_bytes=40 * 1024 * 1024
        ),
        cost_estimate=pl.CostEstimate(flops=2_400_000_000, bytes_accessed=4_000_000, transcendentals=0),
    )(*operands)
    return out[:, None]


def solution(mesh):
    sections, bands = mesh.shape["sec"], mesh.shape["blk"]
    return jax.shard_map(
        functools.partial(per_device, sections, bands),
        mesh=mesh,
        in_specs=(
            P("sec", "blk", None),
            P("sec", "blk", None),
            P("sec", "blk", None),
            P("sec", "blk", None),
            P(None, "sec", "blk", None),
        ),
        out_specs=P(None, "sec", "blk", None),
        check_vma=False,
    )
```

```python
import functools
import math

import jax
import jax.numpy as jnp
import ml_dtypes
import numpy as np
from jax import lax
from jax.experimental import pallas as pl
from jax.experimental.pallas import tpu as pltpu
from jax.sharding import PartitionSpec as P

MESH = pl.DeviceIdType.MESH
ITERS = 4
SIZE = 128
PAIR = 2 * SIZE
LANES = 128
EDGE = 8
SPAN = 4
REACH = 2 * ITERS - 1
SHIFTS = (1.0, 4.0, 1.0, 4.0, 1.0, 4.0, 1.0)
SCALE = 0.25
PAIRS = tuple((i, j) for i in range(ITERS) for j in range(i, ITERS)) + tuple((i, ITERS) for i in range(ITERS))


def tables():
    j = np.arange(SIZE)
    angle = (j[:, None] * j[None, :] % SIZE).astype(np.float32) * np.float32(2.0 * math.pi / SIZE)
    cosine = np.cos(angle).astype(ml_dtypes.bfloat16)
    sine = np.sin(angle).astype(ml_dtypes.bfloat16)
    both = np.block([[cosine, -sine], [sine, cosine]])
    return both, np.concatenate([cosine, -sine], axis=0)


def matmul(left, right):
    return jnp.dot(left, right, preferred_element_type=jnp.float32)


def beside(pair):
    rows = [
        jnp.concatenate([pair[:SIZE, p * SIZE : (p + 1) * SIZE], pair[SIZE:, p * SIZE : (p + 1) * SIZE]], axis=1)
        for p in range(2)
    ]
    return jnp.concatenate(rows, axis=0)


def stacked(re, im):
    rows = [jnp.concatenate([part[:SIZE], part[SIZE:]], axis=1) for part in (re, im)]
    return jnp.concatenate(rows, axis=0)


def spectrum(block, narrow, both):
    half = matmul(narrow, block).astype(jnp.bfloat16)
    return matmul(beside(half), both).astype(jnp.bfloat16)


def offsets(shape, axis):
    index = lax.broadcasted_iota(jnp.int32, shape, axis)
    return (((index + SIZE // 2) % SIZE) - SIZE // 2).astype(jnp.float32)


def flows_of(own, other, narrow, both):
    a = own.astype(jnp.float32)
    b = other.astype(jnp.float32)
    a_re, a_im, b_re, b_im = a[:, :SIZE], a[:, SIZE:], b[:, :SIZE], b[:, SIZE:]
    cross_re = (a_re * b_re + a_im * b_im).astype(jnp.bfloat16)
    cross_im = (a_im * b_re - a_re * b_im).astype(jnp.bfloat16)
    back = matmul(both, stacked(cross_re, cross_im)).astype(jnp.bfloat16)
    corr = matmul(beside(back), narrow)
    weight = (corr * corr).reshape(2, SIZE, SIZE)
    whole = jnp.sum(weight, axis=1)
    tilted = jnp.sum(weight * offsets((1, SIZE, SIZE), 1), axis=1)
    unit = 2.0**-42
    total = jnp.sum(whole, axis=1, keepdims=True) * unit + 1e-6
    row_flow = jnp.sum(tilted, axis=1, keepdims=True) * unit / total
    col_flow = jnp.sum(whole * offsets((2, SIZE), 1), axis=1, keepdims=True) * unit / total
    return row_flow, col_flow


def neighbours(value):
    tiles, rows, _ = value.shape
    lane = lax.broadcasted_iota(jnp.int32, value.shape, 2)
    none = jnp.zeros((1, rows, LANES), value.dtype)
    right = pltpu.roll(value, 1, 2)
    right = jnp.where(lane == 0, jnp.concatenate([none, right[:-1]], axis=0), right)
    left = pltpu.roll(value, LANES - 1, 2)
    left = jnp.where(lane == LANES - 1, jnp.concatenate([left[1:], none], axis=0), left)
    return pltpu.roll(value, 1, 1) + pltpu.roll(value, rows - 1, 1) + right + left


def coefficients(gram):
    def inner(left, right):
        terms = [l * r * gram[min(i, j), max(i, j)] for i, l in enumerate(left) for j, r in enumerate(right)]
        return functools.reduce(lambda p, q: p + q, terms)

    zero = jnp.zeros_like(gram[0, 0])
    solution = [zero] * ITERS
    residual = [jnp.ones_like(zero)]
    direction = list(residual)
    norm_now = gram[0, 0]
    for step in range(ITERS):
        image = [SHIFTS[j] * direction[j] for j in range(step + 1)] + [zero]
        image = [image[j] + (direction[j - 1] / SCALE if j else 0.0) for j in range(step + 2)]
        curve = inner(direction, image)
        alpha = jnp.where(curve > 0.0, jnp.clip(norm_now / curve, 0.0, 10.1), 0.0)
        solution = [solution[j] + alpha * direction[j] if j <= step else solution[j] for j in range(ITERS)]
        if step == ITERS - 1:
            break
        residual = [r - alpha * i for r, i in zip(residual + [zero], image)]
        norm_next = jnp.maximum(inner(residual, residual), 0.0)
        beta = jnp.where(norm_now > 0.0, norm_next / norm_now, 0.0)
        direction = [r + beta * d for r, d in zip(residual, direction + [zero])]
        norm_now = norm_next
    return solution


def kernel(
    sections,
    bands,
    image_hbm,
    mask_hbm,
    anchor_hbm,
    fixed_hbm,
    prior_hbm,
    both_hbm,
    narrow_hbm,
    out_ref,
    image,
    mask,
    masked,
    arrived,
    spectra,
    both,
    narrow,
    anchor,
    fixed,
    prior,
    edge_up,
    edge_down,
    from_below,
    from_above,
    pull,
    diag,
    link,
    base,
    flow,
    flow_in,
    listed,
    pick,
    basis,
    whole,
    share,
    shares,
    load_sem,
    mesh_sem,
    send_sem,
    recv_sem,
    edge_send,
    edge_recv,
    flow_send,
    flow_recv,
    share_send,
    share_recv,
    round_sem,
):
    chunks = image.shape[0]
    tiles = pull.shape[0]
    rows = anchor.shape[0]
    sec = lax.axis_index("sec")
    blk = lax.axis_index("blk")
    has_above, has_below = blk > 0, blk < bands - 1
    has_prev, has_next = sec > 0, sec < sections - 1
    turns = bands // 4
    here = (blk // 4, lax.rem(blk // 2, 2), lax.rem(blk, 2))

    def moved(dx, dy, dc):
        return lax.rem(here[0] + dx, turns) * 4 + lax.rem(here[1] + dy, 2) * 2 + lax.rem(here[2] + dc, 2)

    order = [dx if dx <= turns // 2 else dx - turns for dx in range(turns)]
    steps = sorted(
        ((dx % turns, dy, dc) for dx in order for dy in range(2) for dc in range(2)),
        key=lambda step: (-step[1], -min(step[0], turns - step[0]), -step[2]),
    )
    others = [moved(*step) for step in steps if any(step)]

    def pixels(c):
        return pl.ds(pl.multiple_of(c * PAIR, PAIR), PAIR)

    def loads(c):
        return (
            pltpu.make_async_copy(image_hbm.at[0, :, pixels(c)], image.at[c], load_sem.at[0, c]),
            pltpu.make_async_copy(mask_hbm.at[0, :, pixels(c)], mask.at[c], load_sem.at[1, c]),
        )

    def sent(c):
        return pltpu.make_async_remote_copy(
            masked.at[c], arrived.at[c], send_sem.at[c], recv_sem.at[c], device_id={"sec": sec - 1}, device_id_type=MESH
        )

    mesh_loads = [
        pltpu.make_async_copy(both_hbm, both, mesh_sem.at[0]),
        pltpu.make_async_copy(narrow_hbm, narrow, mesh_sem.at[1]),
        pltpu.make_async_copy(anchor_hbm.at[0], anchor, mesh_sem.at[2]),
        pltpu.make_async_copy(fixed_hbm.at[0], fixed, mesh_sem.at[3]),
        pltpu.make_async_copy(prior_hbm.at[:, 0], prior, mesh_sem.at[4]),
    ]

    barrier = pltpu.get_barrier_semaphore()

    def greet(device):
        pl.semaphore_signal(barrier, inc=1, device_id=device, device_id_type=MESH)

    pl.when(has_prev)(lambda: greet({"sec": sec - 1}))
    pl.when(has_next)(lambda: greet({"sec": sec + 1}))
    pl.when(has_above)(lambda: greet({"blk": blk - 1}))
    pl.when(has_below)(lambda: greet({"blk": blk + 1}))
    across, over = moved(0, 0, 1), moved(0, 1, 0)
    along = [moved(dx, 0, 0) for dx in range(1, turns)]
    for other in [across, over] + along:
        greet({"blk": other})

    def start_loads(c, _):
        for copy in loads(c):
            copy.start()
        return 0

    lax.fori_loop(0, 1, start_loads, 0)
    for copy in mesh_loads:
        copy.start()
    lax.fori_loop(1, chunks, start_loads, 0)

    def hide(c):
        for copy in loads(c):
            copy.wait()
        masked[c] = image[c] * mask[c].astype(jnp.float32).astype(jnp.bfloat16)

    def hide_and_send(c, _):
        hide(c)
        pl.when(has_prev)(lambda: sent(c).start())
        return 0

    hide(0)
    for copy in mesh_loads:
        copy.wait()
    free = 1.0 - fixed[...].astype(jnp.float32)
    own_pull = free * anchor[...]
    own = [own_pull, own_pull * prior[0], own_pull * prior[1]]

    def edge_copy(up):
        slot = 0 if up else 1
        return pltpu.make_async_remote_copy(
            edge_up if up else edge_down,
            from_below if up else from_above,
            edge_send.at[slot],
            edge_recv.at[slot],
            device_id={"blk": blk - 1 if up else blk + 1},
            device_id_type=MESH,
        )

    def flow_copy(up):
        slot = 0 if up else 1
        return pltpu.make_async_remote_copy(
            flow,
            flow_in.at[slot],
            flow_send.at[slot],
            flow_recv.at[slot],
            device_id={"blk": blk - 1 if up else blk + 1},
            device_id_type=MESH,
        )

    nodes = tiles * LANES

    def packed(first, count):
        flat = [part[at : at + SPAN] for part in own for at in range(first, first + count, SPAN)]
        flat = jnp.concatenate(flat, axis=1)
        width = flat.shape[1] // 4
        return jnp.concatenate([flat[:, k * width : (k + 1) * width] for k in range(4)], axis=0).astype(jnp.bfloat16)

    def unpacked(block):
        block = block.astype(jnp.float32)
        flat = jnp.concatenate([block[k * SPAN : (k + 1) * SPAN] for k in range(4)], axis=1)
        parts = [flat[:, k : k + nodes] for k in range(0, flat.shape[1], nodes)]
        each = len(parts) // 3
        return [parts[k * each : (k + 1) * each] for k in range(3)]

    edge_up[...] = packed(0, EDGE)
    edge_down[...] = packed(rows - SPAN, SPAN)
    greeted = has_prev, has_next, has_above, has_below
    pl.semaphore_wait(barrier, turns + 1 + functools.reduce(lambda p, q: p + q, [g.astype(jnp.int32) for g in greeted]))
    pl.when(has_above)(lambda: edge_copy(True).start())
    pl.when(has_below)(lambda: edge_copy(False).start())
    pl.when(has_prev)(lambda: sent(0).start())
    pl.semaphore_signal(round_sem.at[0], inc=1, device_id={"blk": across}, device_id_type=MESH)
    lax.fori_loop(1, 8, hide_and_send, 0)
    pl.semaphore_wait(round_sem.at[0], 1)
    pl.semaphore_signal(round_sem.at[1], inc=1, device_id={"blk": over}, device_id_type=MESH)
    lax.fori_loop(8, chunks, hide_and_send, 0)

    def own_spectrum(c, _):
        spectra[c] = spectrum(masked[c], narrow[...], both[...])
        return 0

    lax.fori_loop(0, chunks, own_spectrum, 0)
    pl.semaphore_wait(round_sem.at[1], 1)

    pull[...] = jnp.zeros_like(pull)
    base[...] = jnp.zeros_like(base)
    for g in range(tiles):
        at = slice(g * LANES, (g + 1) * LANES)
        pull[g, EDGE : EDGE + rows] = own[0][:, at]
        base[0, g, EDGE : EDGE + rows] = own[1][:, at]
        base[1, g, EDGE : EDGE + rows] = own[2][:, at]

    def take_edge(block, first, count):
        parts = unpacked(block)
        for n in range(0, count, SPAN):
            some = min(SPAN, count - n)
            to = slice(first + n, first + n + some)
            for g in range(tiles):
                at = slice(g * LANES, (g + 1) * LANES)
                pull[g, to] = parts[0][n // SPAN][:some, at]
                base[0, g, to] = parts[1][n // SPAN][:some, at]
                base[1, g, to] = parts[2][n // SPAN][:some, at]

    flow[...] = jnp.zeros_like(flow)
    listed[...] = jnp.zeros_like(listed)
    lane = lax.broadcasted_iota(jnp.int32, (8, LANES), 1)
    patch = lax.broadcasted_iota(jnp.int32, (nodes, LANES), 0) // (LANES // 4)
    for k in range(2):
        column = lax.broadcasted_iota(jnp.int32, (nodes, LANES), 1)
        pick[k] = jnp.where(column == patch + k * (LANES // 4), 1.0, 0.0).astype(jnp.bfloat16)
    tile_row = lax.broadcasted_iota(jnp.int32, (tiles, LANES), 0)
    quarter = lax.broadcasted_iota(jnp.int32, (tiles, LANES), 1) // (LANES // 4)

    def correlate(c, _):
        sent(c).wait_recv()
        other = spectrum(arrived[c], narrow[...], both[...])
        for k, value in enumerate(flows_of(spectra[c], other, narrow[...], both[...])):
            held = flow[k]
            for p in range(2):
                slot = lane == k * (LANES // 4) + 2 * c + p
                listed[...] = jnp.where(slot, value[p : p + 1], listed[...])
                spot = (tile_row == c // 2) & (quarter == 2 * (c % 2) + p)
                held = jnp.where(spot, value[p : p + 1], held)
            flow[k] = held
        return 0

    late = chunks * 3 // 4

    @pl.when(has_next)
    def _():
        lax.fori_loop(0, late, correlate, 0)

    @pl.when(has_below)
    def _():
        edge_copy(True).wait_recv()
        take_edge(from_below[...], EDGE + rows, REACH)

    @pl.when(has_above)
    def _():
        edge_copy(False).wait_recv()
        take_edge(from_above[...], EDGE - SPAN, SPAN)

    loose = jnp.where(pull[...] > 0.0, SCALE, 0.0)
    link[...] = loose
    diag[...] = 4.0 * loose + SCALE * pull[...]

    @pl.when(has_next)
    def _():
        lax.fori_loop(late, chunks, correlate, 0)

    pl.when(has_above)(lambda: flow_copy(True).start())
    pl.when(has_below)(lambda: flow_copy(False).start())

    def advance(value, step, at=slice(None)):
        return (diag[:, at] - SCALE * SHIFTS[step]) * value - link[:, at] * neighbours(value)

    part = lane // (LANES // 4)
    sums, strips, priors = [], [], []
    below = slice(EDGE + rows, EDGE + rows + EDGE)
    tail = slice(rows, rows + 2 * EDGE)
    for k in range(2):
        for g in range(tiles):
            inner = slice(EDGE, EDGE + rows)
            basis[k, 0, g, :EDGE] = jnp.zeros((EDGE, LANES), jnp.float32)
            basis[k, 0, g, inner] = base[k, g, inner] + pull[g, inner] * flow[k, g : g + 1, :]
            basis[k, 0, g, below] = jnp.zeros((EDGE, LANES), jnp.float32)
        for step in range(ITERS):
            basis[k, step + 1] = advance(basis[k, step], step)
        lines = []
        for i, j in PAIRS:
            product = basis[k, i] * basis[k, j]
            total = jnp.sum(product.reshape(tiles * (rows + 2 * EDGE) // 8, 8, LANES), axis=0)
            lines.append(jnp.sum(total, axis=0, keepdims=True))
        lines += [jnp.zeros((1, LANES), jnp.float32)] * (16 - len(lines))
        for half in range(2):
            block = jnp.concatenate(lines[8 * half : 8 * half + 8], axis=0)
            block = block + pltpu.roll(block, LANES // 2, 1)
            sums.append(block + pltpu.roll(block, LANES // 4, 1))
        reached = [basis[k, step][:, below] for step in range(1, ITERS + 1)]
        value = basis[k, ITERS][:, tail]
        for step in range(ITERS, REACH):
            value = advance(value, step, tail)
            reached.append(value[:, EDGE:])
        strip, line = [], [jnp.zeros((1, LANES), jnp.float32)]
        for value in reached:
            weighted = pull[:, below] * value
            strip.append(jnp.concatenate([weighted[g] for g in range(tiles)], axis=1))
            line.append(jnp.sum(jnp.sum(base[k, :, below] * value, axis=0), axis=0, keepdims=True))
        strips.append(jnp.concatenate(strip, axis=0))
        block = jnp.concatenate(line, axis=0)
        block = block + pltpu.roll(block, LANES // 2, 1)
        priors.append(block + pltpu.roll(block, LANES // 4, 1))
    mine = sums[3]
    for n in range(3):
        mine = jnp.where(part == n, sums[n], mine)
    share[8:] = mine

    gathered = jnp.zeros((REACH * EDGE, LANES), jnp.float32)
    for k in range(2):
        left = strips[k]
        for _ in range(3):
            piece = left.astype(jnp.bfloat16)
            gathered = gathered + matmul(piece, pick[k])
            left = left - piece.astype(jnp.float32)
    gathered = jnp.sum(gathered.reshape(REACH, EDGE, LANES), axis=1)
    gathered = jnp.concatenate([jnp.zeros((1, LANES), jnp.float32), gathered], axis=0)
    crossing = 2.0 * jnp.where(part < 2, gathered, jnp.where(part == 2, priors[0], priors[1]))
    first = lax.broadcasted_iota(jnp.int32, (8, LANES), 0) == 0
    share[:8] = jnp.where(first, listed[...], crossing)

    def share_copy(n):
        return pltpu.make_async_remote_copy(
            share,
            shares.at[blk],
            share_send.at[n],
            share_recv.at[n],
            device_id={"blk": others[n]},
            device_id_type=MESH,
        )

    for n in range(bands - 1):
        share_copy(n).start()
    shares[blk] = share[...]

    @pl.when(has_below)
    def _():
        flow_copy(True).wait_recv()

    @pl.when(has_above)
    def _():
        flow_copy(False).wait_recv()

    @pl.when(jnp.logical_not(has_below))
    def _():
        flow_in[0] = jnp.zeros_like(flow)

    @pl.when(jnp.logical_not(has_above))
    def _():
        flow_in[1] = jnp.zeros_like(flow)

    for k in range(2):
        for g in range(tiles):
            for source, first_row, count in (
                (flow_in.at[1], 0, EDGE),
                (flow, EDGE, rows),
                (flow_in.at[0], EDGE + rows, EDGE),
            ):
                at = slice(first_row, first_row + count)
                whole[k, 0, g, at] = base[k, g, at] + pull[g, at] * source[k, g : g + 1, :]
        for step in range(ITERS - 1):
            whole[k, step + 1] = advance(whole[k, step], step)

    for n in range(bands - 1):
        share_copy(n).wait_recv()
    total = jnp.sum(shares[:, 8:], axis=0)
    quarters = [jnp.sum(jnp.where(part == n, total, 0.0), axis=1, keepdims=True) for n in range(4)]
    crossed = jnp.zeros((8, LANES), jnp.float32)
    for n in range(bands - 1):
        crossed = crossed + shares[n, :8] * jnp.where(lane[:1] < LANES // 2, shares[n + 1, :1], 1.0)
    halves = [jnp.sum(jnp.where(part % 2 == k, crossed, 0.0), axis=1, keepdims=True) for k in range(2)]
    halves = [jnp.where(lane[:1] < LANES // 2, halves[0][m : m + 1], halves[1][m : m + 1]) for m in range(REACH + 1)]
    gram = {}
    for n, pair in enumerate(PAIRS):
        line = [quarters[2 * k + n // 8][n % 8 : n % 8 + 1] for k in range(2)]
        gram[pair] = jnp.where(lane[:1] < LANES // 2, line[0], line[1])
        degree = sum(pair)
        if degree:
            gram[pair] = gram[pair] + halves[degree]
        if pair[0] % 2 and pair[1] % 2:
            gram[pair] = gram[pair] + SCALE * (SHIFTS[1] - SHIFTS[0]) * halves[degree - 1]
    found = coefficients(gram)
    for k in range(2):
        weights = [value[:, k * LANES // 2 : k * LANES // 2 + 1] for value in found]
        for g in range(tiles):
            at = slice(EDGE, EDGE + rows)
            value = weights[0] * whole[k, 0, g, at]
            for step in range(1, ITERS):
                value = value + weights[step] * whole[k, step, g, at]
            out_ref[k, :, g * LANES : (g + 1) * LANES] = value

    for n in range(bands - 1):
        share_copy(n).wait_send()

    @pl.when(has_above)
    def _():
        edge_copy(True).wait_send()
        flow_copy(True).wait_send()

    @pl.when(has_below)
    def _():
        edge_copy(False).wait_send()
        flow_copy(False).wait_send()

    def drain(c, _):
        sent(c).wait_send()
        return 0

    @pl.when(has_prev)
    def _():
        lax.fori_loop(0, chunks, drain, 0)


def per_device(sections, bands, image, tissue_mask, anchor, fixed_nodes, prior_shift):
    _, size, columns = image.shape
    _, rows, nodes = anchor.shape
    chunks = columns // PAIR
    tiles = nodes // LANES
    wide = 2 * EDGE + rows
    width = 3 * nodes // 4
    both, narrow = tables()
    operands = image, tissue_mask, anchor, fixed_nodes, prior_shift, jnp.asarray(both), jnp.asarray(narrow)
    operands = [pltpu.with_memory_space_constraint(operand, pltpu.HBM) for operand in operands]
    out = pl.pallas_call(
        functools.partial(kernel, sections, bands),
        out_shape=jax.ShapeDtypeStruct((2, rows, nodes), jnp.float32),
        in_specs=[pl.BlockSpec(memory_space=pl.ANY)] * 7,
        out_specs=pl.BlockSpec(memory_space=pltpu.VMEM),
        scratch_shapes=[
            pltpu.VMEM((chunks, size, PAIR), jnp.bfloat16),
            pltpu.VMEM((chunks, size, PAIR), jnp.int32),
            pltpu.VMEM((chunks, size, PAIR), jnp.bfloat16),
            pltpu.VMEM((chunks, size, PAIR), jnp.bfloat16),
            pltpu.VMEM((chunks, PAIR, PAIR), jnp.bfloat16),
            pltpu.VMEM((PAIR, PAIR), jnp.bfloat16),
            pltpu.VMEM((PAIR, SIZE), jnp.bfloat16),
            pltpu.VMEM((rows, nodes), jnp.float32),
            pltpu.VMEM((rows, nodes), jnp.int32),
            pltpu.VMEM((2, rows, nodes), jnp.float32),
            pltpu.VMEM((4 * SPAN, 2 * width), jnp.bfloat16),
            pltpu.VMEM((4 * SPAN, width), jnp.bfloat16),
            pltpu.VMEM((4 * SPAN, 2 * width), jnp.bfloat16),
            pltpu.VMEM((4 * SPAN, width), jnp.bfloat16),
            pltpu.VMEM((tiles, wide, LANES), jnp.float32),
            pltpu.VMEM((tiles, wide, LANES), jnp.float32),
            pltpu.VMEM((tiles, wide, LANES), jnp.float32),
            pltpu.VMEM((2, tiles, wide, LANES), jnp.float32),
            pltpu.VMEM((2, tiles, LANES), jnp.float32),
            pltpu.VMEM((2, 2, tiles, LANES), jnp.float32),
            pltpu.VMEM((8, LANES), jnp.float32),
            pltpu.VMEM((2, nodes, LANES), jnp.bfloat16),
            pltpu.VMEM((2, ITERS + 1, tiles, wide, LANES), jnp.float32),
            pltpu.VMEM((2, ITERS, tiles, wide, LANES), jnp.float32),
            pltpu.VMEM((16, LANES), jnp.float32),
            pltpu.VMEM((bands, 16, LANES), jnp.float32),
            pltpu.SemaphoreType.DMA((2, chunks)),
            pltpu.SemaphoreType.DMA((5,)),
            pltpu.SemaphoreType.DMA((chunks,)),
            pltpu.SemaphoreType.DMA((chunks,)),
            pltpu.SemaphoreType.DMA((2,)),
            pltpu.SemaphoreType.DMA((2,)),
            pltpu.SemaphoreType.DMA((2,)),
            pltpu.SemaphoreType.DMA((2,)),
            pltpu.SemaphoreType.DMA((bands - 1,)),
            pltpu.SemaphoreType.DMA((bands - 1,)),
            pltpu.SemaphoreType.REGULAR((2,)),
        ],
        compiler_params=pltpu.CompilerParams(
            collective_id=0, has_side_effects=True, vmem_limit_bytes=40 * 1024 * 1024
        ),
        cost_estimate=pl.CostEstimate(flops=2_400_000_000, bytes_accessed=4_000_000, transcendentals=0),
    )(*operands)
    return out[:, None]


def solution(mesh):
    sections, bands = mesh.shape["sec"], mesh.shape["blk"]
    return jax.shard_map(
        functools.partial(per_device, sections, bands),
        mesh=mesh,
        in_specs=(
            P("sec", "blk", None),
            P("sec", "blk", None),
            P("sec", "blk", None),
            P("sec", "blk", None),
            P(None, "sec", "blk", None),
        ),
        out_specs=P(None, "sec", "blk", None),
        check_vma=False,
    )
```

```python
import functools
import math

import jax
import jax.numpy as jnp
import ml_dtypes
import numpy as np
from jax import lax
from jax.experimental import pallas as pl
from jax.experimental.pallas import tpu as pltpu
from jax.sharding import PartitionSpec as P

MESH = pl.DeviceIdType.MESH
ITERS = 4
SIZE = 128
PAIR = 2 * SIZE
LANES = 128
EDGE = 8
SPAN = 4
REACH = 2 * ITERS - 1
SHIFTS = (1.0, 4.0, 1.0, 4.0, 1.0, 4.0, 1.0)
SCALE = 0.25
PAIRS = tuple((i, j) for i in range(ITERS) for j in range(i, ITERS)) + tuple((i, ITERS) for i in range(ITERS))


def tables():
    j = np.arange(SIZE)
    angle = (j[:, None] * j[None, :] % SIZE).astype(np.float32) * np.float32(2.0 * math.pi / SIZE)
    cosine = np.cos(angle).astype(ml_dtypes.bfloat16)
    sine = np.sin(angle).astype(ml_dtypes.bfloat16)
    both = np.block([[cosine, -sine], [sine, cosine]])
    return both, np.concatenate([cosine, -sine], axis=0)


def matmul(left, right):
    return jnp.dot(left, right, preferred_element_type=jnp.float32)


def beside(pair):
    rows = [
        jnp.concatenate([pair[:SIZE, p * SIZE : (p + 1) * SIZE], pair[SIZE:, p * SIZE : (p + 1) * SIZE]], axis=1)
        for p in range(2)
    ]
    return jnp.concatenate(rows, axis=0)


def stacked(re, im):
    rows = [jnp.concatenate([part[:SIZE], part[SIZE:]], axis=1) for part in (re, im)]
    return jnp.concatenate(rows, axis=0)


def spectrum(block, narrow, both):
    half = matmul(narrow, block).astype(jnp.bfloat16)
    return matmul(beside(half), both).astype(jnp.bfloat16)


def offsets(shape, axis):
    index = lax.broadcasted_iota(jnp.int32, shape, axis)
    return (((index + SIZE // 2) % SIZE) - SIZE // 2).astype(jnp.float32)


def flows_of(own, other, narrow, both):
    a = own.astype(jnp.float32)
    b = other.astype(jnp.float32)
    a_re, a_im, b_re, b_im = a[:, :SIZE], a[:, SIZE:], b[:, :SIZE], b[:, SIZE:]
    cross_re = (a_re * b_re + a_im * b_im).astype(jnp.bfloat16)
    cross_im = (a_im * b_re - a_re * b_im).astype(jnp.bfloat16)
    back = matmul(both, stacked(cross_re, cross_im)).astype(jnp.bfloat16)
    corr = matmul(beside(back), narrow)
    weight = (corr * corr).reshape(2, SIZE, SIZE)
    whole = jnp.sum(weight, axis=1)
    tilted = jnp.sum(weight * offsets((1, SIZE, SIZE), 1), axis=1)
    unit = 2.0**-42
    total = jnp.sum(whole, axis=1, keepdims=True) * unit + 1e-6
    row_flow = jnp.sum(tilted, axis=1, keepdims=True) * unit / total
    col_flow = jnp.sum(whole * offsets((2, SIZE), 1), axis=1, keepdims=True) * unit / total
    return row_flow, col_flow


def neighbours(value):
    tiles, rows, _ = value.shape
    lane = lax.broadcasted_iota(jnp.int32, value.shape, 2)
    none = jnp.zeros((1, rows, LANES), value.dtype)
    right = pltpu.roll(value, 1, 2)
    right = jnp.where(lane == 0, jnp.concatenate([none, right[:-1]], axis=0), right)
    left = pltpu.roll(value, LANES - 1, 2)
    left = jnp.where(lane == LANES - 1, jnp.concatenate([left[1:], none], axis=0), left)
    return pltpu.roll(value, 1, 1) + pltpu.roll(value, rows - 1, 1) + right + left


def coefficients(gram):
    def inner(left, right):
        terms = [l * r * gram[min(i, j), max(i, j)] for i, l in enumerate(left) for j, r in enumerate(right)]
        return functools.reduce(lambda p, q: p + q, terms)

    zero = jnp.zeros_like(gram[0, 0])
    solution = [zero] * ITERS
    residual = [jnp.ones_like(zero)]
    direction = list(residual)
    norm_now = gram[0, 0]
    for step in range(ITERS):
        image = [SHIFTS[j] * direction[j] for j in range(step + 1)] + [zero]
        image = [image[j] + (direction[j - 1] / SCALE if j else 0.0) for j in range(step + 2)]
        curve = inner(direction, image)
        alpha = jnp.where(curve > 0.0, jnp.clip(norm_now / curve, 0.0, 10.1), 0.0)
        solution = [solution[j] + alpha * direction[j] if j <= step else solution[j] for j in range(ITERS)]
        if step == ITERS - 1:
            break
        residual = [r - alpha * i for r, i in zip(residual + [zero], image)]
        norm_next = jnp.maximum(inner(residual, residual), 0.0)
        beta = jnp.where(norm_now > 0.0, norm_next / norm_now, 0.0)
        direction = [r + beta * d for r, d in zip(residual, direction + [zero])]
        norm_now = norm_next
    return solution


def kernel(
    sections,
    bands,
    image_hbm,
    mask_hbm,
    anchor_hbm,
    fixed_hbm,
    prior_hbm,
    both_hbm,
    narrow_hbm,
    out_ref,
    image,
    mask,
    masked,
    arrived,
    spectra,
    both,
    narrow,
    anchor,
    fixed,
    prior,
    edge_up,
    edge_down,
    from_below,
    from_above,
    pull,
    diag,
    link,
    base,
    flow,
    flow_in,
    listed,
    pick,
    basis,
    reach,
    whole,
    share,
    shares,
    load_sem,
    mesh_sem,
    send_sem,
    recv_sem,
    edge_send,
    edge_recv,
    flow_send,
    flow_recv,
    share_send,
    share_recv,
    round_sem,
):
    chunks = image.shape[0]
    tiles = pull.shape[0]
    rows = anchor.shape[0]
    sec = lax.axis_index("sec")
    blk = lax.axis_index("blk")
    has_above, has_below = blk > 0, blk < bands - 1
    has_prev, has_next = sec > 0, sec < sections - 1
    turns = bands // 4
    here = (blk // 4, lax.rem(blk // 2, 2), lax.rem(blk, 2))

    def moved(dx, dy, dc):
        return lax.rem(here[0] + dx, turns) * 4 + lax.rem(here[1] + dy, 2) * 2 + lax.rem(here[2] + dc, 2)

    order = [dx if dx <= turns // 2 else dx - turns for dx in range(turns)]
    steps = sorted(
        ((dx % turns, dy, dc) for dx in order for dy in range(2) for dc in range(2)),
        key=lambda step: (-step[1], -min(step[0], turns - step[0]), -step[2]),
    )
    others = [moved(*step) for step in steps if any(step)]

    def pixels(c):
        return pl.ds(pl.multiple_of(c * PAIR, PAIR), PAIR)

    def loads(c):
        return (
            pltpu.make_async_copy(image_hbm.at[0, :, pixels(c)], image.at[c], load_sem.at[0, c]),
            pltpu.make_async_copy(mask_hbm.at[0, :, pixels(c)], mask.at[c], load_sem.at[1, c]),
        )

    def sent(c):
        return pltpu.make_async_remote_copy(
            masked.at[c], arrived.at[c], send_sem.at[c], recv_sem.at[c], device_id={"sec": sec - 1}, device_id_type=MESH
        )

    mesh_loads = [
        pltpu.make_async_copy(both_hbm, both, mesh_sem.at[0]),
        pltpu.make_async_copy(narrow_hbm, narrow, mesh_sem.at[1]),
        pltpu.make_async_copy(anchor_hbm.at[0], anchor, mesh_sem.at[2]),
        pltpu.make_async_copy(fixed_hbm.at[0], fixed, mesh_sem.at[3]),
        pltpu.make_async_copy(prior_hbm.at[:, 0], prior, mesh_sem.at[4]),
    ]

    barrier = pltpu.get_barrier_semaphore()

    def greet(device):
        pl.semaphore_signal(barrier, inc=1, device_id=device, device_id_type=MESH)

    pl.when(has_prev)(lambda: greet({"sec": sec - 1}))
    pl.when(has_next)(lambda: greet({"sec": sec + 1}))
    pl.when(has_above)(lambda: greet({"blk": blk - 1}))
    pl.when(has_below)(lambda: greet({"blk": blk + 1}))
    across, over = moved(0, 0, 1), moved(0, 1, 0)
    along = [moved(dx, 0, 0) for dx in range(1, turns)]
    for other in [across, over] + along:
        greet({"blk": other})

    def start_loads(c, _):
        for copy in loads(c):
            copy.start()
        return 0

    lax.fori_loop(0, 1, start_loads, 0)
    for copy in mesh_loads:
        copy.start()
    lax.fori_loop(1, chunks, start_loads, 0)

    def hide(c):
        for copy in loads(c):
            copy.wait()
        masked[c] = image[c] * mask[c].astype(jnp.float32).astype(jnp.bfloat16)

    def hide_and_send(c, _):
        hide(c)
        pl.when(has_prev)(lambda: sent(c).start())
        return 0

    hide(0)
    for copy in mesh_loads:
        copy.wait()
    free = 1.0 - fixed[...].astype(jnp.float32)
    own_pull = free * anchor[...]
    own = [own_pull, own_pull * prior[0], own_pull * prior[1]]

    def edge_copy(up):
        slot = 0 if up else 1
        return pltpu.make_async_remote_copy(
            edge_up if up else edge_down,
            from_below if up else from_above,
            edge_send.at[slot],
            edge_recv.at[slot],
            device_id={"blk": blk - 1 if up else blk + 1},
            device_id_type=MESH,
        )

    def flow_copy(up):
        slot = 0 if up else 1
        return pltpu.make_async_remote_copy(
            flow,
            flow_in.at[slot],
            flow_send.at[slot],
            flow_recv.at[slot],
            device_id={"blk": blk - 1 if up else blk + 1},
            device_id_type=MESH,
        )

    nodes = tiles * LANES

    def packed(first, count):
        flat = [part[at : at + SPAN] for part in own for at in range(first, first + count, SPAN)]
        flat = jnp.concatenate(flat, axis=1)
        width = flat.shape[1] // 4
        return jnp.concatenate([flat[:, k * width : (k + 1) * width] for k in range(4)], axis=0).astype(jnp.bfloat16)

    def unpacked(block):
        block = block.astype(jnp.float32)
        flat = jnp.concatenate([block[k * SPAN : (k + 1) * SPAN] for k in range(4)], axis=1)
        parts = [flat[:, k : k + nodes] for k in range(0, flat.shape[1], nodes)]
        each = len(parts) // 3
        return [parts[k * each : (k + 1) * each] for k in range(3)]

    edge_up[...] = packed(0, EDGE)
    edge_down[...] = packed(rows - SPAN, SPAN)
    greeted = has_prev, has_next, has_above, has_below
    pl.semaphore_wait(barrier, turns + 1 + functools.reduce(lambda p, q: p + q, [g.astype(jnp.int32) for g in greeted]))
    pl.when(has_above)(lambda: edge_copy(True).start())
    pl.when(has_below)(lambda: edge_copy(False).start())
    pl.when(has_prev)(lambda: sent(0).start())
    pl.semaphore_signal(round_sem.at[0], inc=1, device_id={"blk": across}, device_id_type=MESH)
    lax.fori_loop(1, 8, hide_and_send, 0)
    pl.semaphore_wait(round_sem.at[0], 1)
    pl.semaphore_signal(round_sem.at[1], inc=1, device_id={"blk": over}, device_id_type=MESH)
    lax.fori_loop(8, chunks, hide_and_send, 0)

    def own_spectrum(c, _):
        spectra[c] = spectrum(masked[c], narrow[...], both[...])
        return 0

    lax.fori_loop(0, chunks, own_spectrum, 0)
    pl.semaphore_wait(round_sem.at[1], 1)

    pull[...] = jnp.zeros_like(pull)
    base[...] = jnp.zeros_like(base)
    for g in range(tiles):
        at = slice(g * LANES, (g + 1) * LANES)
        pull[g, EDGE : EDGE + rows] = own[0][:, at]
        base[0, g, EDGE : EDGE + rows] = own[1][:, at]
        base[1, g, EDGE : EDGE + rows] = own[2][:, at]

    def take_edge(block, first, count):
        parts = unpacked(block)
        for n in range(0, count, SPAN):
            some = min(SPAN, count - n)
            to = slice(first + n, first + n + some)
            for g in range(tiles):
                at = slice(g * LANES, (g + 1) * LANES)
                pull[g, to] = parts[0][n // SPAN][:some, at]
                base[0, g, to] = parts[1][n // SPAN][:some, at]
                base[1, g, to] = parts[2][n // SPAN][:some, at]

    flow[...] = jnp.zeros_like(flow)
    listed[...] = jnp.zeros_like(listed)
    lane = lax.broadcasted_iota(jnp.int32, (8, LANES), 1)
    patch = lax.broadcasted_iota(jnp.int32, (nodes, LANES), 0) // (LANES // 4)
    for k in range(2):
        column = lax.broadcasted_iota(jnp.int32, (nodes, LANES), 1)
        pick[k] = jnp.where(column == patch + k * (LANES // 4), 1.0, 0.0).astype(jnp.bfloat16)
    tile_row = lax.broadcasted_iota(jnp.int32, (tiles, LANES), 0)
    quarter = lax.broadcasted_iota(jnp.int32, (tiles, LANES), 1) // (LANES // 4)

    def correlate(c, _):
        sent(c).wait_recv()
        other = spectrum(arrived[c], narrow[...], both[...])
        for k, value in enumerate(flows_of(spectra[c], other, narrow[...], both[...])):
            held = flow[k]
            for p in range(2):
                slot = lane == k * (LANES // 4) + 2 * c + p
                listed[...] = jnp.where(slot, value[p : p + 1], listed[...])
                spot = (tile_row == c // 2) & (quarter == 2 * (c % 2) + p)
                held = jnp.where(spot, value[p : p + 1], held)
            flow[k] = held
        return 0

    pause = chunks - 4
    known = pause * PAIR // SIZE // 4

    @pl.when(has_next)
    def _():
        lax.fori_loop(0, pause, correlate, 0)

    @pl.when(has_below)
    def _():
        edge_copy(True).wait_recv()
        take_edge(from_below[...], EDGE + rows, REACH)

    @pl.when(has_above)
    def _():
        edge_copy(False).wait_recv()
        take_edge(from_above[...], EDGE - SPAN, SPAN)

    loose = jnp.where(pull[...] > 0.0, SCALE, 0.0)
    link[...] = loose
    diag[...] = 4.0 * loose + SCALE * pull[...]

    part = lane // (LANES // 4)
    below = slice(EDGE + rows, EDGE + rows + EDGE)
    tail = slice(rows, rows + 2 * EDGE)

    def advance(value, step, tile=slice(None), at=slice(None), kept=0):
        return (diag[tile, at] - SCALE * SHIFTS[step]) * value[kept:] - link[tile, at] * neighbours(value)[kept:]

    def own_basis(first, last, kept):
        new, read = slice(first + kept, last), slice(first, last)
        for k in range(2):
            for g in range(first + kept, last):
                inner = slice(EDGE, EDGE + rows)
                basis[k, 0, g, :EDGE] = jnp.zeros((EDGE, LANES), jnp.float32)
                basis[k, 0, g, inner] = base[k, g, inner] + pull[g, inner] * flow[k, g : g + 1, :]
                basis[k, 0, g, below] = jnp.zeros((EDGE, LANES), jnp.float32)
            for step in range(ITERS):
                basis[k, step + 1, new] = advance(basis[k, step, read], step, new, slice(None), kept)
            for step in range(ITERS, REACH):
                value = basis[k, step, read, tail] if step == ITERS else reach[k, step - ITERS - 1, read]
                reach[k, step - ITERS, new] = advance(value, step, new, tail, kept)

    def own_sums(first, last):
        count = last - first
        over = slice(first, last)
        blocks = []
        gathered = jnp.zeros((REACH * EDGE, LANES), jnp.float32)
        for k in range(2):
            lines = []
            for i, j in PAIRS:
                product = basis[k, i, over] * basis[k, j, over]
                total = jnp.sum(product.reshape(count * (rows + 2 * EDGE) // 8, 8, LANES), axis=0)
                lines.append(jnp.sum(total, axis=0, keepdims=True))
            lines += [jnp.zeros((1, LANES), jnp.float32)] * (16 - len(lines))
            reached = [basis[k, step, over, below] for step in range(1, ITERS + 1)]
            reached += [reach[k, step, over, EDGE:] for step in range(REACH - ITERS)]
            strip = []
            lines.append(jnp.zeros((1, LANES), jnp.float32))
            for value in reached:
                weighted = pull[over, below] * value
                strip.append(jnp.concatenate([weighted[g] for g in range(count)], axis=1))
                lines.append(jnp.sum(jnp.sum(base[k, over, below] * value, axis=0), axis=0, keepdims=True))
            blocks += [jnp.concatenate(lines[n : n + 8], axis=0) for n in (0, 8, 16)]
            left = jnp.concatenate(strip, axis=0)
            for _ in range(3):
                piece = left.astype(jnp.bfloat16)
                gathered = gathered + matmul(piece, pick[k, first * LANES : last * LANES])
                left = left - piece.astype(jnp.float32)
        gathered = jnp.sum(gathered.reshape(REACH, EDGE, LANES), axis=1)
        return blocks + [jnp.concatenate([jnp.zeros((1, LANES), jnp.float32), gathered], axis=0)]

    def folded(block):
        block = block + pltpu.roll(block, LANES // 2, 1)
        return block + pltpu.roll(block, LANES // 4, 1)

    own_basis(0, known, 0)
    early = own_sums(0, known - 1)

    @pl.when(has_next)
    def _():
        lax.fori_loop(pause, chunks, correlate, 0)

    pl.when(has_above)(lambda: flow_copy(True).start())
    pl.when(has_below)(lambda: flow_copy(False).start())
    own_basis(known - 2, tiles, 1)
    blocks = [p + q for p, q in zip(early, own_sums(known - 1, tiles))]
    sums = [folded(blocks[n]) for n in (0, 1, 3, 4)]
    priors = [folded(blocks[n]) for n in (2, 5)]
    mine = sums[3]
    for n in range(3):
        mine = jnp.where(part == n, sums[n], mine)
    share[8:] = mine
    crossing = 2.0 * jnp.where(part < 2, blocks[6], jnp.where(part == 2, priors[0], priors[1]))
    top = lax.broadcasted_iota(jnp.int32, (8, LANES), 0) == 0
    share[:8] = jnp.where(top, listed[...], crossing)

    def share_copy(n):
        return pltpu.make_async_remote_copy(
            share,
            shares.at[blk],
            share_send.at[n],
            share_recv.at[n],
            device_id={"blk": others[n]},
            device_id_type=MESH,
        )

    for n in range(bands - 1):
        share_copy(n).start()
    shares[blk] = share[...]

    @pl.when(has_below)
    def _():
        flow_copy(True).wait_recv()

    @pl.when(has_above)
    def _():
        flow_copy(False).wait_recv()

    @pl.when(jnp.logical_not(has_below))
    def _():
        flow_in[0] = jnp.zeros_like(flow)

    @pl.when(jnp.logical_not(has_above))
    def _():
        flow_in[1] = jnp.zeros_like(flow)

    for k in range(2):
        for g in range(tiles):
            for source, first_row, count in (
                (flow_in.at[1], 0, EDGE),
                (flow, EDGE, rows),
                (flow_in.at[0], EDGE + rows, EDGE),
            ):
                at = slice(first_row, first_row + count)
                whole[k, 0, g, at] = base[k, g, at] + pull[g, at] * source[k, g : g + 1, :]
        for step in range(ITERS - 1):
            whole[k, step + 1] = advance(whole[k, step], step)

    for n in range(bands - 1):
        share_copy(n).wait_recv()
    total = jnp.sum(shares[:, 8:], axis=0)
    quarters = [jnp.sum(jnp.where(part == n, total, 0.0), axis=1, keepdims=True) for n in range(4)]
    crossed = jnp.zeros((8, LANES), jnp.float32)
    for n in range(bands - 1):
        crossed = crossed + shares[n, :8] * jnp.where(lane[:1] < LANES // 2, shares[n + 1, :1], 1.0)
    halves = [jnp.sum(jnp.where(part % 2 == k, crossed, 0.0), axis=1, keepdims=True) for k in range(2)]
    halves = [jnp.where(lane[:1] < LANES // 2, halves[0][m : m + 1], halves[1][m : m + 1]) for m in range(REACH + 1)]
    gram = {}
    for n, pair in enumerate(PAIRS):
        line = [quarters[2 * k + n // 8][n % 8 : n % 8 + 1] for k in range(2)]
        gram[pair] = jnp.where(lane[:1] < LANES // 2, line[0], line[1])
        degree = sum(pair)
        if degree:
            gram[pair] = gram[pair] + halves[degree]
        if pair[0] % 2 and pair[1] % 2:
            gram[pair] = gram[pair] + SCALE * (SHIFTS[1] - SHIFTS[0]) * halves[degree - 1]
    found = coefficients(gram)
    for k in range(2):
        weights = [value[:, k * LANES // 2 : k * LANES // 2 + 1] for value in found]
        for g in range(tiles):
            at = slice(EDGE, EDGE + rows)
            value = weights[0] * whole[k, 0, g, at]
            for step in range(1, ITERS):
                value = value + weights[step] * whole[k, step, g, at]
            out_ref[k, :, g * LANES : (g + 1) * LANES] = value

    for n in range(bands - 1):
        share_copy(n).wait_send()

    @pl.when(has_above)
    def _():
        edge_copy(True).wait_send()
        flow_copy(True).wait_send()

    @pl.when(has_below)
    def _():
        edge_copy(False).wait_send()
        flow_copy(False).wait_send()

    def drain(c, _):
        sent(c).wait_send()
        return 0

    @pl.when(has_prev)
    def _():
        lax.fori_loop(0, chunks, drain, 0)


def per_device(sections, bands, image, tissue_mask, anchor, fixed_nodes, prior_shift):
    _, size, columns = image.shape
    _, rows, nodes = anchor.shape
    chunks = columns // PAIR
    tiles = nodes // LANES
    wide = 2 * EDGE + rows
    width = 3 * nodes // 4
    both, narrow = tables()
    operands = image, tissue_mask, anchor, fixed_nodes, prior_shift, jnp.asarray(both), jnp.asarray(narrow)
    operands = [pltpu.with_memory_space_constraint(operand, pltpu.HBM) for operand in operands]
    out = pl.pallas_call(
        functools.partial(kernel, sections, bands),
        out_shape=jax.ShapeDtypeStruct((2, rows, nodes), jnp.float32),
        in_specs=[pl.BlockSpec(memory_space=pl.ANY)] * 7,
        out_specs=pl.BlockSpec(memory_space=pltpu.VMEM),
        scratch_shapes=[
            pltpu.VMEM((chunks, size, PAIR), jnp.bfloat16),
            pltpu.VMEM((chunks, size, PAIR), jnp.int32),
            pltpu.VMEM((chunks, size, PAIR), jnp.bfloat16),
            pltpu.VMEM((chunks, size, PAIR), jnp.bfloat16),
            pltpu.VMEM((chunks, PAIR, PAIR), jnp.bfloat16),
            pltpu.VMEM((PAIR, PAIR), jnp.bfloat16),
            pltpu.VMEM((PAIR, SIZE), jnp.bfloat16),
            pltpu.VMEM((rows, nodes), jnp.float32),
            pltpu.VMEM((rows, nodes), jnp.int32),
            pltpu.VMEM((2, rows, nodes), jnp.float32),
            pltpu.VMEM((4 * SPAN, 2 * width), jnp.bfloat16),
            pltpu.VMEM((4 * SPAN, width), jnp.bfloat16),
            pltpu.VMEM((4 * SPAN, 2 * width), jnp.bfloat16),
            pltpu.VMEM((4 * SPAN, width), jnp.bfloat16),
            pltpu.VMEM((tiles, wide, LANES), jnp.float32),
            pltpu.VMEM((tiles, wide, LANES), jnp.float32),
            pltpu.VMEM((tiles, wide, LANES), jnp.float32),
            pltpu.VMEM((2, tiles, wide, LANES), jnp.float32),
            pltpu.VMEM((2, tiles, LANES), jnp.float32),
            pltpu.VMEM((2, 2, tiles, LANES), jnp.float32),
            pltpu.VMEM((8, LANES), jnp.float32),
            pltpu.VMEM((2, nodes, LANES), jnp.bfloat16),
            pltpu.VMEM((2, ITERS + 1, tiles, wide, LANES), jnp.float32),
            pltpu.VMEM((2, REACH - ITERS, tiles, 2 * EDGE, LANES), jnp.float32),
            pltpu.VMEM((2, ITERS, tiles, wide, LANES), jnp.float32),
            pltpu.VMEM((16, LANES), jnp.float32),
            pltpu.VMEM((bands, 16, LANES), jnp.float32),
            pltpu.SemaphoreType.DMA((2, chunks)),
            pltpu.SemaphoreType.DMA((5,)),
            pltpu.SemaphoreType.DMA((chunks,)),
            pltpu.SemaphoreType.DMA((chunks,)),
            pltpu.SemaphoreType.DMA((2,)),
            pltpu.SemaphoreType.DMA((2,)),
            pltpu.SemaphoreType.DMA((2,)),
            pltpu.SemaphoreType.DMA((2,)),
            pltpu.SemaphoreType.DMA((bands - 1,)),
            pltpu.SemaphoreType.DMA((bands - 1,)),
            pltpu.SemaphoreType.REGULAR((2,)),
        ],
        compiler_params=pltpu.CompilerParams(
            collective_id=0, has_side_effects=True, vmem_limit_bytes=40 * 1024 * 1024
        ),
        cost_estimate=pl.CostEstimate(flops=2_400_000_000, bytes_accessed=4_000_000, transcendentals=0),
    )(*operands)
    return out[:, None]


def solution(mesh):
    sections, bands = mesh.shape["sec"], mesh.shape["blk"]
    return jax.shard_map(
        functools.partial(per_device, sections, bands),
        mesh=mesh,
        in_specs=(
            P("sec", "blk", None),
            P("sec", "blk", None),
            P("sec", "blk", None),
            P("sec", "blk", None),
            P(None, "sec", "blk", None),
        ),
        out_specs=P(None, "sec", "blk", None),
        check_vma=False,
    )
```

```python
import functools
import math

import jax
import jax.numpy as jnp
import ml_dtypes
import numpy as np
from jax import lax
from jax.experimental import pallas as pl
from jax.experimental.pallas import tpu as pltpu
from jax.sharding import PartitionSpec as P

MESH = pl.DeviceIdType.MESH
ITERS = 4
SIZE = 128
PAIR = 2 * SIZE
LANES = 128
EDGE = 8
SPAN = 4
REACH = 2 * ITERS - 1
SHIFTS = (1.0, 4.0, 1.0, 4.0, 1.0, 4.0, 1.0)
SCALE = 0.25
PAIRS = tuple((i, j) for i in range(ITERS) for j in range(i, ITERS)) + tuple((i, ITERS) for i in range(ITERS))


def tables():
    j = np.arange(SIZE)
    angle = (j[:, None] * j[None, :] % SIZE).astype(np.float32) * np.float32(2.0 * math.pi / SIZE)
    cosine = np.cos(angle).astype(ml_dtypes.bfloat16)
    sine = np.sin(angle).astype(ml_dtypes.bfloat16)
    both = np.block([[cosine, -sine], [sine, cosine]])
    return both, np.concatenate([cosine, -sine], axis=0)


def matmul(left, right):
    return jnp.dot(left, right, preferred_element_type=jnp.float32)


def beside(pair):
    rows = [
        jnp.concatenate([pair[:SIZE, p * SIZE : (p + 1) * SIZE], pair[SIZE:, p * SIZE : (p + 1) * SIZE]], axis=1)
        for p in range(2)
    ]
    return jnp.concatenate(rows, axis=0)


def stacked(re, im):
    rows = [jnp.concatenate([part[:SIZE], part[SIZE:]], axis=1) for part in (re, im)]
    return jnp.concatenate(rows, axis=0)


def spectrum(block, narrow, both):
    half = matmul(narrow, block).astype(jnp.bfloat16)
    return matmul(beside(half), both).astype(jnp.bfloat16)


def offsets(shape, axis):
    index = lax.broadcasted_iota(jnp.int32, shape, axis)
    return (((index + SIZE // 2) % SIZE) - SIZE // 2).astype(jnp.float32)


def flows_of(own, other, narrow, both):
    a = own.astype(jnp.float32)
    b = other.astype(jnp.float32)
    a_re, a_im, b_re, b_im = a[:, :SIZE], a[:, SIZE:], b[:, :SIZE], b[:, SIZE:]
    cross_re = (a_re * b_re + a_im * b_im).astype(jnp.bfloat16)
    cross_im = (a_im * b_re - a_re * b_im).astype(jnp.bfloat16)
    back = matmul(both, stacked(cross_re, cross_im)).astype(jnp.bfloat16)
    corr = matmul(beside(back), narrow)
    weight = (corr * corr).reshape(2, SIZE, SIZE)
    whole = jnp.sum(weight, axis=1)
    tilted = jnp.sum(weight * offsets((1, SIZE, SIZE), 1), axis=1)
    unit = 2.0**-42
    total = jnp.sum(whole, axis=1, keepdims=True) * unit + 1e-6
    row_flow = jnp.sum(tilted, axis=1, keepdims=True) * unit / total
    col_flow = jnp.sum(whole * offsets((2, SIZE), 1), axis=1, keepdims=True) * unit / total
    return row_flow, col_flow


def neighbours(value):
    tiles, rows, _ = value.shape
    lane = lax.broadcasted_iota(jnp.int32, value.shape, 2)
    none = jnp.zeros((1, rows, LANES), value.dtype)
    right = pltpu.roll(value, 1, 2)
    right = jnp.where(lane == 0, jnp.concatenate([none, right[:-1]], axis=0), right)
    left = pltpu.roll(value, LANES - 1, 2)
    left = jnp.where(lane == LANES - 1, jnp.concatenate([left[1:], none], axis=0), left)
    return pltpu.roll(value, 1, 1) + pltpu.roll(value, rows - 1, 1) + right + left


def crossed(pair, powers):
    degree = sum(pair)
    if pair[0] % 2 and pair[1] % 2:
        return powers[degree] + SCALE * (SHIFTS[1] - SHIFTS[0]) * powers[degree - 1]
    return powers[degree]


def coefficients(gram):
    def inner(left, right):
        terms = [l * r * gram[min(i, j), max(i, j)] for i, l in enumerate(left) for j, r in enumerate(right)]
        return functools.reduce(lambda p, q: p + q, terms)

    zero = jnp.zeros_like(gram[0, 0])
    solution = [zero] * ITERS
    residual = [jnp.ones_like(zero)]
    direction = list(residual)
    norm_now = gram[0, 0]
    for step in range(ITERS):
        image = [SHIFTS[j] * direction[j] for j in range(step + 1)] + [zero]
        image = [image[j] + (direction[j - 1] / SCALE if j else 0.0) for j in range(step + 2)]
        curve = inner(direction, image)
        alpha = jnp.where(curve > 0.0, jnp.clip(norm_now / curve, 0.0, 10.1), 0.0)
        solution = [solution[j] + alpha * direction[j] if j <= step else solution[j] for j in range(ITERS)]
        if step == ITERS - 1:
            break
        residual = [r - alpha * i for r, i in zip(residual + [zero], image)]
        norm_next = jnp.maximum(inner(residual, residual), 0.0)
        beta = jnp.where(norm_now > 0.0, norm_next / norm_now, 0.0)
        direction = [r + beta * d for r, d in zip(residual, direction + [zero])]
        norm_now = norm_next
    return solution


def kernel(
    sections,
    bands,
    image_hbm,
    mask_hbm,
    anchor_hbm,
    fixed_hbm,
    prior_hbm,
    both_hbm,
    narrow_hbm,
    out_ref,
    image,
    mask,
    masked,
    arrived,
    spectra,
    both,
    narrow,
    anchor,
    fixed,
    prior,
    edge_up,
    edge_down,
    from_below,
    from_above,
    pull,
    diag,
    link,
    base,
    flow,
    flow_in,
    listed,
    pick,
    basis,
    reach,
    whole,
    share,
    shares,
    load_sem,
    mesh_sem,
    send_sem,
    recv_sem,
    edge_send,
    edge_recv,
    flow_send,
    flow_recv,
    share_send,
    share_recv,
    round_sem,
):
    chunks = image.shape[0]
    tiles = pull.shape[0]
    rows = anchor.shape[0]
    sec = lax.axis_index("sec")
    blk = lax.axis_index("blk")
    has_above, has_below = blk > 0, blk < bands - 1
    has_prev, has_next = sec > 0, sec < sections - 1
    turns = bands // 4
    here = (blk // 4, lax.rem(blk // 2, 2), lax.rem(blk, 2))

    def moved(dx, dy, dc):
        return lax.rem(here[0] + dx, turns) * 4 + lax.rem(here[1] + dy, 2) * 2 + lax.rem(here[2] + dc, 2)

    order = [dx if dx <= turns // 2 else dx - turns for dx in range(turns)]
    steps = sorted(
        ((dx % turns, dy, dc) for dx in order for dy in range(2) for dc in range(2)),
        key=lambda step: (-step[1], -min(step[0], turns - step[0]), -step[2]),
    )
    others = [moved(*step) for step in steps if any(step)]

    def pixels(c):
        return pl.ds(pl.multiple_of(c * PAIR, PAIR), PAIR)

    def loads(c):
        return (
            pltpu.make_async_copy(image_hbm.at[0, :, pixels(c)], image.at[c], load_sem.at[0, c]),
            pltpu.make_async_copy(mask_hbm.at[0, :, pixels(c)], mask.at[c], load_sem.at[1, c]),
        )

    def sent(c):
        return pltpu.make_async_remote_copy(
            masked.at[c], arrived.at[c], send_sem.at[c], recv_sem.at[c], device_id={"sec": sec - 1}, device_id_type=MESH
        )

    mesh_loads = [
        pltpu.make_async_copy(both_hbm, both, mesh_sem.at[0]),
        pltpu.make_async_copy(narrow_hbm, narrow, mesh_sem.at[1]),
        pltpu.make_async_copy(anchor_hbm.at[0], anchor, mesh_sem.at[2]),
        pltpu.make_async_copy(fixed_hbm.at[0], fixed, mesh_sem.at[3]),
        pltpu.make_async_copy(prior_hbm.at[:, 0], prior, mesh_sem.at[4]),
    ]

    barrier = pltpu.get_barrier_semaphore()

    def greet(device):
        pl.semaphore_signal(barrier, inc=1, device_id=device, device_id_type=MESH)

    pl.when(has_prev)(lambda: greet({"sec": sec - 1}))
    pl.when(has_next)(lambda: greet({"sec": sec + 1}))
    pl.when(has_above)(lambda: greet({"blk": blk - 1}))
    pl.when(has_below)(lambda: greet({"blk": blk + 1}))
    across, over = moved(0, 0, 1), moved(0, 1, 0)
    along = [moved(dx, 0, 0) for dx in range(1, turns)]
    for other in [across, over] + along:
        greet({"blk": other})

    def start_loads(c, _):
        for copy in loads(c):
            copy.start()
        return 0

    lax.fori_loop(0, 1, start_loads, 0)
    for copy in mesh_loads:
        copy.start()
    lax.fori_loop(1, chunks, start_loads, 0)

    def hide(c):
        for copy in loads(c):
            copy.wait()
        masked[c] = image[c] * mask[c].astype(jnp.float32).astype(jnp.bfloat16)

    def hide_and_send(c, _):
        hide(c)
        pl.when(has_prev)(lambda: sent(c).start())
        return 0

    hide(0)
    for copy in mesh_loads:
        copy.wait()
    free = 1.0 - fixed[...].astype(jnp.float32)
    own_pull = free * anchor[...]
    own = [own_pull, own_pull * prior[0], own_pull * prior[1]]

    def edge_copy(up):
        slot = 0 if up else 1
        return pltpu.make_async_remote_copy(
            edge_up if up else edge_down,
            from_below if up else from_above,
            edge_send.at[slot],
            edge_recv.at[slot],
            device_id={"blk": blk - 1 if up else blk + 1},
            device_id_type=MESH,
        )

    def flow_copy(up):
        slot = 0 if up else 1
        return pltpu.make_async_remote_copy(
            flow,
            flow_in.at[slot],
            flow_send.at[slot],
            flow_recv.at[slot],
            device_id={"blk": blk - 1 if up else blk + 1},
            device_id_type=MESH,
        )

    nodes = tiles * LANES

    def packed(first, count):
        flat = [part[at : at + SPAN] for part in own for at in range(first, first + count, SPAN)]
        flat = jnp.concatenate(flat, axis=1)
        width = flat.shape[1] // 4
        return jnp.concatenate([flat[:, k * width : (k + 1) * width] for k in range(4)], axis=0).astype(jnp.bfloat16)

    def unpacked(block):
        block = block.astype(jnp.float32)
        flat = jnp.concatenate([block[k * SPAN : (k + 1) * SPAN] for k in range(4)], axis=1)
        parts = [flat[:, k : k + nodes] for k in range(0, flat.shape[1], nodes)]
        each = len(parts) // 3
        return [parts[k * each : (k + 1) * each] for k in range(3)]

    edge_up[...] = packed(0, EDGE)
    edge_down[...] = packed(rows - SPAN, SPAN)
    greeted = has_prev, has_next, has_above, has_below
    pl.semaphore_wait(barrier, turns + 1 + functools.reduce(lambda p, q: p + q, [g.astype(jnp.int32) for g in greeted]))
    pl.when(has_above)(lambda: edge_copy(True).start())
    pl.when(has_below)(lambda: edge_copy(False).start())
    pl.when(has_prev)(lambda: sent(0).start())
    pl.semaphore_signal(round_sem.at[0], inc=1, device_id={"blk": across}, device_id_type=MESH)
    lax.fori_loop(1, 8, hide_and_send, 0)
    pl.semaphore_wait(round_sem.at[0], 1)
    pl.semaphore_signal(round_sem.at[1], inc=1, device_id={"blk": over}, device_id_type=MESH)
    lax.fori_loop(8, chunks, hide_and_send, 0)

    def own_spectrum(c, _):
        spectra[c] = spectrum(masked[c], narrow[...], both[...])
        return 0

    lax.fori_loop(0, chunks, own_spectrum, 0)
    pl.semaphore_wait(round_sem.at[1], 1)

    pull[...] = jnp.zeros_like(pull)
    base[...] = jnp.zeros_like(base)
    for g in range(tiles):
        at = slice(g * LANES, (g + 1) * LANES)
        pull[g, EDGE : EDGE + rows] = own[0][:, at]
        base[0, g, EDGE : EDGE + rows] = own[1][:, at]
        base[1, g, EDGE : EDGE + rows] = own[2][:, at]

    def take_edge(block, first, count):
        parts = unpacked(block)
        for n in range(0, count, SPAN):
            some = min(SPAN, count - n)
            to = slice(first + n, first + n + some)
            for g in range(tiles):
                at = slice(g * LANES, (g + 1) * LANES)
                pull[g, to] = parts[0][n // SPAN][:some, at]
                base[0, g, to] = parts[1][n // SPAN][:some, at]
                base[1, g, to] = parts[2][n // SPAN][:some, at]

    flow[...] = jnp.zeros_like(flow)
    listed[...] = jnp.zeros_like(listed)
    lane = lax.broadcasted_iota(jnp.int32, (8, LANES), 1)
    patch = lax.broadcasted_iota(jnp.int32, (nodes, LANES), 0) // (LANES // 4)
    for k in range(2):
        column = lax.broadcasted_iota(jnp.int32, (nodes, LANES), 1)
        pick[k] = jnp.where(column == patch + k * (LANES // 4), 1.0, 0.0).astype(jnp.bfloat16)
    tile_row = lax.broadcasted_iota(jnp.int32, (tiles, LANES), 0)
    quarter = lax.broadcasted_iota(jnp.int32, (tiles, LANES), 1) // (LANES // 4)

    def correlate(c, _):
        sent(c).wait_recv()
        other = spectrum(arrived[c], narrow[...], both[...])
        for k, value in enumerate(flows_of(spectra[c], other, narrow[...], both[...])):
            held = flow[k]
            for p in range(2):
                slot = lane == k * (LANES // 4) + 2 * c + p
                listed[...] = jnp.where(slot, value[p : p + 1], listed[...])
                spot = (tile_row == c // 2) & (quarter == 2 * (c % 2) + p)
                held = jnp.where(spot, value[p : p + 1], held)
            flow[k] = held
        return 0

    pause = chunks - 4
    known = pause * PAIR // SIZE // 4

    @pl.when(has_next)
    def _():
        lax.fori_loop(0, pause, correlate, 0)

    @pl.when(has_below)
    def _():
        edge_copy(True).wait_recv()
        take_edge(from_below[...], EDGE + rows, REACH)

    @pl.when(has_above)
    def _():
        edge_copy(False).wait_recv()
        take_edge(from_above[...], EDGE - SPAN, SPAN)

    loose = jnp.where(pull[...] > 0.0, SCALE, 0.0)
    link[...] = loose
    diag[...] = 4.0 * loose + SCALE * pull[...]

    part = lane // (LANES // 8)
    below = slice(EDGE + rows, EDGE + rows + EDGE)
    tail = slice(rows, rows + 2 * EDGE)

    def advance(value, step, tile=slice(None), at=slice(None), kept=0):
        return (diag[tile, at] - SCALE * SHIFTS[step]) * value[kept:] - link[tile, at] * neighbours(value)[kept:]

    def own_basis(first, last, kept):
        new, read = slice(first + kept, last), slice(first, last)
        for k in range(2):
            for g in range(first + kept, last):
                inner = slice(EDGE, EDGE + rows)
                basis[k, 0, g, :EDGE] = jnp.zeros((EDGE, LANES), jnp.float32)
                basis[k, 0, g, inner] = base[k, g, inner] + pull[g, inner] * flow[k, g : g + 1, :]
                basis[k, 0, g, below] = jnp.zeros((EDGE, LANES), jnp.float32)
            for step in range(ITERS):
                basis[k, step + 1, new] = advance(basis[k, step, read], step, new, slice(None), kept)
            for step in range(ITERS, REACH):
                value = basis[k, step, read, tail] if step == ITERS else reach[k, step - ITERS - 1, read]
                reach[k, step - ITERS, new] = advance(value, step, new, tail, kept)

    def own_sums(first, last):
        count = last - first
        over = slice(first, last)
        blocks = []
        gathered = jnp.zeros((REACH * EDGE, LANES), jnp.float32)
        for k in range(2):
            lines = []
            for i, j in PAIRS:
                product = basis[k, i, over] * basis[k, j, over]
                total = jnp.sum(product.reshape(count * (rows + 2 * EDGE) // 8, 8, LANES), axis=0)
                lines.append(jnp.sum(total, axis=0, keepdims=True))
            reached = [basis[k, step, over, below] for step in range(1, ITERS + 1)]
            reached += [reach[k, step, over, EDGE:] for step in range(REACH - ITERS)]
            strip, prior_lines = [], [jnp.zeros((1, LANES), jnp.float32)]
            for value in reached:
                weighted = pull[over, below] * value
                strip.append(jnp.concatenate([weighted[g] for g in range(count)], axis=1))
                prior_lines.append(2.0 * jnp.sum(jnp.sum(base[k, over, below] * value, axis=0), axis=0, keepdims=True))
            lines = [line + crossed(pair, prior_lines) for line, pair in zip(lines, PAIRS)]
            lines += [jnp.zeros((1, LANES), jnp.float32)] * (16 - len(lines))
            blocks += [jnp.concatenate(lines[n : n + 8], axis=0) for n in (0, 8)]
            left = jnp.concatenate(strip, axis=0)
            for _ in range(3):
                piece = left.astype(jnp.bfloat16)
                gathered = gathered + matmul(piece, pick[k, first * LANES : last * LANES])
                left = left - piece.astype(jnp.float32)
        gathered = jnp.sum(gathered.reshape(REACH, EDGE, LANES), axis=1)
        return blocks + [jnp.concatenate([jnp.zeros((1, LANES), jnp.float32), gathered], axis=0)]

    def folded(block):
        for lanes in (LANES // 2, LANES // 4, LANES // 8):
            block = block + pltpu.roll(block, lanes, 1)
        return block

    own_basis(0, known, 0)
    early = own_sums(0, known - 1)

    @pl.when(has_next)
    def _():
        lax.fori_loop(pause, chunks, correlate, 0)

    pl.when(has_above)(lambda: flow_copy(True).start())
    pl.when(has_below)(lambda: flow_copy(False).start())
    own_basis(known - 2, tiles, 1)
    blocks = [p + q for p, q in zip(early, own_sums(known - 1, tiles))]
    mine = 2.0 * blocks[4]
    for n in range(4):
        mine = jnp.where(part == 4 + n, folded(blocks[n]), mine)
    top = lax.broadcasted_iota(jnp.int32, (8, LANES), 0) == 0
    share[...] = jnp.where(top & (part < 4), listed[...], mine)

    def share_copy(n):
        return pltpu.make_async_remote_copy(
            share,
            shares.at[blk],
            share_send.at[n],
            share_recv.at[n],
            device_id={"blk": others[n]},
            device_id_type=MESH,
        )

    for n in range(bands - 1):
        share_copy(n).start()
    shares[blk] = share[...]

    @pl.when(has_below)
    def _():
        flow_copy(True).wait_recv()

    @pl.when(has_above)
    def _():
        flow_copy(False).wait_recv()

    @pl.when(jnp.logical_not(has_below))
    def _():
        flow_in[0] = jnp.zeros_like(flow)

    @pl.when(jnp.logical_not(has_above))
    def _():
        flow_in[1] = jnp.zeros_like(flow)

    for k in range(2):
        for g in range(tiles):
            for source, first_row, count in (
                (flow_in.at[1], 0, EDGE),
                (flow, EDGE, rows),
                (flow_in.at[0], EDGE + rows, EDGE),
            ):
                at = slice(first_row, first_row + count)
                whole[k, 0, g, at] = base[k, g, at] + pull[g, at] * source[k, g : g + 1, :]
        for step in range(ITERS - 1):
            whole[k, step + 1] = advance(whole[k, step], step)

    for n in range(bands - 1):
        share_copy(n).wait_recv()
    total = shares[bands - 1]
    for n in range(bands - 1):
        total = total + shares[n] * jnp.where(lane[:1] < LANES // 2, shares[n + 1, :1], 1.0)
    sums = [jnp.sum(jnp.where(part == 4 + n, total, 0.0), axis=1, keepdims=True) for n in range(4)]
    across_bands = [jnp.sum(jnp.where(part // 2 == k, total, 0.0), axis=1, keepdims=True) for k in range(2)]

    def by_component(pair, n):
        return jnp.where(lane[:1] < LANES // 2, pair[0][n : n + 1], pair[1][n : n + 1])

    none = jnp.zeros((1, LANES), jnp.float32)
    cross_lines = [none] + [by_component(across_bands, m) for m in range(1, REACH + 1)]
    gram = {}
    for n, pair in enumerate(PAIRS):
        own_line = by_component((sums[n // 8], sums[2 + n // 8]), n % 8)
        gram[pair] = own_line + crossed(pair, cross_lines)
    found = coefficients(gram)
    for k in range(2):
        weights = [value[:, k * LANES // 2 : k * LANES // 2 + 1] for value in found]
        for g in range(tiles):
            at = slice(EDGE, EDGE + rows)
            value = weights[0] * whole[k, 0, g, at]
            for step in range(1, ITERS):
                value = value + weights[step] * whole[k, step, g, at]
            out_ref[k, :, g * LANES : (g + 1) * LANES] = value

    for n in range(bands - 1):
        share_copy(n).wait_send()

    @pl.when(has_above)
    def _():
        edge_copy(True).wait_send()
        flow_copy(True).wait_send()

    @pl.when(has_below)
    def _():
        edge_copy(False).wait_send()
        flow_copy(False).wait_send()

    def drain(c, _):
        sent(c).wait_send()
        return 0

    @pl.when(has_prev)
    def _():
        lax.fori_loop(0, chunks, drain, 0)


def per_device(sections, bands, image, tissue_mask, anchor, fixed_nodes, prior_shift):
    _, size, columns = image.shape
    _, rows, nodes = anchor.shape
    chunks = columns // PAIR
    tiles = nodes // LANES
    wide = 2 * EDGE + rows
    width = 3 * nodes // 4
    both, narrow = tables()
    operands = image, tissue_mask, anchor, fixed_nodes, prior_shift, jnp.asarray(both), jnp.asarray(narrow)
    operands = [pltpu.with_memory_space_constraint(operand, pltpu.HBM) for operand in operands]
    out = pl.pallas_call(
        functools.partial(kernel, sections, bands),
        out_shape=jax.ShapeDtypeStruct((2, rows, nodes), jnp.float32),
        in_specs=[pl.BlockSpec(memory_space=pl.ANY)] * 7,
        out_specs=pl.BlockSpec(memory_space=pltpu.VMEM),
        scratch_shapes=[
            pltpu.VMEM((chunks, size, PAIR), jnp.bfloat16),
            pltpu.VMEM((chunks, size, PAIR), jnp.int32),
            pltpu.VMEM((chunks, size, PAIR), jnp.bfloat16),
            pltpu.VMEM((chunks, size, PAIR), jnp.bfloat16),
            pltpu.VMEM((chunks, PAIR, PAIR), jnp.bfloat16),
            pltpu.VMEM((PAIR, PAIR), jnp.bfloat16),
            pltpu.VMEM((PAIR, SIZE), jnp.bfloat16),
            pltpu.VMEM((rows, nodes), jnp.float32),
            pltpu.VMEM((rows, nodes), jnp.int32),
            pltpu.VMEM((2, rows, nodes), jnp.float32),
            pltpu.VMEM((4 * SPAN, 2 * width), jnp.bfloat16),
            pltpu.VMEM((4 * SPAN, width), jnp.bfloat16),
            pltpu.VMEM((4 * SPAN, 2 * width), jnp.bfloat16),
            pltpu.VMEM((4 * SPAN, width), jnp.bfloat16),
            pltpu.VMEM((tiles, wide, LANES), jnp.float32),
            pltpu.VMEM((tiles, wide, LANES), jnp.float32),
            pltpu.VMEM((tiles, wide, LANES), jnp.float32),
            pltpu.VMEM((2, tiles, wide, LANES), jnp.float32),
            pltpu.VMEM((2, tiles, LANES), jnp.float32),
            pltpu.VMEM((2, 2, tiles, LANES), jnp.float32),
            pltpu.VMEM((8, LANES), jnp.float32),
            pltpu.VMEM((2, nodes, LANES), jnp.bfloat16),
            pltpu.VMEM((2, ITERS + 1, tiles, wide, LANES), jnp.float32),
            pltpu.VMEM((2, REACH - ITERS, tiles, 2 * EDGE, LANES), jnp.float32),
            pltpu.VMEM((2, ITERS, tiles, wide, LANES), jnp.float32),
            pltpu.VMEM((8, LANES), jnp.float32),
            pltpu.VMEM((bands, 8, LANES), jnp.float32),
            pltpu.SemaphoreType.DMA((2, chunks)),
            pltpu.SemaphoreType.DMA((5,)),
            pltpu.SemaphoreType.DMA((chunks,)),
            pltpu.SemaphoreType.DMA((chunks,)),
            pltpu.SemaphoreType.DMA((2,)),
            pltpu.SemaphoreType.DMA((2,)),
            pltpu.SemaphoreType.DMA((2,)),
            pltpu.SemaphoreType.DMA((2,)),
            pltpu.SemaphoreType.DMA((bands - 1,)),
            pltpu.SemaphoreType.DMA((bands - 1,)),
            pltpu.SemaphoreType.REGULAR((2,)),
        ],
        compiler_params=pltpu.CompilerParams(
            collective_id=0, has_side_effects=True, vmem_limit_bytes=40 * 1024 * 1024
        ),
        cost_estimate=pl.CostEstimate(flops=2_400_000_000, bytes_accessed=4_000_000, transcendentals=0),
    )(*operands)
    return out[:, None]


def solution(mesh):
    sections, bands = mesh.shape["sec"], mesh.shape["blk"]
    return jax.shard_map(
        functools.partial(per_device, sections, bands),
        mesh=mesh,
        in_specs=(
            P("sec", "blk", None),
            P("sec", "blk", None),
            P("sec", "blk", None),
            P("sec", "blk", None),
            P(None, "sec", "blk", None),
        ),
        out_specs=P(None, "sec", "blk", None),
        check_vma=False,
    )
```

```python
import functools
import math

import jax
import jax.numpy as jnp
import ml_dtypes
import numpy as np
from jax import lax
from jax.experimental import pallas as pl
from jax.experimental.pallas import tpu as pltpu
from jax.sharding import PartitionSpec as P

MESH = pl.DeviceIdType.MESH
ITERS = 4
SIZE = 128
PAIR = 2 * SIZE
LANES = 128
EDGE = 8
SPAN = 4
REACH = 2 * ITERS - 1
GROUP = 4
ASIDE = 10
SHIFTS = (1.0, 4.0, 1.0, 4.0, 1.0, 4.0, 1.0)
SCALE = 0.25
PAIRS = tuple((i, j) for i in range(ITERS) for j in range(i, ITERS)) + tuple((i, ITERS) for i in range(ITERS))


def tables():
    j = np.arange(SIZE)
    angle = (j[:, None] * j[None, :] % SIZE).astype(np.float32) * np.float32(2.0 * math.pi / SIZE)
    cosine = np.cos(angle).astype(ml_dtypes.bfloat16)
    sine = np.sin(angle).astype(ml_dtypes.bfloat16)
    both = np.block([[cosine, -sine], [sine, cosine]])
    return both, np.concatenate([cosine, -sine], axis=0)


def matmul(left, right):
    return jnp.dot(left, right, preferred_element_type=jnp.float32)


def beside(pair):
    rows = [
        jnp.concatenate([pair[:SIZE, p * SIZE : (p + 1) * SIZE], pair[SIZE:, p * SIZE : (p + 1) * SIZE]], axis=1)
        for p in range(2)
    ]
    return jnp.concatenate(rows, axis=0)


def stacked(re, im):
    rows = [jnp.concatenate([part[:SIZE], part[SIZE:]], axis=1) for part in (re, im)]
    return jnp.concatenate(rows, axis=0)


def spectrum(block, narrow, both):
    half = matmul(narrow, block).astype(jnp.bfloat16)
    return matmul(beside(half), both).astype(jnp.bfloat16)


def offsets(shape, axis):
    index = lax.broadcasted_iota(jnp.int32, shape, axis)
    return (((index + SIZE // 2) % SIZE) - SIZE // 2).astype(jnp.float32)


def flows_of(own, other, narrow, both):
    a = own.astype(jnp.float32)
    b = other.astype(jnp.float32)
    a_re, a_im, b_re, b_im = a[:, :SIZE], a[:, SIZE:], b[:, :SIZE], b[:, SIZE:]
    cross_re = (a_re * b_re + a_im * b_im).astype(jnp.bfloat16)
    cross_im = (a_im * b_re - a_re * b_im).astype(jnp.bfloat16)
    back = matmul(both, stacked(cross_re, cross_im)).astype(jnp.bfloat16)
    corr = matmul(beside(back), narrow)
    weight = (corr * corr).reshape(2, SIZE, SIZE)
    whole = jnp.sum(weight, axis=1)
    tilted = jnp.sum(weight * offsets((1, SIZE, SIZE), 1), axis=1)
    unit = 2.0**-42
    total = jnp.sum(whole, axis=1, keepdims=True) * unit + 1e-6
    row_flow = jnp.sum(tilted, axis=1, keepdims=True) * unit / total
    col_flow = jnp.sum(whole * offsets((2, SIZE), 1), axis=1, keepdims=True) * unit / total
    return row_flow, col_flow


def neighbours(value):
    tiles, rows, _ = value.shape
    lane = lax.broadcasted_iota(jnp.int32, value.shape, 2)
    none = jnp.zeros((1, rows, LANES), value.dtype)
    right = pltpu.roll(value, 1, 2)
    right = jnp.where(lane == 0, jnp.concatenate([none, right[:-1]], axis=0), right)
    left = pltpu.roll(value, LANES - 1, 2)
    left = jnp.where(lane == LANES - 1, jnp.concatenate([left[1:], none], axis=0), left)
    return pltpu.roll(value, 1, 1) + pltpu.roll(value, rows - 1, 1) + right + left


def crossed(pair, powers):
    degree = sum(pair)
    if pair[0] % 2 and pair[1] % 2:
        return powers[degree] + SCALE * (SHIFTS[1] - SHIFTS[0]) * powers[degree - 1]
    return powers[degree]


def coefficients(gram):
    def inner(left, right):
        terms = [l * r * gram[min(i, j), max(i, j)] for i, l in enumerate(left) for j, r in enumerate(right)]
        return functools.reduce(lambda p, q: p + q, terms)

    zero = jnp.zeros_like(gram[0, 0])
    solution = [zero] * ITERS
    residual = [jnp.ones_like(zero)]
    direction = list(residual)
    norm_now = gram[0, 0]
    for step in range(ITERS):
        image = [SHIFTS[j] * direction[j] for j in range(step + 1)] + [zero]
        image = [image[j] + (direction[j - 1] / SCALE if j else 0.0) for j in range(step + 2)]
        curve = inner(direction, image)
        alpha = jnp.where(curve > 0.0, jnp.clip(norm_now / curve, 0.0, 10.1), 0.0)
        solution = [solution[j] + alpha * direction[j] if j <= step else solution[j] for j in range(ITERS)]
        if step == ITERS - 1:
            break
        residual = [r - alpha * i for r, i in zip(residual + [zero], image)]
        norm_next = jnp.maximum(inner(residual, residual), 0.0)
        beta = jnp.where(norm_now > 0.0, norm_next / norm_now, 0.0)
        direction = [r + beta * d for r, d in zip(residual, direction + [zero])]
        norm_now = norm_next
    return solution


def kernel(
    sections,
    bands,
    image_hbm,
    mask_hbm,
    anchor_hbm,
    fixed_hbm,
    prior_hbm,
    both_hbm,
    narrow_hbm,
    out_ref,
    image,
    mask,
    masked,
    arrived,
    relay,
    spectra,
    both,
    narrow,
    anchor,
    fixed,
    prior,
    edge_up,
    edge_down,
    from_below,
    from_above,
    pull,
    diag,
    link,
    base,
    flow,
    flow_in,
    listed,
    pick,
    basis,
    reach,
    whole,
    share,
    shares,
    load_sem,
    mesh_sem,
    send_sem,
    recv_sem,
    edge_send,
    edge_recv,
    flow_send,
    flow_recv,
    share_send,
    share_recv,
    round_sem,
    relay_recv,
    relay_send,
):
    chunks = image.shape[0]
    tiles = pull.shape[0]
    rows = anchor.shape[0]
    sec = lax.axis_index("sec")
    blk = lax.axis_index("blk")
    has_above, has_below = blk > 0, blk < bands - 1
    has_prev, has_next = sec > 0, sec < sections - 1
    turns = bands // 4
    here = (blk // 4, lax.rem(blk // 2, 2), lax.rem(blk, 2))

    def moved(dx, dy, dc):
        return lax.rem(here[0] + dx, turns) * 4 + lax.rem(here[1] + dy, 2) * 2 + lax.rem(here[2] + dc, 2)

    order = [dx if dx <= turns // 2 else dx - turns for dx in range(turns)]
    steps = sorted(
        ((dx % turns, dy, dc) for dx in order for dy in range(2) for dc in range(2)),
        key=lambda step: (-step[1], -min(step[0], turns - step[0]), -step[2]),
    )
    others = [moved(*step) for step in steps if any(step)]

    group, groups = sec // GROUP, sections // GROUP
    place = lax.rem(sec, GROUP)
    gives = (place == 0) & (group > 0)
    passes = (place == 0) & (group < groups - 1)
    takes = (place == GROUP - 1) & (group < groups - 1)
    aside = jnp.where(gives, jnp.minimum(2 * (groups - group), ASIDE), 0)
    passing = jnp.where(passes, jnp.minimum(2 * (groups - 1 - group), ASIDE), 0)

    def pixels(c):
        return pl.ds(pl.multiple_of(c * PAIR, PAIR), PAIR)

    def loads(c):
        return (
            pltpu.make_async_copy(image_hbm.at[0, :, pixels(c)], image.at[c], load_sem.at[0, c]),
            pltpu.make_async_copy(mask_hbm.at[0, :, pixels(c)], mask.at[c], load_sem.at[1, c]),
        )

    def sent(c):
        return pltpu.make_async_remote_copy(
            masked.at[c], arrived.at[c], send_sem.at[c], recv_sem.at[c], device_id={"sec": sec - 1}, device_id_type=MESH
        )

    def sent_aside(c):
        slot = c - (chunks - aside)
        return pltpu.make_async_remote_copy(
            masked.at[c],
            relay.at[slot],
            send_sem.at[c],
            relay_recv.at[slot],
            device_id={"sec": sec - GROUP},
            device_id_type=MESH,
        )

    def passed_on(slot):
        c = chunks - passing + slot
        return pltpu.make_async_remote_copy(
            relay.at[slot],
            arrived.at[c],
            relay_send.at[slot],
            recv_sem.at[c],
            device_id={"sec": sec + GROUP - 1},
            device_id_type=MESH,
        )

    def pass_on(slot):
        pltpu.make_async_remote_copy(
            masked.at[slot],
            relay.at[slot],
            send_sem.at[slot],
            relay_recv.at[slot],
            device_id={"sec": sec + GROUP},
            device_id_type=MESH,
        ).wait_recv()
        passed_on(slot).start()

    mesh_loads = [
        pltpu.make_async_copy(both_hbm, both, mesh_sem.at[0]),
        pltpu.make_async_copy(narrow_hbm, narrow, mesh_sem.at[1]),
        pltpu.make_async_copy(anchor_hbm.at[0], anchor, mesh_sem.at[2]),
        pltpu.make_async_copy(fixed_hbm.at[0], fixed, mesh_sem.at[3]),
        pltpu.make_async_copy(prior_hbm.at[:, 0], prior, mesh_sem.at[4]),
    ]

    barrier = pltpu.get_barrier_semaphore()

    def greet(device):
        pl.semaphore_signal(barrier, inc=1, device_id=device, device_id_type=MESH)

    pl.when(has_prev)(lambda: greet({"sec": sec - 1}))
    pl.when(has_next)(lambda: greet({"sec": sec + 1}))
    pl.when(gives)(lambda: greet({"sec": sec - GROUP}))
    pl.when(passes)(lambda: greet({"sec": sec + GROUP}))
    pl.when(passes)(lambda: greet({"sec": sec + GROUP - 1}))
    pl.when(takes)(lambda: greet({"sec": sec - GROUP + 1}))
    pl.when(has_above)(lambda: greet({"blk": blk - 1}))
    pl.when(has_below)(lambda: greet({"blk": blk + 1}))
    across, over = moved(0, 0, 1), moved(0, 1, 0)
    along = [moved(dx, 0, 0) for dx in range(1, turns)]
    for other in [across, over] + along:
        greet({"blk": other})

    def start_loads(c, _):
        for copy in loads(c):
            copy.start()
        return 0

    lax.fori_loop(0, 1, start_loads, 0)
    for copy in mesh_loads:
        copy.start()
    lax.fori_loop(1, chunks, start_loads, 0)

    def hide(c):
        for copy in loads(c):
            copy.wait()
        masked[c] = image[c] * mask[c].astype(jnp.float32).astype(jnp.bfloat16)

    def hide_and_send(c, _):
        hide(c)
        straight = c < chunks - aside
        pl.when(has_prev & straight)(lambda: sent(c).start())
        pl.when(has_prev & jnp.logical_not(straight))(lambda: sent_aside(c).start())
        return 0

    hide(0)
    for copy in mesh_loads:
        copy.wait()
    free = 1.0 - fixed[...].astype(jnp.float32)
    own_pull = free * anchor[...]
    own = [own_pull, own_pull * prior[0], own_pull * prior[1]]

    def edge_copy(up):
        slot = 0 if up else 1
        return pltpu.make_async_remote_copy(
            edge_up if up else edge_down,
            from_below if up else from_above,
            edge_send.at[slot],
            edge_recv.at[slot],
            device_id={"blk": blk - 1 if up else blk + 1},
            device_id_type=MESH,
        )

    def flow_copy(up):
        slot = 0 if up else 1
        return pltpu.make_async_remote_copy(
            flow,
            flow_in.at[slot],
            flow_send.at[slot],
            flow_recv.at[slot],
            device_id={"blk": blk - 1 if up else blk + 1},
            device_id_type=MESH,
        )

    nodes = tiles * LANES

    def packed(first, count):
        flat = [part[at : at + SPAN] for part in own for at in range(first, first + count, SPAN)]
        flat = jnp.concatenate(flat, axis=1)
        width = flat.shape[1] // 4
        return jnp.concatenate([flat[:, k * width : (k + 1) * width] for k in range(4)], axis=0).astype(jnp.bfloat16)

    def unpacked(block):
        block = block.astype(jnp.float32)
        flat = jnp.concatenate([block[k * SPAN : (k + 1) * SPAN] for k in range(4)], axis=1)
        parts = [flat[:, k : k + nodes] for k in range(0, flat.shape[1], nodes)]
        each = len(parts) // 3
        return [parts[k * each : (k + 1) * each] for k in range(3)]

    edge_up[...] = packed(0, EDGE)
    edge_down[...] = packed(rows - SPAN, SPAN)
    greeted = has_prev, has_next, has_above, has_below, gives, passes, passes, takes
    pl.semaphore_wait(barrier, turns + 1 + functools.reduce(lambda p, q: p + q, [g.astype(jnp.int32) for g in greeted]))
    pl.when(has_above)(lambda: edge_copy(True).start())
    pl.when(has_below)(lambda: edge_copy(False).start())
    pl.when(has_prev)(lambda: sent(0).start())
    pl.semaphore_signal(round_sem.at[0], inc=1, device_id={"blk": across}, device_id_type=MESH)
    lax.fori_loop(1, 8, hide_and_send, 0)
    pl.semaphore_wait(round_sem.at[0], 1)
    pl.semaphore_signal(round_sem.at[1], inc=1, device_id={"blk": over}, device_id_type=MESH)
    lax.fori_loop(8, chunks, hide_and_send, 0)

    def own_spectrum(c, _):
        spectra[c] = spectrum(masked[c], narrow[...], both[...])
        return 0

    lax.fori_loop(0, chunks, own_spectrum, 0)
    pl.semaphore_wait(round_sem.at[1], 1)

    pull[...] = jnp.zeros_like(pull)
    base[...] = jnp.zeros_like(base)
    for g in range(tiles):
        at = slice(g * LANES, (g + 1) * LANES)
        pull[g, EDGE : EDGE + rows] = own[0][:, at]
        base[0, g, EDGE : EDGE + rows] = own[1][:, at]
        base[1, g, EDGE : EDGE + rows] = own[2][:, at]

    def take_edge(block, first, count):
        parts = unpacked(block)
        for n in range(0, count, SPAN):
            some = min(SPAN, count - n)
            to = slice(first + n, first + n + some)
            for g in range(tiles):
                at = slice(g * LANES, (g + 1) * LANES)
                pull[g, to] = parts[0][n // SPAN][:some, at]
                base[0, g, to] = parts[1][n // SPAN][:some, at]
                base[1, g, to] = parts[2][n // SPAN][:some, at]

    flow[...] = jnp.zeros_like(flow)
    listed[...] = jnp.zeros_like(listed)
    lane = lax.broadcasted_iota(jnp.int32, (8, LANES), 1)
    patch = lax.broadcasted_iota(jnp.int32, (nodes, LANES), 0) // (LANES // 4)
    for k in range(2):
        column = lax.broadcasted_iota(jnp.int32, (nodes, LANES), 1)
        pick[k] = jnp.where(column == patch + k * (LANES // 4), 1.0, 0.0).astype(jnp.bfloat16)
    tile_row = lax.broadcasted_iota(jnp.int32, (tiles, LANES), 0)
    quarter = lax.broadcasted_iota(jnp.int32, (tiles, LANES), 1) // (LANES // 4)

    def correlate(c, _):
        sent(c).wait_recv()
        pl.when(c < passing)(lambda: pass_on(c))
        other = spectrum(arrived[c], narrow[...], both[...])
        for k, value in enumerate(flows_of(spectra[c], other, narrow[...], both[...])):
            held = flow[k]
            for p in range(2):
                slot = lane == k * (LANES // 4) + 2 * c + p
                listed[...] = jnp.where(slot, value[p : p + 1], listed[...])
                spot = (tile_row == c // 2) & (quarter == 2 * (c % 2) + p)
                held = jnp.where(spot, value[p : p + 1], held)
            flow[k] = held
        return 0

    pause = chunks - 4
    known = pause * PAIR // SIZE // 4

    @pl.when(has_next)
    def _():
        lax.fori_loop(0, pause, correlate, 0)

    @pl.when(has_below)
    def _():
        edge_copy(True).wait_recv()
        take_edge(from_below[...], EDGE + rows, REACH)

    @pl.when(has_above)
    def _():
        edge_copy(False).wait_recv()
        take_edge(from_above[...], EDGE - SPAN, SPAN)

    loose = jnp.where(pull[...] > 0.0, SCALE, 0.0)
    link[...] = loose
    diag[...] = 4.0 * loose + SCALE * pull[...]

    part = lane // (LANES // 8)
    below = slice(EDGE + rows, EDGE + rows + EDGE)
    tail = slice(rows, rows + 2 * EDGE)

    def advance(value, step, tile=slice(None), at=slice(None), kept=0):
        return (diag[tile, at] - SCALE * SHIFTS[step]) * value[kept:] - link[tile, at] * neighbours(value)[kept:]

    def own_basis(first, last, kept):
        new, read = slice(first + kept, last), slice(first, last)
        for k in range(2):
            for g in range(first + kept, last):
                inner = slice(EDGE, EDGE + rows)
                basis[k, 0, g, :EDGE] = jnp.zeros((EDGE, LANES), jnp.float32)
                basis[k, 0, g, inner] = base[k, g, inner] + pull[g, inner] * flow[k, g : g + 1, :]
                basis[k, 0, g, below] = jnp.zeros((EDGE, LANES), jnp.float32)
            for step in range(ITERS):
                basis[k, step + 1, new] = advance(basis[k, step, read], step, new, slice(None), kept)
            for step in range(ITERS, REACH):
                value = basis[k, step, read, tail] if step == ITERS else reach[k, step - ITERS - 1, read]
                reach[k, step - ITERS, new] = advance(value, step, new, tail, kept)

    def own_sums(first, last):
        count = last - first
        over = slice(first, last)
        blocks = []
        gathered = jnp.zeros((REACH * EDGE, LANES), jnp.float32)
        for k in range(2):
            lines = []
            for i, j in PAIRS:
                product = basis[k, i, over] * basis[k, j, over]
                total = jnp.sum(product.reshape(count * (rows + 2 * EDGE) // 8, 8, LANES), axis=0)
                lines.append(jnp.sum(total, axis=0, keepdims=True))
            reached = [basis[k, step, over, below] for step in range(1, ITERS + 1)]
            reached += [reach[k, step, over, EDGE:] for step in range(REACH - ITERS)]
            strip, prior_lines = [], [jnp.zeros((1, LANES), jnp.float32)]
            for value in reached:
                weighted = pull[over, below] * value
                strip.append(jnp.concatenate([weighted[g] for g in range(count)], axis=1))
                prior_lines.append(2.0 * jnp.sum(jnp.sum(base[k, over, below] * value, axis=0), axis=0, keepdims=True))
            lines = [line + crossed(pair, prior_lines) for line, pair in zip(lines, PAIRS)]
            lines += [jnp.zeros((1, LANES), jnp.float32)] * (16 - len(lines))
            blocks += [jnp.concatenate(lines[n : n + 8], axis=0) for n in (0, 8)]
            left = jnp.concatenate(strip, axis=0)
            for _ in range(3):
                piece = left.astype(jnp.bfloat16)
                gathered = gathered + matmul(piece, pick[k, first * LANES : last * LANES])
                left = left - piece.astype(jnp.float32)
        gathered = jnp.sum(gathered.reshape(REACH, EDGE, LANES), axis=1)
        return blocks + [jnp.concatenate([jnp.zeros((1, LANES), jnp.float32), gathered], axis=0)]

    def folded(block):
        for lanes in (LANES // 2, LANES // 4, LANES // 8):
            block = block + pltpu.roll(block, lanes, 1)
        return block

    own_basis(0, known, 0)
    early = own_sums(0, known - 1)

    @pl.when(has_next)
    def _():
        lax.fori_loop(pause, chunks, correlate, 0)

    pl.when(has_above)(lambda: flow_copy(True).start())
    pl.when(has_below)(lambda: flow_copy(False).start())
    own_basis(known - 2, tiles, 1)
    blocks = [p + q for p, q in zip(early, own_sums(known - 1, tiles))]
    mine = 2.0 * blocks[4]
    for n in range(4):
        mine = jnp.where(part == 4 + n, folded(blocks[n]), mine)
    top = lax.broadcasted_iota(jnp.int32, (8, LANES), 0) == 0
    share[...] = jnp.where(top & (part < 4), listed[...], mine)

    def share_copy(n):
        return pltpu.make_async_remote_copy(
            share,
            shares.at[blk],
            share_send.at[n],
            share_recv.at[n],
            device_id={"blk": others[n]},
            device_id_type=MESH,
        )

    for n in range(bands - 1):
        share_copy(n).start()
    shares[blk] = share[...]

    @pl.when(has_below)
    def _():
        flow_copy(True).wait_recv()

    @pl.when(has_above)
    def _():
        flow_copy(False).wait_recv()

    @pl.when(jnp.logical_not(has_below))
    def _():
        flow_in[0] = jnp.zeros_like(flow)

    @pl.when(jnp.logical_not(has_above))
    def _():
        flow_in[1] = jnp.zeros_like(flow)

    for k in range(2):
        for g in range(tiles):
            for source, first_row, count in (
                (flow_in.at[1], 0, EDGE),
                (flow, EDGE, rows),
                (flow_in.at[0], EDGE + rows, EDGE),
            ):
                at = slice(first_row, first_row + count)
                whole[k, 0, g, at] = base[k, g, at] + pull[g, at] * source[k, g : g + 1, :]
        for step in range(ITERS - 1):
            whole[k, step + 1] = advance(whole[k, step], step)

    for n in range(bands - 1):
        share_copy(n).wait_recv()
    total = shares[bands - 1]
    for n in range(bands - 1):
        total = total + shares[n] * jnp.where(lane[:1] < LANES // 2, shares[n + 1, :1], 1.0)
    sums = [jnp.sum(jnp.where(part == 4 + n, total, 0.0), axis=1, keepdims=True) for n in range(4)]
    across_bands = [jnp.sum(jnp.where(part // 2 == k, total, 0.0), axis=1, keepdims=True) for k in range(2)]

    def by_component(pair, n):
        return jnp.where(lane[:1] < LANES // 2, pair[0][n : n + 1], pair[1][n : n + 1])

    none = jnp.zeros((1, LANES), jnp.float32)
    cross_lines = [none] + [by_component(across_bands, m) for m in range(1, REACH + 1)]
    gram = {}
    for n, pair in enumerate(PAIRS):
        own_line = by_component((sums[n // 8], sums[2 + n // 8]), n % 8)
        gram[pair] = own_line + crossed(pair, cross_lines)
    found = coefficients(gram)
    for k in range(2):
        weights = [value[:, k * LANES // 2 : k * LANES // 2 + 1] for value in found]
        for g in range(tiles):
            at = slice(EDGE, EDGE + rows)
            value = weights[0] * whole[k, 0, g, at]
            for step in range(1, ITERS):
                value = value + weights[step] * whole[k, step, g, at]
            out_ref[k, :, g * LANES : (g + 1) * LANES] = value

    for n in range(bands - 1):
        share_copy(n).wait_send()

    @pl.when(has_above)
    def _():
        edge_copy(True).wait_send()
        flow_copy(True).wait_send()

    @pl.when(has_below)
    def _():
        edge_copy(False).wait_send()
        flow_copy(False).wait_send()

    def drain(c, _):
        sent(c).wait_send()
        return 0

    @pl.when(has_prev)
    def _():
        lax.fori_loop(0, chunks, drain, 0)

    def drain_passed(slot, _):
        passed_on(slot).wait_send()
        return 0

    lax.fori_loop(0, passing, drain_passed, 0)


def per_device(sections, bands, image, tissue_mask, anchor, fixed_nodes, prior_shift):
    _, size, columns = image.shape
    _, rows, nodes = anchor.shape
    chunks = columns // PAIR
    tiles = nodes // LANES
    wide = 2 * EDGE + rows
    width = 3 * nodes // 4
    both, narrow = tables()
    operands = image, tissue_mask, anchor, fixed_nodes, prior_shift, jnp.asarray(both), jnp.asarray(narrow)
    operands = [pltpu.with_memory_space_constraint(operand, pltpu.HBM) for operand in operands]
    out = pl.pallas_call(
        functools.partial(kernel, sections, bands),
        out_shape=jax.ShapeDtypeStruct((2, rows, nodes), jnp.float32),
        in_specs=[pl.BlockSpec(memory_space=pl.ANY)] * 7,
        out_specs=pl.BlockSpec(memory_space=pltpu.VMEM),
        scratch_shapes=[
            pltpu.VMEM((chunks, size, PAIR), jnp.bfloat16),
            pltpu.VMEM((chunks, size, PAIR), jnp.int32),
            pltpu.VMEM((chunks, size, PAIR), jnp.bfloat16),
            pltpu.VMEM((chunks, size, PAIR), jnp.bfloat16),
            pltpu.VMEM((ASIDE, size, PAIR), jnp.bfloat16),
            pltpu.VMEM((chunks, PAIR, PAIR), jnp.bfloat16),
            pltpu.VMEM((PAIR, PAIR), jnp.bfloat16),
            pltpu.VMEM((PAIR, SIZE), jnp.bfloat16),
            pltpu.VMEM((rows, nodes), jnp.float32),
            pltpu.VMEM((rows, nodes), jnp.int32),
            pltpu.VMEM((2, rows, nodes), jnp.float32),
            pltpu.VMEM((4 * SPAN, 2 * width), jnp.bfloat16),
            pltpu.VMEM((4 * SPAN, width), jnp.bfloat16),
            pltpu.VMEM((4 * SPAN, 2 * width), jnp.bfloat16),
            pltpu.VMEM((4 * SPAN, width), jnp.bfloat16),
            pltpu.VMEM((tiles, wide, LANES), jnp.float32),
            pltpu.VMEM((tiles, wide, LANES), jnp.float32),
            pltpu.VMEM((tiles, wide, LANES), jnp.float32),
            pltpu.VMEM((2, tiles, wide, LANES), jnp.float32),
            pltpu.VMEM((2, tiles, LANES), jnp.float32),
            pltpu.VMEM((2, 2, tiles, LANES), jnp.float32),
            pltpu.VMEM((8, LANES), jnp.float32),
            pltpu.VMEM((2, nodes, LANES), jnp.bfloat16),
            pltpu.VMEM((2, ITERS + 1, tiles, wide, LANES), jnp.float32),
            pltpu.VMEM((2, REACH - ITERS, tiles, 2 * EDGE, LANES), jnp.float32),
            pltpu.VMEM((2, ITERS, tiles, wide, LANES), jnp.float32),
            pltpu.VMEM((8, LANES), jnp.float32),
            pltpu.VMEM((bands, 8, LANES), jnp.float32),
            pltpu.SemaphoreType.DMA((2, chunks)),
            pltpu.SemaphoreType.DMA((5,)),
            pltpu.SemaphoreType.DMA((chunks,)),
            pltpu.SemaphoreType.DMA((chunks,)),
            pltpu.SemaphoreType.DMA((2,)),
            pltpu.SemaphoreType.DMA((2,)),
            pltpu.SemaphoreType.DMA((2,)),
            pltpu.SemaphoreType.DMA((2,)),
            pltpu.SemaphoreType.DMA((bands - 1,)),
            pltpu.SemaphoreType.DMA((bands - 1,)),
            pltpu.SemaphoreType.REGULAR((2,)),
            pltpu.SemaphoreType.DMA((ASIDE,)),
            pltpu.SemaphoreType.DMA((ASIDE,)),
        ],
        compiler_params=pltpu.CompilerParams(
            collective_id=0, has_side_effects=True, vmem_limit_bytes=40 * 1024 * 1024
        ),
        cost_estimate=pl.CostEstimate(flops=2_400_000_000, bytes_accessed=4_000_000, transcendentals=0),
    )(*operands)
    return out[:, None]


def solution(mesh):
    sections, bands = mesh.shape["sec"], mesh.shape["blk"]
    return jax.shard_map(
        functools.partial(per_device, sections, bands),
        mesh=mesh,
        in_specs=(
            P("sec", "blk", None),
            P("sec", "blk", None),
            P("sec", "blk", None),
            P("sec", "blk", None),
            P(None, "sec", "blk", None),
        ),
        out_specs=P(None, "sec", "blk", None),
        check_vma=False,
    )
```

```python
import functools
import math

import jax
import jax.numpy as jnp
import ml_dtypes
import numpy as np
from jax import lax
from jax.experimental import pallas as pl
from jax.experimental.pallas import tpu as pltpu
from jax.sharding import PartitionSpec as P

MESH = pl.DeviceIdType.MESH
ITERS = 4
SIZE = 128
PAIR = 2 * SIZE
LANES = 128
EDGE = 8
SPAN = 4
REACH = 2 * ITERS - 1
GROUP = 4
ASIDE = 10
SHIFTS = (1.0, 4.0, 1.0, 4.0, 1.0, 4.0, 1.0)
SCALE = 0.25
PAIRS = tuple((i, j) for i in range(ITERS) for j in range(i, ITERS)) + tuple((i, ITERS) for i in range(ITERS))


def tables():
    j = np.arange(SIZE)
    angle = (j[:, None] * j[None, :] % SIZE).astype(np.float32) * np.float32(2.0 * math.pi / SIZE)
    cosine = np.cos(angle).astype(ml_dtypes.bfloat16)
    sine = np.sin(angle).astype(ml_dtypes.bfloat16)
    both = np.block([[cosine, -sine], [sine, cosine]])
    return both, np.concatenate([cosine, -sine], axis=0)


def matmul(left, right):
    return jnp.dot(left, right, preferred_element_type=jnp.float32)


def beside(pair):
    rows = [
        jnp.concatenate([pair[:SIZE, p * SIZE : (p + 1) * SIZE], pair[SIZE:, p * SIZE : (p + 1) * SIZE]], axis=1)
        for p in range(2)
    ]
    return jnp.concatenate(rows, axis=0)


def stacked(re, im):
    rows = [jnp.concatenate([part[:SIZE], part[SIZE:]], axis=1) for part in (re, im)]
    return jnp.concatenate(rows, axis=0)


def spectrum(block, narrow, both):
    half = matmul(narrow, block).astype(jnp.bfloat16)
    return matmul(beside(half), both).astype(jnp.bfloat16)


def offsets(shape, axis):
    index = lax.broadcasted_iota(jnp.int32, shape, axis)
    return (((index + SIZE // 2) % SIZE) - SIZE // 2).astype(jnp.float32)


def flows_of(own, other, narrow, both):
    a = own.astype(jnp.float32)
    b = other.astype(jnp.float32)
    a_re, a_im, b_re, b_im = a[:, :SIZE], a[:, SIZE:], b[:, :SIZE], b[:, SIZE:]
    cross_re = (a_re * b_re + a_im * b_im).astype(jnp.bfloat16)
    cross_im = (a_im * b_re - a_re * b_im).astype(jnp.bfloat16)
    back = matmul(both, stacked(cross_re, cross_im)).astype(jnp.bfloat16)
    corr = matmul(beside(back), narrow)
    weight = (corr * corr).reshape(2, SIZE, SIZE)
    whole = jnp.sum(weight, axis=1)
    tilted = jnp.sum(weight * offsets((1, SIZE, SIZE), 1), axis=1)
    unit = 2.0**-42
    total = jnp.sum(whole, axis=1, keepdims=True) * unit + 1e-6
    row_flow = jnp.sum(tilted, axis=1, keepdims=True) * unit / total
    col_flow = jnp.sum(whole * offsets((2, SIZE), 1), axis=1, keepdims=True) * unit / total
    return row_flow, col_flow


def neighbours(value):
    tiles, rows, _ = value.shape
    lane = lax.broadcasted_iota(jnp.int32, value.shape, 2)
    none = jnp.zeros((1, rows, LANES), value.dtype)
    right = pltpu.roll(value, 1, 2)
    right = jnp.where(lane == 0, jnp.concatenate([none, right[:-1]], axis=0), right)
    left = pltpu.roll(value, LANES - 1, 2)
    left = jnp.where(lane == LANES - 1, jnp.concatenate([left[1:], none], axis=0), left)
    return pltpu.roll(value, 1, 1) + pltpu.roll(value, rows - 1, 1) + right + left


def crossed(pair, powers):
    degree = sum(pair)
    if pair[0] % 2 and pair[1] % 2:
        return powers[degree] + SCALE * (SHIFTS[1] - SHIFTS[0]) * powers[degree - 1]
    return powers[degree]


def coefficients(gram):
    def inner(left, right):
        terms = [l * r * gram[min(i, j), max(i, j)] for i, l in enumerate(left) for j, r in enumerate(right)]
        return functools.reduce(lambda p, q: p + q, terms)

    zero = jnp.zeros_like(gram[0, 0])
    solution = [zero] * ITERS
    residual = [jnp.ones_like(zero)]
    direction = list(residual)
    norm_now = gram[0, 0]
    for step in range(ITERS):
        image = [SHIFTS[j] * direction[j] for j in range(step + 1)] + [zero]
        image = [image[j] + (direction[j - 1] / SCALE if j else 0.0) for j in range(step + 2)]
        curve = inner(direction, image)
        alpha = jnp.where(curve > 0.0, jnp.clip(norm_now / curve, 0.0, 10.1), 0.0)
        solution = [solution[j] + alpha * direction[j] if j <= step else solution[j] for j in range(ITERS)]
        if step == ITERS - 1:
            break
        residual = [r - alpha * i for r, i in zip(residual + [zero], image)]
        norm_next = jnp.maximum(inner(residual, residual), 0.0)
        beta = jnp.where(norm_now > 0.0, norm_next / norm_now, 0.0)
        direction = [r + beta * d for r, d in zip(residual, direction + [zero])]
        norm_now = norm_next
    return solution


def kernel(
    sections,
    bands,
    image_hbm,
    mask_hbm,
    anchor_hbm,
    fixed_hbm,
    prior_hbm,
    both_hbm,
    narrow_hbm,
    out_ref,
    image,
    mask,
    masked,
    arrived,
    relay,
    spectra,
    both,
    narrow,
    anchor,
    fixed,
    prior,
    edge_up,
    edge_down,
    from_below,
    from_above,
    via_up,
    via_down,
    pull,
    diag,
    link,
    base,
    flow,
    flow_in,
    listed,
    pick,
    basis,
    reach,
    whole,
    share,
    shares,
    load_sem,
    mesh_sem,
    send_sem,
    recv_sem,
    edge_send,
    edge_recv,
    flow_send,
    flow_recv,
    share_send,
    share_recv,
    round_sem,
    relay_recv,
    relay_send,
    via_recv,
    via_send,
):
    chunks = image.shape[0]
    tiles = pull.shape[0]
    rows = anchor.shape[0]
    sec = lax.axis_index("sec")
    blk = lax.axis_index("blk")
    has_above, has_below = blk > 0, blk < bands - 1
    has_prev, has_next = sec > 0, sec < sections - 1
    turns = bands // 4
    here = (blk // 4, lax.rem(blk // 2, 2), lax.rem(blk, 2))

    def moved(dx, dy, dc):
        return lax.rem(here[0] + dx, turns) * 4 + lax.rem(here[1] + dy, 2) * 2 + lax.rem(here[2] + dc, 2)

    order = [dx if dx <= turns // 2 else dx - turns for dx in range(turns)]
    steps = sorted(
        ((dx % turns, dy, dc) for dx in order for dy in range(2) for dc in range(2)),
        key=lambda step: (-step[1], -min(step[0], turns - step[0]), -step[2]),
    )
    others = [moved(*step) for step in steps if any(step)]

    group, groups = sec // GROUP, sections // GROUP
    place = lax.rem(sec, GROUP)
    gives = (place == 0) & (group > 0)
    passes = (place == 0) & (group < groups - 1)
    takes = (place == GROUP - 1) & (group < groups - 1)
    aside = jnp.where(gives, jnp.minimum(2 * (groups - group), ASIDE), 0)
    passing = jnp.where(passes, jnp.minimum(2 * (groups - 1 - group), ASIDE), 0)

    def pixels(c):
        return pl.ds(pl.multiple_of(c * PAIR, PAIR), PAIR)

    def loads(c):
        return (
            pltpu.make_async_copy(image_hbm.at[0, :, pixels(c)], image.at[c], load_sem.at[0, c]),
            pltpu.make_async_copy(mask_hbm.at[0, :, pixels(c)], mask.at[c], load_sem.at[1, c]),
        )

    def sent(c):
        return pltpu.make_async_remote_copy(
            masked.at[c], arrived.at[c], send_sem.at[c], recv_sem.at[c], device_id={"sec": sec - 1}, device_id_type=MESH
        )

    def sent_aside(c):
        slot = c - (chunks - aside)
        return pltpu.make_async_remote_copy(
            masked.at[c],
            relay.at[slot],
            send_sem.at[c],
            relay_recv.at[slot],
            device_id={"sec": sec - GROUP},
            device_id_type=MESH,
        )

    def passed_on(slot):
        c = chunks - passing + slot
        return pltpu.make_async_remote_copy(
            relay.at[slot],
            arrived.at[c],
            relay_send.at[slot],
            recv_sem.at[c],
            device_id={"sec": sec + GROUP - 1},
            device_id_type=MESH,
        )

    def pass_on(slot):
        pltpu.make_async_remote_copy(
            masked.at[slot],
            relay.at[slot],
            send_sem.at[slot],
            relay_recv.at[slot],
            device_id={"sec": sec + GROUP},
            device_id_type=MESH,
        ).wait_recv()
        passed_on(slot).start()

    mesh_loads = [
        pltpu.make_async_copy(both_hbm, both, mesh_sem.at[0]),
        pltpu.make_async_copy(narrow_hbm, narrow, mesh_sem.at[1]),
        pltpu.make_async_copy(anchor_hbm.at[0], anchor, mesh_sem.at[2]),
        pltpu.make_async_copy(fixed_hbm.at[0], fixed, mesh_sem.at[3]),
        pltpu.make_async_copy(prior_hbm.at[:, 0], prior, mesh_sem.at[4]),
    ]

    barrier = pltpu.get_barrier_semaphore()

    def greet(device):
        pl.semaphore_signal(barrier, inc=1, device_id=device, device_id_type=MESH)

    across, over, facing = moved(0, 0, 1), moved(0, 1, 0), moved(0, 1, 1)
    along = [moved(dx, 0, 0) for dx in range(1, turns)]
    greet({"blk": facing})
    greet({"blk": over})
    pl.when(has_prev)(lambda: greet({"sec": sec - 1}))
    pl.when(has_next)(lambda: greet({"sec": sec + 1}))
    pl.when(passes)(lambda: greet({"sec": sec + GROUP - 1}))
    pl.when(takes)(lambda: greet({"sec": sec - GROUP + 1}))
    pl.when(gives)(lambda: greet({"sec": sec - GROUP}))
    pl.when(passes)(lambda: greet({"sec": sec + GROUP}))
    for other in along + [across]:
        greet({"blk": other})

    def start_loads(c, _):
        for copy in loads(c):
            copy.start()
        return 0

    lax.fori_loop(0, 1, start_loads, 0)
    for copy in mesh_loads:
        copy.start()
    lax.fori_loop(1, chunks, start_loads, 0)

    def hide(c):
        for copy in loads(c):
            copy.wait()
        masked[c] = image[c] * mask[c].astype(jnp.float32).astype(jnp.bfloat16)

    def hide_and_send(c, _):
        hide(c)
        straight = c < chunks - aside
        pl.when(has_prev & straight)(lambda: sent(c).start())
        pl.when(has_prev & jnp.logical_not(straight))(lambda: sent_aside(c).start())
        return 0

    hide(0)
    for copy in mesh_loads:
        copy.wait()
    free = 1.0 - fixed[...].astype(jnp.float32)
    own_pull = free * anchor[...]
    own = [own_pull, own_pull * prior[0], own_pull * prior[1]]

    def edge_copy(up):
        slot = 0 if up else 1
        return pltpu.make_async_remote_copy(
            edge_up if up else edge_down,
            from_below if up else from_above,
            edge_send.at[slot],
            edge_recv.at[slot],
            device_id={"blk": blk - 1 if up else blk + 1},
            device_id_type=MESH,
        )

    def edge_via(up):
        slot = 0 if up else 1
        return pltpu.make_async_remote_copy(
            edge_up if up else edge_down,
            via_up if up else via_down,
            edge_send.at[slot],
            via_recv.at[slot],
            device_id={"blk": facing},
            device_id_type=MESH,
        )

    def edge_onward(up):
        slot = 0 if up else 1
        return pltpu.make_async_remote_copy(
            via_up if up else via_down,
            from_below if up else from_above,
            via_send.at[slot],
            edge_recv.at[slot],
            device_id={"blk": blk - 4 if up else blk + 4},
            device_id_type=MESH,
        )

    def flow_copy(up):
        slot = 0 if up else 1
        return pltpu.make_async_remote_copy(
            flow,
            flow_in.at[slot],
            flow_send.at[slot],
            flow_recv.at[slot],
            device_id={"blk": blk - 1 if up else blk + 1},
            device_id_type=MESH,
        )

    nodes = tiles * LANES

    def packed(first, count):
        flat = [part[at : at + SPAN] for part in own for at in range(first, first + count, SPAN)]
        flat = jnp.concatenate(flat, axis=1)
        width = flat.shape[1] // 4
        return jnp.concatenate([flat[:, k * width : (k + 1) * width] for k in range(4)], axis=0).astype(jnp.bfloat16)

    def unpacked(block):
        block = block.astype(jnp.float32)
        flat = jnp.concatenate([block[k * SPAN : (k + 1) * SPAN] for k in range(4)], axis=1)
        parts = [flat[:, k : k + nodes] for k in range(0, flat.shape[1], nodes)]
        each = len(parts) // 3
        return [parts[k * each : (k + 1) * each] for k in range(3)]

    edge_up[...] = packed(0, EDGE)
    edge_down[...] = packed(rows - SPAN, SPAN)
    greeted = has_prev, has_next, gives, passes, passes, takes
    pl.semaphore_wait(barrier, turns + 2 + functools.reduce(lambda p, q: p + q, [g.astype(jnp.int32) for g in greeted]))
    lowest = (here[1] == 0) & (here[2] == 0)
    highest = (here[1] == 1) & (here[2] == 1)
    pl.when(has_above & jnp.logical_not(lowest))(lambda: edge_copy(True).start())
    pl.when(has_below & jnp.logical_not(highest))(lambda: edge_copy(False).start())
    pl.when(has_above & lowest)(lambda: edge_via(True).start())
    pl.when(has_below & highest)(lambda: edge_via(False).start())
    pl.when(has_prev)(lambda: sent(0).start())
    pl.semaphore_signal(round_sem.at[0], inc=1, device_id={"blk": across}, device_id_type=MESH)
    lax.fori_loop(1, 8, hide_and_send, 0)
    pl.semaphore_wait(round_sem.at[0], 1)
    pl.semaphore_signal(round_sem.at[1], inc=1, device_id={"blk": over}, device_id_type=MESH)
    lax.fori_loop(8, chunks, hide_and_send, 0)

    def own_spectrum(c, _):
        spectra[c] = spectrum(masked[c], narrow[...], both[...])
        return 0

    lax.fori_loop(0, chunks, own_spectrum, 0)
    onward_up = highest & (here[0] > 0)
    onward_down = lowest & (here[0] < turns - 1)

    @pl.when(onward_up)
    def _():
        edge_via(True).wait_recv()
        edge_onward(True).start()

    @pl.when(onward_down)
    def _():
        edge_via(False).wait_recv()
        edge_onward(False).start()

    pl.semaphore_wait(round_sem.at[1], 1)

    pull[...] = jnp.zeros_like(pull)
    base[...] = jnp.zeros_like(base)
    for g in range(tiles):
        at = slice(g * LANES, (g + 1) * LANES)
        pull[g, EDGE : EDGE + rows] = own[0][:, at]
        base[0, g, EDGE : EDGE + rows] = own[1][:, at]
        base[1, g, EDGE : EDGE + rows] = own[2][:, at]

    def take_edge(block, first, count):
        parts = unpacked(block)
        for n in range(0, count, SPAN):
            some = min(SPAN, count - n)
            to = slice(first + n, first + n + some)
            for g in range(tiles):
                at = slice(g * LANES, (g + 1) * LANES)
                pull[g, to] = parts[0][n // SPAN][:some, at]
                base[0, g, to] = parts[1][n // SPAN][:some, at]
                base[1, g, to] = parts[2][n // SPAN][:some, at]

    flow[...] = jnp.zeros_like(flow)
    listed[...] = jnp.zeros_like(listed)
    lane = lax.broadcasted_iota(jnp.int32, (8, LANES), 1)
    patch = lax.broadcasted_iota(jnp.int32, (nodes, LANES), 0) // (LANES // 4)
    for k in range(2):
        column = lax.broadcasted_iota(jnp.int32, (nodes, LANES), 1)
        pick[k] = jnp.where(column == patch + k * (LANES // 4), 1.0, 0.0).astype(jnp.bfloat16)
    tile_row = lax.broadcasted_iota(jnp.int32, (tiles, LANES), 0)
    quarter = lax.broadcasted_iota(jnp.int32, (tiles, LANES), 1) // (LANES // 4)

    def correlate(c, _):
        sent(c).wait_recv()
        pl.when(c < passing)(lambda: pass_on(c))
        other = spectrum(arrived[c], narrow[...], both[...])
        for k, value in enumerate(flows_of(spectra[c], other, narrow[...], both[...])):
            held = flow[k]
            for p in range(2):
                slot = lane == k * (LANES // 4) + 2 * c + p
                listed[...] = jnp.where(slot, value[p : p + 1], listed[...])
                spot = (tile_row == c // 2) & (quarter == 2 * (c % 2) + p)
                held = jnp.where(spot, value[p : p + 1], held)
            flow[k] = held
        return 0

    pause = chunks - 4
    known = pause * PAIR // SIZE // 4

    @pl.when(has_next)
    def _():
        lax.fori_loop(0, pause, correlate, 0)

    @pl.when(has_below)
    def _():
        edge_copy(True).wait_recv()
        take_edge(from_below[...], EDGE + rows, REACH)

    @pl.when(has_above)
    def _():
        edge_copy(False).wait_recv()
        take_edge(from_above[...], EDGE - SPAN, SPAN)

    loose = jnp.where(pull[...] > 0.0, SCALE, 0.0)
    link[...] = loose
    diag[...] = 4.0 * loose + SCALE * pull[...]

    part = lane // (LANES // 8)
    below = slice(EDGE + rows, EDGE + rows + EDGE)
    tail = slice(rows, rows + 2 * EDGE)

    def advance(value, step, tile=slice(None), at=slice(None), kept=0):
        return (diag[tile, at] - SCALE * SHIFTS[step]) * value[kept:] - link[tile, at] * neighbours(value)[kept:]

    def own_basis(first, last, kept):
        new, read = slice(first + kept, last), slice(first, last)
        for k in range(2):
            for g in range(first + kept, last):
                inner = slice(EDGE, EDGE + rows)
                basis[k, 0, g, :EDGE] = jnp.zeros((EDGE, LANES), jnp.float32)
                basis[k, 0, g, inner] = base[k, g, inner] + pull[g, inner] * flow[k, g : g + 1, :]
                basis[k, 0, g, below] = jnp.zeros((EDGE, LANES), jnp.float32)
            for step in range(ITERS):
                basis[k, step + 1, new] = advance(basis[k, step, read], step, new, slice(None), kept)
            for step in range(ITERS, REACH):
                value = basis[k, step, read, tail] if step == ITERS else reach[k, step - ITERS - 1, read]
                reach[k, step - ITERS, new] = advance(value, step, new, tail, kept)

    def own_sums(first, last):
        count = last - first
        over = slice(first, last)
        blocks = []
        gathered = jnp.zeros((REACH * EDGE, LANES), jnp.float32)
        for k in range(2):
            lines = []
            for i, j in PAIRS:
                product = basis[k, i, over] * basis[k, j, over]
                total = jnp.sum(product.reshape(count * (rows + 2 * EDGE) // 8, 8, LANES), axis=0)
                lines.append(jnp.sum(total, axis=0, keepdims=True))
            reached = [basis[k, step, over, below] for step in range(1, ITERS + 1)]
            reached += [reach[k, step, over, EDGE:] for step in range(REACH - ITERS)]
            strip, prior_lines = [], [jnp.zeros((1, LANES), jnp.float32)]
            for value in reached:
                weighted = pull[over, below] * value
                strip.append(jnp.concatenate([weighted[g] for g in range(count)], axis=1))
                prior_lines.append(2.0 * jnp.sum(jnp.sum(base[k, over, below] * value, axis=0), axis=0, keepdims=True))
            lines = [line + crossed(pair, prior_lines) for line, pair in zip(lines, PAIRS)]
            lines += [jnp.zeros((1, LANES), jnp.float32)] * (16 - len(lines))
            blocks += [jnp.concatenate(lines[n : n + 8], axis=0) for n in (0, 8)]
            left = jnp.concatenate(strip, axis=0)
            for _ in range(3):
                piece = left.astype(jnp.bfloat16)
                gathered = gathered + matmul(piece, pick[k, first * LANES : last * LANES])
                left = left - piece.astype(jnp.float32)
        gathered = jnp.sum(gathered.reshape(REACH, EDGE, LANES), axis=1)
        return blocks + [jnp.concatenate([jnp.zeros((1, LANES), jnp.float32), gathered], axis=0)]

    def folded(block):
        for lanes in (LANES // 2, LANES // 4, LANES // 8):
            block = block + pltpu.roll(block, lanes, 1)
        return block

    own_basis(0, known, 0)
    early = own_sums(0, known - 1)

    @pl.when(has_next)
    def _():
        lax.fori_loop(pause, chunks, correlate, 0)

    pl.when(has_above)(lambda: flow_copy(True).start())
    pl.when(has_below)(lambda: flow_copy(False).start())
    own_basis(known - 2, tiles, 1)
    blocks = [p + q for p, q in zip(early, own_sums(known - 1, tiles))]
    mine = 2.0 * blocks[4]
    for n in range(4):
        mine = jnp.where(part == 4 + n, folded(blocks[n]), mine)
    top = lax.broadcasted_iota(jnp.int32, (8, LANES), 0) == 0
    share[...] = jnp.where(top & (part < 4), listed[...], mine)

    def share_copy(n):
        return pltpu.make_async_remote_copy(
            share,
            shares.at[blk],
            share_send.at[n],
            share_recv.at[n],
            device_id={"blk": others[n]},
            device_id_type=MESH,
        )

    for n in range(bands - 1):
        share_copy(n).start()
    shares[blk] = share[...]

    def drain(c, _):
        sent(c).wait_send()
        return 0

    def drain_passed(slot, _):
        passed_on(slot).wait_send()
        return 0

    @pl.when(has_prev)
    def _():
        lax.fori_loop(0, chunks, drain, 0)

    lax.fori_loop(0, passing, drain_passed, 0)
    pl.when(onward_up)(lambda: edge_onward(True).wait_send())
    pl.when(onward_down)(lambda: edge_onward(False).wait_send())

    @pl.when(has_above)
    def _():
        edge_copy(True).wait_send()

    @pl.when(has_below)
    def _():
        edge_copy(False).wait_send()

    @pl.when(has_below)
    def _():
        flow_copy(True).wait_recv()

    @pl.when(has_above)
    def _():
        flow_copy(False).wait_recv()

    @pl.when(jnp.logical_not(has_below))
    def _():
        flow_in[0] = jnp.zeros_like(flow)

    @pl.when(jnp.logical_not(has_above))
    def _():
        flow_in[1] = jnp.zeros_like(flow)

    for k in range(2):
        for g in range(tiles):
            for source, first_row, count in (
                (flow_in.at[1], 0, EDGE),
                (flow, EDGE, rows),
                (flow_in.at[0], EDGE + rows, EDGE),
            ):
                at = slice(first_row, first_row + count)
                whole[k, 0, g, at] = base[k, g, at] + pull[g, at] * source[k, g : g + 1, :]
        for step in range(ITERS - 1):
            whole[k, step + 1] = advance(whole[k, step], step)

    @pl.when(has_above)
    def _():
        flow_copy(True).wait_send()

    @pl.when(has_below)
    def _():
        flow_copy(False).wait_send()

    for n in reversed(range(bands - 1)):
        share_copy(n).wait_recv()
    total = shares[bands - 1]
    for n in range(bands - 1):
        total = total + shares[n] * jnp.where(lane[:1] < LANES // 2, shares[n + 1, :1], 1.0)
    sums = [jnp.sum(jnp.where(part == 4 + n, total, 0.0), axis=1, keepdims=True) for n in range(4)]
    across_bands = [jnp.sum(jnp.where(part // 2 == k, total, 0.0), axis=1, keepdims=True) for k in range(2)]

    def by_component(pair, n):
        return jnp.where(lane[:1] < LANES // 2, pair[0][n : n + 1], pair[1][n : n + 1])

    none = jnp.zeros((1, LANES), jnp.float32)
    cross_lines = [none] + [by_component(across_bands, m) for m in range(1, REACH + 1)]
    gram = {}
    for n, pair in enumerate(PAIRS):
        own_line = by_component((sums[n // 8], sums[2 + n // 8]), n % 8)
        gram[pair] = own_line + crossed(pair, cross_lines)
    found = coefficients(gram)
    for k in range(2):
        weights = [value[:, k * LANES // 2 : k * LANES // 2 + 1] for value in found]
        for g in range(tiles):
            at = slice(EDGE, EDGE + rows)
            value = weights[0] * whole[k, 0, g, at]
            for step in range(1, ITERS):
                value = value + weights[step] * whole[k, step, g, at]
            out_ref[k, :, g * LANES : (g + 1) * LANES] = value

    for n in range(bands - 1):
        share_copy(n).wait_send()


def per_device(sections, bands, image, tissue_mask, anchor, fixed_nodes, prior_shift):
    _, size, columns = image.shape
    _, rows, nodes = anchor.shape
    chunks = columns // PAIR
    tiles = nodes // LANES
    wide = 2 * EDGE + rows
    width = 3 * nodes // 4
    both, narrow = tables()
    operands = image, tissue_mask, anchor, fixed_nodes, prior_shift, jnp.asarray(both), jnp.asarray(narrow)
    operands = [pltpu.with_memory_space_constraint(operand, pltpu.HBM) for operand in operands]
    out = pl.pallas_call(
        functools.partial(kernel, sections, bands),
        out_shape=jax.ShapeDtypeStruct((2, rows, nodes), jnp.float32),
        in_specs=[pl.BlockSpec(memory_space=pl.ANY)] * 7,
        out_specs=pl.BlockSpec(memory_space=pltpu.VMEM),
        scratch_shapes=[
            pltpu.VMEM((chunks, size, PAIR), jnp.bfloat16),
            pltpu.VMEM((chunks, size, PAIR), jnp.int32),
            pltpu.VMEM((chunks, size, PAIR), jnp.bfloat16),
            pltpu.VMEM((chunks, size, PAIR), jnp.bfloat16),
            pltpu.VMEM((ASIDE, size, PAIR), jnp.bfloat16),
            pltpu.VMEM((chunks, PAIR, PAIR), jnp.bfloat16),
            pltpu.VMEM((PAIR, PAIR), jnp.bfloat16),
            pltpu.VMEM((PAIR, SIZE), jnp.bfloat16),
            pltpu.VMEM((rows, nodes), jnp.float32),
            pltpu.VMEM((rows, nodes), jnp.int32),
            pltpu.VMEM((2, rows, nodes), jnp.float32),
            pltpu.VMEM((4 * SPAN, 2 * width), jnp.bfloat16),
            pltpu.VMEM((4 * SPAN, width), jnp.bfloat16),
            pltpu.VMEM((4 * SPAN, 2 * width), jnp.bfloat16),
            pltpu.VMEM((4 * SPAN, width), jnp.bfloat16),
            pltpu.VMEM((4 * SPAN, 2 * width), jnp.bfloat16),
            pltpu.VMEM((4 * SPAN, width), jnp.bfloat16),
            pltpu.VMEM((tiles, wide, LANES), jnp.float32),
            pltpu.VMEM((tiles, wide, LANES), jnp.float32),
            pltpu.VMEM((tiles, wide, LANES), jnp.float32),
            pltpu.VMEM((2, tiles, wide, LANES), jnp.float32),
            pltpu.VMEM((2, tiles, LANES), jnp.float32),
            pltpu.VMEM((2, 2, tiles, LANES), jnp.float32),
            pltpu.VMEM((8, LANES), jnp.float32),
            pltpu.VMEM((2, nodes, LANES), jnp.bfloat16),
            pltpu.VMEM((2, ITERS + 1, tiles, wide, LANES), jnp.float32),
            pltpu.VMEM((2, REACH - ITERS, tiles, 2 * EDGE, LANES), jnp.float32),
            pltpu.VMEM((2, ITERS, tiles, wide, LANES), jnp.float32),
            pltpu.VMEM((8, LANES), jnp.float32),
            pltpu.VMEM((bands, 8, LANES), jnp.float32),
            pltpu.SemaphoreType.DMA((2, chunks)),
            pltpu.SemaphoreType.DMA((5,)),
            pltpu.SemaphoreType.DMA((chunks,)),
            pltpu.SemaphoreType.DMA((chunks,)),
            pltpu.SemaphoreType.DMA((2,)),
            pltpu.SemaphoreType.DMA((2,)),
            pltpu.SemaphoreType.DMA((2,)),
            pltpu.SemaphoreType.DMA((2,)),
            pltpu.SemaphoreType.DMA((bands - 1,)),
            pltpu.SemaphoreType.DMA((bands - 1,)),
            pltpu.SemaphoreType.REGULAR((2,)),
            pltpu.SemaphoreType.DMA((ASIDE,)),
            pltpu.SemaphoreType.DMA((ASIDE,)),
            pltpu.SemaphoreType.DMA((2,)),
            pltpu.SemaphoreType.DMA((2,)),
        ],
        compiler_params=pltpu.CompilerParams(
            collective_id=0, has_side_effects=True, vmem_limit_bytes=40 * 1024 * 1024
        ),
        cost_estimate=pl.CostEstimate(flops=2_400_000_000, bytes_accessed=4_000_000, transcendentals=0),
    )(*operands)
    return out[:, None]


def solution(mesh):
    sections, bands = mesh.shape["sec"], mesh.shape["blk"]
    return jax.shard_map(
        functools.partial(per_device, sections, bands),
        mesh=mesh,
        in_specs=(
            P("sec", "blk", None),
            P("sec", "blk", None),
            P("sec", "blk", None),
            P("sec", "blk", None),
            P(None, "sec", "blk", None),
        ),
        out_specs=P(None, "sec", "blk", None),
        check_vma=False,
    )
```

```python
import functools
import math

import jax
import jax.numpy as jnp
import ml_dtypes
import numpy as np
from jax import lax
from jax.experimental import pallas as pl
from jax.experimental.pallas import tpu as pltpu
from jax.sharding import PartitionSpec as P

MESH = pl.DeviceIdType.MESH
ITERS = 4
SIZE = 128
PAIR = 2 * SIZE
LANES = 128
EDGE = 8
SPAN = 4
REACH = 2 * ITERS - 1
GROUP = 4
ASIDE = 8
SHIFTS = (1.0, 4.0, 1.0, 4.0, 1.0, 4.0, 1.0)
SCALE = 0.25
PAIRS = tuple((i, j) for i in range(ITERS) for j in range(i, ITERS)) + tuple((i, ITERS) for i in range(ITERS))


def tables():
    j = np.arange(SIZE)
    angle = (j[:, None] * j[None, :] % SIZE).astype(np.float32) * np.float32(2.0 * math.pi / SIZE)
    cosine = np.cos(angle).astype(ml_dtypes.bfloat16)
    sine = np.sin(angle).astype(ml_dtypes.bfloat16)
    both = np.block([[cosine, -sine], [sine, cosine]])
    return both, np.concatenate([cosine, -sine], axis=0)


def matmul(left, right):
    return jnp.dot(left, right, preferred_element_type=jnp.float32)


def beside(pair):
    rows = [
        jnp.concatenate([pair[:SIZE, p * SIZE : (p + 1) * SIZE], pair[SIZE:, p * SIZE : (p + 1) * SIZE]], axis=1)
        for p in range(2)
    ]
    return jnp.concatenate(rows, axis=0)


def stacked(re, im):
    rows = [jnp.concatenate([part[:SIZE], part[SIZE:]], axis=1) for part in (re, im)]
    return jnp.concatenate(rows, axis=0)


def spectrum(block, narrow, both):
    half = matmul(narrow, block).astype(jnp.bfloat16)
    return matmul(beside(half), both).astype(jnp.bfloat16)


def offsets(shape, axis):
    index = lax.broadcasted_iota(jnp.int32, shape, axis)
    return (((index + SIZE // 2) % SIZE) - SIZE // 2).astype(jnp.float32)


def flows_of(own, other, narrow, both):
    a = own.astype(jnp.float32)
    b = other.astype(jnp.float32)
    a_re, a_im, b_re, b_im = a[:, :SIZE], a[:, SIZE:], b[:, :SIZE], b[:, SIZE:]
    cross_re = (a_re * b_re + a_im * b_im).astype(jnp.bfloat16)
    cross_im = (a_im * b_re - a_re * b_im).astype(jnp.bfloat16)
    back = matmul(both, stacked(cross_re, cross_im)).astype(jnp.bfloat16)
    corr = matmul(beside(back), narrow)
    weight = (corr * corr).reshape(2, SIZE, SIZE)
    whole = jnp.sum(weight, axis=1)
    tilted = jnp.sum(weight * offsets((1, SIZE, SIZE), 1), axis=1)
    unit = 2.0**-42
    total = jnp.sum(whole, axis=1, keepdims=True) * unit + 1e-6
    row_flow = jnp.sum(tilted, axis=1, keepdims=True) * unit / total
    col_flow = jnp.sum(whole * offsets((2, SIZE), 1), axis=1, keepdims=True) * unit / total
    return row_flow, col_flow


def neighbours(value):
    tiles, rows, _ = value.shape
    lane = lax.broadcasted_iota(jnp.int32, value.shape, 2)
    none = jnp.zeros((1, rows, LANES), value.dtype)
    right = pltpu.roll(value, 1, 2)
    right = jnp.where(lane == 0, jnp.concatenate([none, right[:-1]], axis=0), right)
    left = pltpu.roll(value, LANES - 1, 2)
    left = jnp.where(lane == LANES - 1, jnp.concatenate([left[1:], none], axis=0), left)
    return pltpu.roll(value, 1, 1) + pltpu.roll(value, rows - 1, 1) + right + left


def crossed(pair, powers):
    degree = sum(pair)
    if pair[0] % 2 and pair[1] % 2:
        return powers[degree] + SCALE * (SHIFTS[1] - SHIFTS[0]) * powers[degree - 1]
    return powers[degree]


def coefficients(gram):
    def inner(left, right):
        terms = [l * r * gram[min(i, j), max(i, j)] for i, l in enumerate(left) for j, r in enumerate(right)]
        return functools.reduce(lambda p, q: p + q, terms)

    zero = jnp.zeros_like(gram[0, 0])
    solution = [zero] * ITERS
    residual = [jnp.ones_like(zero)]
    direction = list(residual)
    norm_now = gram[0, 0]
    for step in range(ITERS):
        image = [SHIFTS[j] * direction[j] for j in range(step + 1)] + [zero]
        image = [image[j] + (direction[j - 1] / SCALE if j else 0.0) for j in range(step + 2)]
        curve = inner(direction, image)
        alpha = jnp.where(curve > 0.0, jnp.clip(norm_now / curve, 0.0, 10.1), 0.0)
        solution = [solution[j] + alpha * direction[j] if j <= step else solution[j] for j in range(ITERS)]
        if step == ITERS - 1:
            break
        residual = [r - alpha * i for r, i in zip(residual + [zero], image)]
        norm_next = jnp.maximum(inner(residual, residual), 0.0)
        beta = jnp.where(norm_now > 0.0, norm_next / norm_now, 0.0)
        direction = [r + beta * d for r, d in zip(residual, direction + [zero])]
        norm_now = norm_next
    return solution


def kernel(
    sections,
    bands,
    image_hbm,
    mask_hbm,
    anchor_hbm,
    fixed_hbm,
    prior_hbm,
    both_hbm,
    narrow_hbm,
    out_ref,
    image,
    mask,
    masked,
    arrived,
    relay,
    spectra,
    both,
    narrow,
    anchor,
    fixed,
    prior,
    edge_up,
    edge_down,
    from_below,
    from_above,
    via_up,
    via_down,
    pull,
    diag,
    link,
    base,
    flow,
    flow_in,
    listed,
    pick,
    basis,
    reach,
    whole,
    share,
    shares,
    load_sem,
    mesh_sem,
    send_sem,
    recv_sem,
    edge_send,
    edge_recv,
    flow_send,
    flow_recv,
    share_send,
    share_recv,
    round_sem,
    relay_recv,
    relay_send,
    via_recv,
    via_send,
):
    chunks = image.shape[0]
    tiles = pull.shape[0]
    rows = anchor.shape[0]
    sec = lax.axis_index("sec")
    blk = lax.axis_index("blk")
    has_above, has_below = blk > 0, blk < bands - 1
    has_prev, has_next = sec > 0, sec < sections - 1
    turns = bands // 4
    here = (blk // 4, lax.rem(blk // 2, 2), lax.rem(blk, 2))

    def moved(dx, dy, dc):
        return lax.rem(here[0] + dx, turns) * 4 + lax.rem(here[1] + dy, 2) * 2 + lax.rem(here[2] + dc, 2)

    order = [dx if dx <= turns // 2 else dx - turns for dx in range(turns)]
    steps = sorted(
        ((dx % turns, dy, dc) for dx in order for dy in range(2) for dc in range(2)),
        key=lambda step: (-step[1], -min(step[0], turns - step[0]), -step[2]),
    )
    others = [moved(*step) for step in steps if any(step)]

    group, groups = sec // GROUP, sections // GROUP
    place = lax.rem(sec, GROUP)
    gives = (place == 0) & (group > 0)
    passes = (place == 0) & (group < groups - 1)
    takes = (place == GROUP - 1) & (group < groups - 1)
    aside = jnp.where(gives, jnp.minimum(2 * (groups - group), ASIDE), 0)
    passing = jnp.where(passes, jnp.minimum(2 * (groups - 1 - group), ASIDE), 0)

    def pixels(c):
        return pl.ds(pl.multiple_of(c * PAIR, PAIR), PAIR)

    def loads(c):
        return (
            pltpu.make_async_copy(image_hbm.at[0, :, pixels(c)], image.at[c], load_sem.at[0, c]),
            pltpu.make_async_copy(mask_hbm.at[0, :, pixels(c)], mask.at[c], load_sem.at[1, c]),
        )

    def sent(c):
        return pltpu.make_async_remote_copy(
            masked.at[c], arrived.at[c], send_sem.at[c], recv_sem.at[c], device_id={"sec": sec - 1}, device_id_type=MESH
        )

    def sent_aside(c):
        slot = c - (chunks - aside)
        return pltpu.make_async_remote_copy(
            masked.at[c],
            relay.at[slot],
            send_sem.at[c],
            relay_recv.at[slot],
            device_id={"sec": sec - GROUP},
            device_id_type=MESH,
        )

    def passed_on(slot):
        c = chunks - passing + slot
        return pltpu.make_async_remote_copy(
            relay.at[slot],
            arrived.at[c],
            relay_send.at[slot],
            recv_sem.at[c],
            device_id={"sec": sec + GROUP - 1},
            device_id_type=MESH,
        )

    def pass_on(slot):
        pltpu.make_async_remote_copy(
            masked.at[slot],
            relay.at[slot],
            send_sem.at[slot],
            relay_recv.at[slot],
            device_id={"sec": sec + GROUP},
            device_id_type=MESH,
        ).wait_recv()
        passed_on(slot).start()

    mesh_loads = [
        pltpu.make_async_copy(both_hbm, both, mesh_sem.at[0]),
        pltpu.make_async_copy(narrow_hbm, narrow, mesh_sem.at[1]),
        pltpu.make_async_copy(anchor_hbm.at[0], anchor, mesh_sem.at[2]),
        pltpu.make_async_copy(fixed_hbm.at[0], fixed, mesh_sem.at[3]),
        pltpu.make_async_copy(prior_hbm.at[:, 0], prior, mesh_sem.at[4]),
    ]

    barrier = pltpu.get_barrier_semaphore()

    def greet(device):
        pl.semaphore_signal(barrier, inc=1, device_id=device, device_id_type=MESH)

    across, over, facing = moved(0, 0, 1), moved(0, 1, 0), moved(0, 1, 1)
    along = [moved(dx, 0, 0) for dx in range(1, turns)]
    greet({"blk": facing})
    greet({"blk": over})
    pl.when(has_prev)(lambda: greet({"sec": sec - 1}))
    pl.when(has_next)(lambda: greet({"sec": sec + 1}))
    pl.when(passes)(lambda: greet({"sec": sec + GROUP - 1}))
    pl.when(takes)(lambda: greet({"sec": sec - GROUP + 1}))
    pl.when(gives)(lambda: greet({"sec": sec - GROUP}))
    pl.when(passes)(lambda: greet({"sec": sec + GROUP}))
    for other in along + [across]:
        greet({"blk": other})

    def start_loads(c, _):
        for copy in loads(c):
            copy.start()
        return 0

    lax.fori_loop(0, 1, start_loads, 0)
    for copy in mesh_loads:
        copy.start()
    lax.fori_loop(1, chunks, start_loads, 0)

    def hide(c):
        for copy in loads(c):
            copy.wait()
        masked[c] = image[c] * mask[c].astype(jnp.float32).astype(jnp.bfloat16)

    def hide_and_send(c, _):
        hide(c)
        straight = c < chunks - aside
        pl.when(has_prev & straight)(lambda: sent(c).start())
        pl.when(has_prev & jnp.logical_not(straight))(lambda: sent_aside(c).start())
        return 0

    hide(0)
    for copy in mesh_loads:
        copy.wait()
    free = 1.0 - fixed[...].astype(jnp.float32)
    own_pull = free * anchor[...]
    own = [own_pull, own_pull * prior[0], own_pull * prior[1]]

    def edge_copy(up):
        slot = 0 if up else 1
        return pltpu.make_async_remote_copy(
            edge_up if up else edge_down,
            from_below if up else from_above,
            edge_send.at[slot],
            edge_recv.at[slot],
            device_id={"blk": blk - 1 if up else blk + 1},
            device_id_type=MESH,
        )

    def edge_via(up):
        slot = 0 if up else 1
        return pltpu.make_async_remote_copy(
            edge_up if up else edge_down,
            via_up if up else via_down,
            edge_send.at[slot],
            via_recv.at[slot],
            device_id={"blk": facing},
            device_id_type=MESH,
        )

    def edge_onward(up):
        slot = 0 if up else 1
        return pltpu.make_async_remote_copy(
            via_up if up else via_down,
            from_below if up else from_above,
            via_send.at[slot],
            edge_recv.at[slot],
            device_id={"blk": blk - 4 if up else blk + 4},
            device_id_type=MESH,
        )

    def flow_copy(up):
        slot = 0 if up else 1
        return pltpu.make_async_remote_copy(
            flow,
            flow_in.at[slot],
            flow_send.at[slot],
            flow_recv.at[slot],
            device_id={"blk": blk - 1 if up else blk + 1},
            device_id_type=MESH,
        )

    nodes = tiles * LANES

    def packed(first, count):
        flat = [part[at : at + SPAN] for part in own for at in range(first, first + count, SPAN)]
        flat = jnp.concatenate(flat, axis=1)
        width = flat.shape[1] // 4
        return jnp.concatenate([flat[:, k * width : (k + 1) * width] for k in range(4)], axis=0).astype(jnp.bfloat16)

    def unpacked(block):
        block = block.astype(jnp.float32)
        flat = jnp.concatenate([block[k * SPAN : (k + 1) * SPAN] for k in range(4)], axis=1)
        parts = [flat[:, k : k + nodes] for k in range(0, flat.shape[1], nodes)]
        each = len(parts) // 3
        return [parts[k * each : (k + 1) * each] for k in range(3)]

    edge_up[...] = packed(0, EDGE)
    edge_down[...] = packed(rows - SPAN, SPAN)
    greeted = has_prev, has_next, gives, passes, passes, takes
    pl.semaphore_wait(barrier, turns + 2 + functools.reduce(lambda p, q: p + q, [g.astype(jnp.int32) for g in greeted]))
    lowest = (here[1] == 0) & (here[2] == 0)
    highest = (here[1] == 1) & (here[2] == 1)
    pl.when(has_above & jnp.logical_not(lowest))(lambda: edge_copy(True).start())
    pl.when(has_below & jnp.logical_not(highest))(lambda: edge_copy(False).start())
    pl.when(has_above & lowest)(lambda: edge_via(True).start())
    pl.when(has_below & highest)(lambda: edge_via(False).start())
    pl.when(has_prev)(lambda: sent(0).start())
    pl.semaphore_signal(round_sem.at[0], inc=1, device_id={"blk": across}, device_id_type=MESH)
    lax.fori_loop(1, 8, hide_and_send, 0)
    pl.semaphore_wait(round_sem.at[0], 1)
    pl.semaphore_signal(round_sem.at[1], inc=1, device_id={"blk": over}, device_id_type=MESH)
    lax.fori_loop(8, chunks, hide_and_send, 0)

    def own_spectrum(c, _):
        spectra[c] = spectrum(masked[c], narrow[...], both[...])
        return 0

    lax.fori_loop(0, chunks, own_spectrum, 0)
    onward_up = highest & (here[0] > 0)
    onward_down = lowest & (here[0] < turns - 1)

    @pl.when(onward_up)
    def _():
        edge_via(True).wait_recv()
        edge_onward(True).start()

    @pl.when(onward_down)
    def _():
        edge_via(False).wait_recv()
        edge_onward(False).start()

    pl.semaphore_wait(round_sem.at[1], 1)

    pull[...] = jnp.zeros_like(pull)
    base[...] = jnp.zeros_like(base)
    for g in range(tiles):
        at = slice(g * LANES, (g + 1) * LANES)
        pull[g, EDGE : EDGE + rows] = own[0][:, at]
        base[0, g, EDGE : EDGE + rows] = own[1][:, at]
        base[1, g, EDGE : EDGE + rows] = own[2][:, at]

    def take_edge(block, first, count):
        parts = unpacked(block)
        for n in range(0, count, SPAN):
            some = min(SPAN, count - n)
            to = slice(first + n, first + n + some)
            for g in range(tiles):
                at = slice(g * LANES, (g + 1) * LANES)
                pull[g, to] = parts[0][n // SPAN][:some, at]
                base[0, g, to] = parts[1][n // SPAN][:some, at]
                base[1, g, to] = parts[2][n // SPAN][:some, at]

    flow[...] = jnp.zeros_like(flow)
    listed[...] = jnp.zeros_like(listed)
    lane = lax.broadcasted_iota(jnp.int32, (8, LANES), 1)
    patch = lax.broadcasted_iota(jnp.int32, (nodes, LANES), 0) // (LANES // 4)
    for k in range(2):
        column = lax.broadcasted_iota(jnp.int32, (nodes, LANES), 1)
        pick[k] = jnp.where(column == patch + k * (LANES // 4), 1.0, 0.0).astype(jnp.bfloat16)
    tile_row = lax.broadcasted_iota(jnp.int32, (tiles, LANES), 0)
    quarter = lax.broadcasted_iota(jnp.int32, (tiles, LANES), 1) // (LANES // 4)

    def correlate(c, _):
        sent(c).wait_recv()
        pl.when(c < passing)(lambda: pass_on(c))
        other = spectrum(arrived[c], narrow[...], both[...])
        for k, value in enumerate(flows_of(spectra[c], other, narrow[...], both[...])):
            held = flow[k]
            for p in range(2):
                slot = lane == k * (LANES // 4) + 2 * c + p
                listed[...] = jnp.where(slot, value[p : p + 1], listed[...])
                spot = (tile_row == c // 2) & (quarter == 2 * (c % 2) + p)
                held = jnp.where(spot, value[p : p + 1], held)
            flow[k] = held
        return 0

    pause = chunks - 4
    known = pause * PAIR // SIZE // 4

    @pl.when(has_next)
    def _():
        lax.fori_loop(0, pause, correlate, 0)

    @pl.when(has_below)
    def _():
        edge_copy(True).wait_recv()
        take_edge(from_below[...], EDGE + rows, REACH)

    @pl.when(has_above)
    def _():
        edge_copy(False).wait_recv()
        take_edge(from_above[...], EDGE - SPAN, SPAN)

    loose = jnp.where(pull[...] > 0.0, SCALE, 0.0)
    link[...] = loose
    diag[...] = 4.0 * loose + SCALE * pull[...]

    part = lane // (LANES // 8)
    below = slice(EDGE + rows, EDGE + rows + EDGE)
    tail = slice(rows, rows + 2 * EDGE)

    def advance(value, step, tile=slice(None), at=slice(None), kept=0):
        return (diag[tile, at] - SCALE * SHIFTS[step]) * value[kept:] - link[tile, at] * neighbours(value)[kept:]

    def own_basis(first, last, kept):
        new, read = slice(first + kept, last), slice(first, last)
        for k in range(2):
            for g in range(first + kept, last):
                inner = slice(EDGE, EDGE + rows)
                basis[k, 0, g, :EDGE] = jnp.zeros((EDGE, LANES), jnp.float32)
                basis[k, 0, g, inner] = base[k, g, inner] + pull[g, inner] * flow[k, g : g + 1, :]
                basis[k, 0, g, below] = jnp.zeros((EDGE, LANES), jnp.float32)
            for step in range(ITERS):
                basis[k, step + 1, new] = advance(basis[k, step, read], step, new, slice(None), kept)
            for step in range(ITERS, REACH):
                value = basis[k, step, read, tail] if step == ITERS else reach[k, step - ITERS - 1, read]
                reach[k, step - ITERS, new] = advance(value, step, new, tail, kept)

    def own_sums(first, last):
        count = last - first
        over = slice(first, last)
        blocks = []
        gathered = jnp.zeros((REACH * EDGE, LANES), jnp.float32)
        for k in range(2):
            lines = []
            for i, j in PAIRS:
                product = basis[k, i, over] * basis[k, j, over]
                total = jnp.sum(product.reshape(count * (rows + 2 * EDGE) // 8, 8, LANES), axis=0)
                lines.append(jnp.sum(total, axis=0, keepdims=True))
            reached = [basis[k, step, over, below] for step in range(1, ITERS + 1)]
            reached += [reach[k, step, over, EDGE:] for step in range(REACH - ITERS)]
            strip, prior_lines = [], [jnp.zeros((1, LANES), jnp.float32)]
            for value in reached:
                weighted = pull[over, below] * value
                strip.append(jnp.concatenate([weighted[g] for g in range(count)], axis=1))
                prior_lines.append(2.0 * jnp.sum(jnp.sum(base[k, over, below] * value, axis=0), axis=0, keepdims=True))
            lines = [line + crossed(pair, prior_lines) for line, pair in zip(lines, PAIRS)]
            lines += [jnp.zeros((1, LANES), jnp.float32)] * (16 - len(lines))
            blocks += [jnp.concatenate(lines[n : n + 8], axis=0) for n in (0, 8)]
            left = jnp.concatenate(strip, axis=0)
            for _ in range(3):
                piece = left.astype(jnp.bfloat16)
                gathered = gathered + matmul(piece, pick[k, first * LANES : last * LANES])
                left = left - piece.astype(jnp.float32)
        gathered = jnp.sum(gathered.reshape(REACH, EDGE, LANES), axis=1)
        return blocks + [jnp.concatenate([jnp.zeros((1, LANES), jnp.float32), gathered], axis=0)]

    def folded(block):
        for lanes in (LANES // 2, LANES // 4, LANES // 8):
            block = block + pltpu.roll(block, lanes, 1)
        return block

    own_basis(0, known, 0)
    early = own_sums(0, known - 1)

    @pl.when(has_next)
    def _():
        lax.fori_loop(pause, chunks, correlate, 0)

    pl.when(has_above)(lambda: flow_copy(True).start())
    pl.when(has_below)(lambda: flow_copy(False).start())
    own_basis(known - 2, tiles, 1)
    blocks = [p + q for p, q in zip(early, own_sums(known - 1, tiles))]
    mine = 2.0 * blocks[4]
    for n in range(4):
        mine = jnp.where(part == 4 + n, folded(blocks[n]), mine)
    top = lax.broadcasted_iota(jnp.int32, (8, LANES), 0) == 0
    share[...] = jnp.where(top & (part < 4), listed[...], mine)

    def share_copy(n):
        return pltpu.make_async_remote_copy(
            share,
            shares.at[blk],
            share_send.at[n],
            share_recv.at[n],
            device_id={"blk": others[n]},
            device_id_type=MESH,
        )

    for n in range(bands - 1):
        share_copy(n).start()
    shares[blk] = share[...]

    def drain(c, _):
        sent(c).wait_send()
        return 0

    def drain_passed(slot, _):
        passed_on(slot).wait_send()
        return 0

    @pl.when(has_prev)
    def _():
        lax.fori_loop(0, chunks, drain, 0)

    lax.fori_loop(0, passing, drain_passed, 0)
    pl.when(onward_up)(lambda: edge_onward(True).wait_send())
    pl.when(onward_down)(lambda: edge_onward(False).wait_send())

    @pl.when(has_above)
    def _():
        edge_copy(True).wait_send()

    @pl.when(has_below)
    def _():
        edge_copy(False).wait_send()

    @pl.when(has_below)
    def _():
        flow_copy(True).wait_recv()

    @pl.when(has_above)
    def _():
        flow_copy(False).wait_recv()

    @pl.when(jnp.logical_not(has_below))
    def _():
        flow_in[0] = jnp.zeros_like(flow)

    @pl.when(jnp.logical_not(has_above))
    def _():
        flow_in[1] = jnp.zeros_like(flow)

    for k in range(2):
        for g in range(tiles):
            for source, first_row, count in (
                (flow_in.at[1], 0, EDGE),
                (flow, EDGE, rows),
                (flow_in.at[0], EDGE + rows, EDGE),
            ):
                at = slice(first_row, first_row + count)
                whole[k, 0, g, at] = base[k, g, at] + pull[g, at] * source[k, g : g + 1, :]
        for step in range(ITERS - 1):
            whole[k, step + 1] = advance(whole[k, step], step)

    @pl.when(has_above)
    def _():
        flow_copy(True).wait_send()

    @pl.when(has_below)
    def _():
        flow_copy(False).wait_send()

    for n in reversed(range(bands - 1)):
        share_copy(n).wait_recv()
    total = shares[bands - 1]
    for n in range(bands - 1):
        total = total + shares[n] * jnp.where(lane[:1] < LANES // 2, shares[n + 1, :1], 1.0)
    sums = [jnp.sum(jnp.where(part == 4 + n, total, 0.0), axis=1, keepdims=True) for n in range(4)]
    across_bands = [jnp.sum(jnp.where(part // 2 == k, total, 0.0), axis=1, keepdims=True) for k in range(2)]

    def by_component(pair, n):
        return jnp.where(lane[:1] < LANES // 2, pair[0][n : n + 1], pair[1][n : n + 1])

    none = jnp.zeros((1, LANES), jnp.float32)
    cross_lines = [none] + [by_component(across_bands, m) for m in range(1, REACH + 1)]
    gram = {}
    for n, pair in enumerate(PAIRS):
        own_line = by_component((sums[n // 8], sums[2 + n // 8]), n % 8)
        gram[pair] = own_line + crossed(pair, cross_lines)
    found = coefficients(gram)
    for k in range(2):
        weights = [value[:, k * LANES // 2 : k * LANES // 2 + 1] for value in found]
        for g in range(tiles):
            at = slice(EDGE, EDGE + rows)
            value = weights[0] * whole[k, 0, g, at]
            for step in range(1, ITERS):
                value = value + weights[step] * whole[k, step, g, at]
            out_ref[k, :, g * LANES : (g + 1) * LANES] = value

    for n in range(bands - 1):
        share_copy(n).wait_send()


def per_device(sections, bands, image, tissue_mask, anchor, fixed_nodes, prior_shift):
    _, size, columns = image.shape
    _, rows, nodes = anchor.shape
    chunks = columns // PAIR
    tiles = nodes // LANES
    wide = 2 * EDGE + rows
    width = 3 * nodes // 4
    both, narrow = tables()
    operands = image, tissue_mask, anchor, fixed_nodes, prior_shift, jnp.asarray(both), jnp.asarray(narrow)
    operands = [pltpu.with_memory_space_constraint(operand, pltpu.HBM) for operand in operands]
    out = pl.pallas_call(
        functools.partial(kernel, sections, bands),
        out_shape=jax.ShapeDtypeStruct((2, rows, nodes), jnp.float32),
        in_specs=[pl.BlockSpec(memory_space=pl.ANY)] * 7,
        out_specs=pl.BlockSpec(memory_space=pltpu.VMEM),
        scratch_shapes=[
            pltpu.VMEM((chunks, size, PAIR), jnp.bfloat16),
            pltpu.VMEM((chunks, size, PAIR), jnp.int32),
            pltpu.VMEM((chunks, size, PAIR), jnp.bfloat16),
            pltpu.VMEM((chunks, size, PAIR), jnp.bfloat16),
            pltpu.VMEM((ASIDE, size, PAIR), jnp.bfloat16),
            pltpu.VMEM((chunks, PAIR, PAIR), jnp.bfloat16),
            pltpu.VMEM((PAIR, PAIR), jnp.bfloat16),
            pltpu.VMEM((PAIR, SIZE), jnp.bfloat16),
            pltpu.VMEM((rows, nodes), jnp.float32),
            pltpu.VMEM((rows, nodes), jnp.int32),
            pltpu.VMEM((2, rows, nodes), jnp.float32),
            pltpu.VMEM((4 * SPAN, 2 * width), jnp.bfloat16),
            pltpu.VMEM((4 * SPAN, width), jnp.bfloat16),
            pltpu.VMEM((4 * SPAN, 2 * width), jnp.bfloat16),
            pltpu.VMEM((4 * SPAN, width), jnp.bfloat16),
            pltpu.VMEM((4 * SPAN, 2 * width), jnp.bfloat16),
            pltpu.VMEM((4 * SPAN, width), jnp.bfloat16),
            pltpu.VMEM((tiles, wide, LANES), jnp.float32),
            pltpu.VMEM((tiles, wide, LANES), jnp.float32),
            pltpu.VMEM((tiles, wide, LANES), jnp.float32),
            pltpu.VMEM((2, tiles, wide, LANES), jnp.float32),
            pltpu.VMEM((2, tiles, LANES), jnp.float32),
            pltpu.VMEM((2, 2, tiles, LANES), jnp.float32),
            pltpu.VMEM((8, LANES), jnp.float32),
            pltpu.VMEM((2, nodes, LANES), jnp.bfloat16),
            pltpu.VMEM((2, ITERS + 1, tiles, wide, LANES), jnp.float32),
            pltpu.VMEM((2, REACH - ITERS, tiles, 2 * EDGE, LANES), jnp.float32),
            pltpu.VMEM((2, ITERS, tiles, wide, LANES), jnp.float32),
            pltpu.VMEM((8, LANES), jnp.float32),
            pltpu.VMEM((bands, 8, LANES), jnp.float32),
            pltpu.SemaphoreType.DMA((2, chunks)),
            pltpu.SemaphoreType.DMA((5,)),
            pltpu.SemaphoreType.DMA((chunks,)),
            pltpu.SemaphoreType.DMA((chunks,)),
            pltpu.SemaphoreType.DMA((2,)),
            pltpu.SemaphoreType.DMA((2,)),
            pltpu.SemaphoreType.DMA((2,)),
            pltpu.SemaphoreType.DMA((2,)),
            pltpu.SemaphoreType.DMA((bands - 1,)),
            pltpu.SemaphoreType.DMA((bands - 1,)),
            pltpu.SemaphoreType.REGULAR((2,)),
            pltpu.SemaphoreType.DMA((ASIDE,)),
            pltpu.SemaphoreType.DMA((ASIDE,)),
            pltpu.SemaphoreType.DMA((2,)),
            pltpu.SemaphoreType.DMA((2,)),
        ],
        compiler_params=pltpu.CompilerParams(
            collective_id=0, has_side_effects=True, vmem_limit_bytes=40 * 1024 * 1024
        ),
        cost_estimate=pl.CostEstimate(flops=2_400_000_000, bytes_accessed=4_000_000, transcendentals=0),
    )(*operands)
    return out[:, None]


def solution(mesh):
    sections, bands = mesh.shape["sec"], mesh.shape["blk"]
    return jax.shard_map(
        functools.partial(per_device, sections, bands),
        mesh=mesh,
        in_specs=(
            P("sec", "blk", None),
            P("sec", "blk", None),
            P("sec", "blk", None),
            P("sec", "blk", None),
            P(None, "sec", "blk", None),
        ),
        out_specs=P(None, "sec", "blk", None),
        check_vma=False,
    )
```
